32 devices in a mesh: group: 4 (over y, x), member: 8 (over z, core).
Axes of the slice: x: 2, y: 2, z: 4, core: 2. Of those that a mesh axis runs over, the one named last changes fastest.
Arguments:
- clips: bfloat16 [32, 14, 64, 640], P(('group', 'member')), may hold values from -4 to 4
- targets: bfloat16 [32, 14, 64, 640], P(('group', 'member')), may hold values from -6 to 6
- timestep: int32 [32], P(('group', 'member')), may hold values from 0 to 999
- identity: int32 [32], P(('group', 'member')), may hold values from 0 to 63
- conv1_weight: bfloat16 [1920, 640], P('member', 'group'), may hold values from -6 to 6
- conv2_weight: bfloat16 [1920, 640], P('member', 'group'), may hold values from -6 to 6
- rate1: bfloat16 [1920, 640], P('member', 'group'), may hold values from 0.029907227 to 0.29882812
- rate2: bfloat16 [1920, 640], P('member', 'group'), may hold values from 0.029907227 to 0.29882812
- time_proj: bfloat16 [1280, 640], replicated, may hold values from -0.15625 to 0.15625
- subject_table: float32 [64, 1280], replicated, may hold values from -6 to 6
Outputs:
- adapted_first: float32 [4, 1920, 640], P('group', 'member')
- adapted_second: float32 [4, 1920, 640], P('group', 'member')
The draws below stay inside these ranges and needn't reach their ends.
All inputs are finite; a program needn't handle non-finite values.
Results may differ from the reference program's by a relative error of at most 0.0016.
Values may be sent and summed in bfloat16 or wider, within the bound.
No kernel may reach another device: no remote copies, remote signals or barrier semaphores. Data moves between devices by JAX's collectives and lax.ppermute only.
A program may use at most 128 MiB of HBM per device.

```python
import math
import jax
import jax.numpy as jnp
from jax import lax

C = 640
TEMB = 1280
FRAMES = 14
HW = 64
GN_GROUPS = 32
IDENTS = 64
CLIPS = 32
N_GROUP = 4
N_MEMBER = 8


def draw_clips(key, part):
    key_values, key_channel, key_position = jax.random.split(key, 3)
    reach = math.log(10.0)
    channel_scale = jnp.exp(jax.random.uniform(key_channel, (CLIPS, 1, 1, C), jnp.float32, -reach, 0.0))
    position_scale = jnp.exp(jax.random.uniform(key_position, (CLIPS, FRAMES, HW, 1), jnp.float32, -reach, 0.0))
    rough = jax.random.truncated_normal(key_values, -4.0, 4.0, (CLIPS, FRAMES, HW, C), jnp.float32)
    values = rough * channel_scale * position_scale
    return values.astype(jnp.bfloat16)


def plant(drawn, rng, smallest, high):
    dims = drawn.shape
    place = [jax.random.randint(jax.random.fold_in(rng, axis), (), 0, dims[axis]) for axis in range(len(dims))]
    drawn = drawn.at[tuple(place)].set(smallest)
    longest = dims.index(max(dims))
    place[longest] = (place[longest] + 1) % dims[longest]
    return drawn.at[tuple(place)].set(high)


def steps_of(key, dims, pieces, smallest, top_value):
    def one(position, blocks):
        draws = jax.random.uniform(jax.random.fold_in(jax.random.fold_in(key, 6), position), (blocks,), jnp.float32, smallest / len(pieces), top_value / len(pieces))
        return jnp.repeat(jnp.exp(draws), dims[position] // blocks).reshape((-1,) + (1,) * (len(dims) - position - 1))

    loudness = one(*pieces[0])
    for cut in pieces[1:]:
        loudness = loudness * one(*cut)
    return loudness


def normal_values(key, extent, scale, bound, cuts=(), held_as=jnp.bfloat16):
    drawn = scale * jax.random.normal(key, extent, jnp.float32)
    if cuts:
        drawn = drawn * steps_of(key, extent, cuts, -0.22, 0.18)
    return jnp.clip(drawn, -bound, bound).astype(held_as)


def setup_inputs(seed: int = 0) -> dict:
    seeds = jax.random.split(jax.random.key(seed), 11)
    clips = draw_clips(jax.random.fold_in(seeds[10], 71), 0)
    targets = normal_values(seeds[1], (CLIPS, FRAMES, HW, C), 1.0, 6.0, ((0, 32),))
    timestep = plant(jax.random.randint(seeds[2], (CLIPS,), 0, 1000), jax.random.fold_in(seeds[2], 1), 0, 999).astype(jnp.int32)
    identity = plant(jax.random.randint(seeds[3], (CLIPS,), 0, IDENTS), jax.random.fold_in(seeds[3], 1), 0, IDENTS - 1).astype(jnp.int32)
    conv1_weight = normal_values(seeds[4], (3 * C, C), 1.0, 6.0, ((0, 8), (1, 4)))
    conv2_weight = normal_values(seeds[5], (3 * C, C), 1.0, 6.0, ((0, 8), (1, 4)))
    rate1 = jnp.clip(jnp.exp(math.log(0.29882812) - 2.30176843 * jax.random.uniform(seeds[6], (3 * C, C), jnp.float32) ** steps_of(seeds[6], (3 * C, C), ((0, 8), (1, 4)), -0.2, 0.2)), 0.029907227, 0.29882812).astype(jnp.bfloat16)
    rate2 = jnp.clip(jnp.exp(math.log(0.29882812) - 2.30176843 * jax.random.uniform(seeds[7], (3 * C, C), jnp.float32) ** steps_of(seeds[7], (3 * C, C), ((0, 8), (1, 4)), -0.2, 0.2)), 0.029907227, 0.29882812).astype(jnp.bfloat16)
    time_proj = normal_values(seeds[8], (TEMB, C), TEMB ** -0.5, 0.15625)
    subject_table = normal_values(seeds[9], (IDENTS, TEMB), 1.0, 6.0, (), jnp.float32)
    return {"clips": clips, "targets": targets, "timestep": timestep, "identity": identity, "conv1_weight": conv1_weight, "conv2_weight": conv2_weight, "rate1": rate1, "rate2": rate2, "time_proj": time_proj, "subject_table": subject_table}


def time_bias(step_index, ident, subject_table, time_proj):
    half_width = subject_table.shape[1] // 2
    freqs = jnp.exp(-math.log(10000.0) * jnp.arange(half_width, dtype=jnp.float32) / half_width)
    angles = step_index.astype(jnp.float32) * freqs
    embedding = jnp.concatenate([jnp.cos(angles), jnp.sin(angles)])
    onehot = (jnp.arange(subject_table.shape[0], dtype=jnp.int32) == ident.astype(jnp.int32)).astype(jnp.float32)
    embedding = embedding + jnp.dot(onehot, subject_table, precision=lax.Precision.HIGHEST)
    activated = jax.nn.silu(embedding).astype(jnp.bfloat16)
    return jnp.dot(activated[None, :], time_proj, preferred_element_type=jnp.float32)[0]

def group_norm(values):
    channels = values.shape[2]
    per_group = channels // GN_GROUPS
    counted = values.shape[0] * values.shape[1] * per_group

    def spread(sums):
        return jnp.repeat(sums.reshape(GN_GROUPS, per_group).sum(axis=1) / counted, per_group)
    centre = spread(values.sum(axis=(0, 1)))
    centred = values - centre
    variance = spread((centred * centred).sum(axis=(0, 1)))
    return centred * lax.rsqrt(variance + 1e-05)

def activate(values):
    return jax.nn.silu(group_norm(values))

def stack_taps(act_values):
    frames, points, channels = act_values.shape
    blank = jnp.zeros((1, points, channels), act_values.dtype)
    before = jnp.concatenate([blank, act_values[:-1]], axis=0)
    after = jnp.concatenate([act_values[1:], blank], axis=0)
    return jnp.concatenate([before, act_values, after], axis=2).reshape(frames * points, 3 * channels)

def fold_taps(grad_rows, frames, points, channels):
    shaped = grad_rows.reshape(frames, points, 3 * channels)
    blank = jnp.zeros((1, points, channels), jnp.float32)
    from_before = jnp.concatenate([shaped[1:, :, :channels], blank], axis=0)
    from_after = jnp.concatenate([blank, shaped[:-1, :, 2 * channels:]], axis=0)
    return shaped[:, :, channels:2 * channels] + from_before + from_after

def clip_grads(clip, target, step_index, ident, conv1_weight, conv2_weight, time_proj, subject_table):
    weight_scale = 1.0 / math.sqrt(3 * C)
    latent = clip.astype(jnp.float32)
    bias_row = time_bias(step_index, ident, subject_table, time_proj)
    stacked_one = stack_taps(activate(latent).astype(jnp.bfloat16))
    hidden = weight_scale * jnp.dot(stacked_one, conv1_weight, preferred_element_type=jnp.float32) + bias_row
    hidden = hidden.reshape(FRAMES, HW, C)
    act_two, backward = jax.vjp(activate, hidden)
    stacked_two = stack_taps(act_two.astype(jnp.bfloat16))
    mixed_two = jnp.dot(stacked_two, conv2_weight, preferred_element_type=jnp.float32)
    output = latent + (weight_scale * mixed_two).reshape(FRAMES, HW, C)
    error = (output - target.astype(jnp.float32)).reshape(FRAMES * HW, C).astype(jnp.bfloat16)
    back_rows = lax.dot_general(error, conv2_weight, (((1,), (1,)), ((), ())), preferred_element_type=jnp.float32)
    grad_act = fold_taps(weight_scale * back_rows, FRAMES, HW, C)
    grad_hidden = backward(grad_act)[0].reshape(FRAMES * HW, C).astype(jnp.bfloat16)
    first_dims = (((0,), (0,)), ((), ()))
    grad_one = weight_scale * lax.dot_general(stacked_one, grad_hidden, first_dims, preferred_element_type=jnp.float32)
    grad_two = weight_scale * lax.dot_general(stacked_two, error, first_dims, preferred_element_type=jnp.float32)
    return (grad_one, grad_two)

def reference(clips, targets, timestep, identity, conv1_weight, conv2_weight, rate1, rate2, time_proj, subject_table):

    def by_group(array):
        return array.reshape((N_GROUP, N_MEMBER) + array.shape[1:])

    def group_grads(items):

        def accumulate(running, single):
            grad_one, grad_two = clip_grads(single[0], single[1], single[2], single[3], conv1_weight, conv2_weight, time_proj, subject_table)
            return ((running[0] + grad_one, running[1] + grad_two), None)
        empty_sum = jnp.zeros((3 * C, C), jnp.float32)
        summed, unused = lax.scan(accumulate, (empty_sum, empty_sum), items)
        return summed
    grad_first, grad_second = lax.map(group_grads, (by_group(clips), by_group(targets), by_group(timestep), by_group(identity)))
    adapted_first = conv1_weight.astype(jnp.float32)[None] - rate1.astype(jnp.float32)[None] * grad_first
    adapted_second = conv2_weight.astype(jnp.float32)[None] - rate2.astype(jnp.float32)[None] * grad_second
    return (adapted_first, adapted_second)
```

```python
import math

import jax
import jax.numpy as jnp
from jax import lax
from jax.sharding import PartitionSpec as P

GN_GROUPS = 32


def time_bias(step_index, ident, subject_table, time_proj):
    half_width = subject_table.shape[1] // 2
    freqs = jnp.exp(-math.log(10000.0) * jnp.arange(half_width, dtype=jnp.float32) / half_width)
    angles = step_index.astype(jnp.float32) * freqs
    embedding = jnp.concatenate([jnp.cos(angles), jnp.sin(angles)])
    onehot = (jnp.arange(subject_table.shape[0], dtype=jnp.int32) == ident).astype(jnp.float32)
    embedding = embedding + jnp.dot(onehot, subject_table, precision=lax.Precision.HIGHEST)
    activated = jax.nn.silu(embedding).astype(jnp.bfloat16)
    return jnp.dot(activated[None, :], time_proj, preferred_element_type=jnp.float32)[0]


def group_norm(values):
    channels = values.shape[2]
    per_group = channels // GN_GROUPS
    counted = values.shape[0] * values.shape[1] * per_group

    def spread(sums):
        return jnp.repeat(sums.reshape(GN_GROUPS, per_group).sum(axis=1) / counted, per_group)

    centre = spread(values.sum(axis=(0, 1)))
    centred = values - centre
    variance = spread((centred * centred).sum(axis=(0, 1)))
    return centred * lax.rsqrt(variance + 1e-05)


def activate(values):
    return jax.nn.silu(group_norm(values))


def stack_taps(act_values):
    frames, points, channels = act_values.shape
    blank = jnp.zeros((1, points, channels), act_values.dtype)
    before = jnp.concatenate([blank, act_values[:-1]], axis=0)
    after = jnp.concatenate([act_values[1:], blank], axis=0)
    return jnp.concatenate([before, act_values, after], axis=2).reshape(
        frames * points, 3 * channels
    )


def fold_taps(grad_rows, frames, points, channels):
    shaped = grad_rows.reshape(frames, points, 3 * channels)
    blank = jnp.zeros((1, points, channels), jnp.float32)
    from_before = jnp.concatenate([shaped[1:, :, :channels], blank], axis=0)
    from_after = jnp.concatenate([blank, shaped[:-1, :, 2 * channels :]], axis=0)
    return shaped[:, :, channels : 2 * channels] + from_before + from_after


def grad_terms(stacked, cotangent, weight_scale):
    product = lax.dot_general(
        stacked, cotangent, (((0,), (0,)), ((), ())), preferred_element_type=jnp.float32
    )
    return weight_scale * product


def swap(value, axis, size, offset):
    return lax.ppermute(value, axis, [(i, i ^ offset) for i in range(size)])


def gather_xor(value, axis, size, stride):
    count = size // stride
    place = lax.axis_index(axis) // stride
    blocks = [value] + [swap(value, axis, size, k * stride) for k in range(1, count)]
    bit = 1
    while bit < count:
        odd = (place & bit) != 0
        blocks = [
            jnp.where(odd, blocks[i ^ bit], blocks[i]) for i in range(count)
        ]
        bit *= 2
    return blocks


def sum_to_owner(grad, axis, size):
    rows, cols = grad.shape[0] // size, grad.shape[1]
    me = lax.axis_index(axis)
    core, place = me % 2, me // 2
    shaped = grad.reshape(size // 2, 2, rows, cols)
    away = lax.dynamic_index_in_dim(shaped, 1 - core, 1, keepdims=False).astype(jnp.bfloat16)
    home = lax.dynamic_index_in_dim(shaped, core, 1, keepdims=False)
    pair = home + swap(away, axis, size, 1).astype(jnp.float32)
    total = lax.dynamic_index_in_dim(pair, place, 0, keepdims=False)
    for k in reversed(range(1, size // 2)):
        piece = lax.dynamic_index_in_dim(pair, place ^ k, 0, keepdims=False)
        total = total + swap(piece.astype(jnp.bfloat16), axis, size, 2 * k).astype(jnp.float32)
    return total


def shards(
    n_group,
    n_member,
    clips,
    targets,
    timestep,
    identity,
    conv1_weight,
    conv2_weight,
    rate1,
    rate2,
    time_proj,
    subject_table,
):
    frames, points, channels = (clips.shape[1], clips.shape[2], clips.shape[3])
    weight_scale = 1.0 / math.sqrt(3 * channels)
    me = lax.axis_index("member")
    rows = conv1_weight.shape[0]
    contract_last = (((1,), (1,)), ((), ()))
    gathered = lax.all_gather(conv1_weight, ("member", "group"), axis=0, tiled=False)
    full_one = (
        gathered.reshape(n_member, n_group, rows, conv1_weight.shape[1])
        .transpose(0, 2, 1, 3)
        .reshape(3 * channels, channels)
    )
    own_two = jnp.concatenate(gather_xor(conv2_weight, "group", n_group, 1), axis=1)
    same_core = jnp.stack(gather_xor(own_two, "member", n_member, 2))
    other_core = swap(same_core, "member", n_member, 1)
    odd = (me % 2) != 0
    full_two = jnp.stack(
        [jnp.where(odd, other_core, same_core), jnp.where(odd, same_core, other_core)], axis=1
    ).reshape(3 * channels, channels)

    latent = clips[0].astype(jnp.float32)
    bias_row = time_bias(timestep[0], identity[0], subject_table, time_proj)
    stacked_one = stack_taps(activate(latent).astype(jnp.bfloat16))
    mixed_one = jnp.dot(stacked_one, full_one, preferred_element_type=jnp.float32)
    hidden = (weight_scale * mixed_one + bias_row).reshape(frames, points, channels)
    act_two, backward = jax.vjp(activate, hidden)
    stacked_two = stack_taps(act_two.astype(jnp.bfloat16))
    mixed_two = jnp.dot(stacked_two, full_two, preferred_element_type=jnp.float32)
    output = latent + (weight_scale * mixed_two).reshape(frames, points, channels)
    error = (
        (output - targets[0].astype(jnp.float32))
        .reshape(frames * points, channels)
        .astype(jnp.bfloat16)
    )
    local_two = grad_terms(stacked_two, error, weight_scale)
    grad_two = sum_to_owner(local_two, "member", n_member)
    rates, error = lax.optimization_barrier((jnp.concatenate([rate1, rate2]), error))
    rates = jnp.concatenate(gather_xor(rates, "group", n_group, 1), axis=1)
    rate_one, rate_two = rates[:rows], rates[rows:]
    back_rows = lax.dot_general(
        error, full_two, contract_last, preferred_element_type=jnp.float32
    )
    grad_act = fold_taps(weight_scale * back_rows, frames, points, channels)
    grad_hidden = backward(grad_act)[0].reshape(frames * points, channels).astype(jnp.bfloat16)
    grad_one = sum_to_owner(
        grad_terms(stacked_one, grad_hidden, weight_scale), "member", n_member
    )
    own_one = lax.dynamic_slice_in_dim(full_one, me * rows, rows, 0)
    adapted_one = own_one.astype(jnp.float32) - rate_one.astype(jnp.float32) * grad_one
    adapted_two = own_two.astype(jnp.float32) - rate_two.astype(jnp.float32) * grad_two
    return (adapted_one[None], adapted_two[None])


def solution(mesh):
    n_group, n_member = mesh.shape["group"], mesh.shape["member"]
    return jax.shard_map(
        lambda *arrays: shards(n_group, n_member, *arrays),
        mesh=mesh,
        in_specs=(
            P(("group", "member"), None, None, None),
            P(("group", "member"), None, None, None),
            P(("group", "member")),
            P(("group", "member")),
            P("member", "group"),
            P("member", "group"),
            P("member", "group"),
            P("member", "group"),
            P(),
            P(),
        ),
        out_specs=(P("group", "member", None), P("group", "member", None)),
        check_vma=False,
    )
```

```python
import functools
import math

import jax
import jax.numpy as jnp
import numpy as np
from jax import lax
from jax.experimental import pallas as pl
from jax.experimental.pallas import tpu as pltpu
from jax.sharding import PartitionSpec as P

GN_GROUPS = 32
CHUNK = 128
MEGA = 1024 * 1024
BF16 = jnp.bfloat16
F32 = jnp.float32


def time_bias(step_index, ident, subject_table, time_proj):
    half_width = subject_table.shape[1] // 2
    freqs = jnp.exp(-math.log(10000.0) * jnp.arange(half_width, dtype=F32) / half_width)
    angles = step_index.astype(F32) * freqs
    embedding = jnp.concatenate([jnp.cos(angles), jnp.sin(angles)])
    onehot = (jnp.arange(subject_table.shape[0], dtype=jnp.int32) == ident).astype(F32)
    embedding = embedding + jnp.dot(onehot, subject_table, precision=lax.Precision.HIGHEST)
    activated = jax.nn.silu(embedding).astype(BF16)
    return jnp.dot(activated[None, :], time_proj, preferred_element_type=F32)


def vmem(count):
    return [pl.BlockSpec(memory_space=pltpu.VMEM)] * count


def smem(count):
    return [pl.BlockSpec(memory_space=pltpu.SMEM)] * count


def call(body, out_shape, scratch, flops, moved, name, in_specs):
    outs = len(out_shape)
    return pl.pallas_call(
        body,
        out_shape=tuple(jax.ShapeDtypeStruct(s, d) for s, d in out_shape),
        in_specs=in_specs,
        out_specs=tuple(vmem(outs)),
        scratch_shapes=scratch,
        compiler_params=pltpu.CompilerParams(vmem_limit_bytes=40 * MEGA),
        cost_estimate=pl.CostEstimate(flops=flops, bytes_accessed=moved, transcendentals=0),
        name=name,
    )


def spread(row, same_group):
    high = row.astype(BF16)
    rest = row - high.astype(F32)
    middle = rest.astype(BF16)
    low = (rest - middle.astype(F32)).astype(BF16)
    stacked = jnp.concatenate(
        [jnp.broadcast_to(part, (16, row.shape[1])) for part in (high, middle, low)], axis=0
    )
    sums = jnp.dot(stacked, same_group, preferred_element_type=F32)
    return sums[0:1] + sums[16:17] + sums[32:33]


def norm_stats(read, rows, channels, same_group):
    counted = rows * (channels // GN_GROUPS)
    steps = rows // CHUNK
    total = lax.fori_loop(
        0,
        steps,
        lambda i, acc: acc + read(i).reshape(CHUNK // 8, 8, channels).sum(axis=0),
        jnp.zeros((8, channels), F32),
    ).sum(axis=0, keepdims=True)
    centre = spread(total, same_group) * (1.0 / counted)

    def squares(i, acc):
        centred = read(i) - centre
        return acc + (centred * centred).reshape(CHUNK // 8, 8, channels).sum(axis=0)

    square = lax.fori_loop(0, steps, squares, jnp.zeros((8, channels), F32)).sum(
        axis=0, keepdims=True
    )
    variance = spread(square, same_group) * (1.0 / counted)
    return centre, lax.rsqrt(variance + 1e-05)


def at(i, shift=0):
    return pl.ds(pl.multiple_of(i * CHUNK + shift, 64), CHUNK)


def clear_edges(padded_ref, points):
    edge = jnp.zeros((points, padded_ref.shape[1]), padded_ref.dtype)
    padded_ref[0:points] = edge
    padded_ref[padded_ref.shape[0] - points :] = edge


def enter_kernel(points, clip_ref, same_ref, padded_ref, turned_ref):
    rows, channels = clip_ref.shape
    same_group = same_ref[...]
    centre, inverse = norm_stats(
        lambda i: clip_ref[at(i)].astype(F32), rows, channels, same_group
    )
    clear_edges(padded_ref, points)

    @pl.loop(0, rows // CHUNK)
    def _(i):
        normal = (clip_ref[at(i)].astype(F32) - centre) * inverse
        act = (normal / (1.0 + jnp.exp(-normal))).astype(BF16)
        padded_ref[at(i, points)] = act
        turned_ref[:, at(i)] = act.T


def taps_of(padded_ref, start, size, points):
    return jnp.concatenate(
        [padded_ref[pl.ds(start + t * points, size)] for t in range(3)], axis=1
    )


def first_kernel(
    points, scale, in_ref, weight_ref, bias_ref, same_ref,
    normal_ref, inverse_ref, padded_ref, turned_ref, hidden_ref,
):
    rows, channels = normal_ref.shape
    half = rows // 2
    bias = bias_ref[...]

    @pl.loop(0, 2)
    def _(i):
        start = pl.multiple_of(i * half, 64)
        mixed = jnp.dot(
            taps_of(in_ref, start, half, points), weight_ref[...], preferred_element_type=F32
        )
        hidden_ref[pl.ds(start, half)] = scale * mixed + bias

    centre, inverse = norm_stats(lambda i: hidden_ref[at(i)], rows, channels, same_ref[...])
    inverse_ref[...] = inverse
    clear_edges(padded_ref, points)

    @pl.loop(0, rows // CHUNK)
    def _(i):
        normal = (hidden_ref[at(i)] - centre) * inverse
        normal_ref[at(i)] = normal
        act = (normal / (1.0 + jnp.exp(-normal))).astype(BF16)
        padded_ref[at(i, points)] = act
        turned_ref[:, at(i)] = act.T


def second_kernel(points, scale, in_ref, weight_ref, clip_ref, target_ref, error_ref):
    rows = clip_ref.shape[0]
    half = rows // 2
    clear_edges(error_ref, points)

    @pl.loop(0, 2)
    def _(i):
        start = pl.multiple_of(i * half, 64)
        mixed = jnp.dot(
            taps_of(in_ref, start, half, points), weight_ref[...], preferred_element_type=F32
        )
        here = pl.ds(start, half)
        output = clip_ref[here].astype(F32) + scale * mixed
        error_ref[pl.ds(pl.multiple_of(start + points, 64), half)] = (
            output - target_ref[here].astype(F32)
        ).astype(BF16)


def back_kernel(
    points, scale, error_ref, weight_ref, normal_ref, inverse_ref, same_ref, out_ref, grad_ref
):
    rows, channels = normal_ref.shape
    half = rows // 2
    counted = rows * (channels // GN_GROUPS)
    last = (((1,), (1,)), ((), ()))

    @pl.loop(0, 2)
    def _(i):
        start = pl.multiple_of(i * half, 64)
        total = None
        for t in range(3):
            part = lax.dot_general(
                error_ref[pl.ds(pl.multiple_of(start + (2 - t) * points, 64), half)],
                weight_ref[t * channels : (t + 1) * channels],
                last,
                preferred_element_type=F32,
            )
            total = part if total is None else total + part
        grad_ref[pl.ds(start, half)] = total

    def through(i, sums):
        normal = normal_ref[at(i)]
        gate = 1.0 / (1.0 + jnp.exp(-normal))
        grad = scale * grad_ref[at(i)] * (gate * (1.0 + normal * (1.0 - gate)))
        grad_ref[at(i)] = grad

        def fold(value):
            return value.reshape(CHUNK // 8, 8, channels).sum(axis=0)

        return sums[0] + fold(grad), sums[1] + fold(grad * normal)

    zero = jnp.zeros((8, channels), F32)
    plain, crossed = lax.fori_loop(0, rows // CHUNK, through, (zero, zero))
    same_group = same_ref[...]
    mean = spread(plain.sum(axis=0, keepdims=True), same_group) * (1.0 / counted)
    slope = spread(crossed.sum(axis=0, keepdims=True), same_group) * (1.0 / counted)
    inverse = inverse_ref[...]
    clear_edges(out_ref, points)

    @pl.loop(0, rows // CHUNK)
    def _(i):
        value = (grad_ref[at(i)] - mean - normal_ref[at(i)] * slope) * inverse
        out_ref[at(i, points)] = value.astype(BF16)


def grad_kernel(points, scale, block, me_ref, turned_ref, cotangent_ref, *refs):
    channels, rows = turned_ref.shape
    total_ref = refs[-1]

    @pl.loop(0, 3)
    def _(t):
        shifted = cotangent_ref[pl.ds(pl.multiple_of((2 - t) * points, 64), rows)]
        total_ref[pl.ds(pl.multiple_of(t * channels, 128), channels)] = scale * jnp.dot(
            turned_ref[...], shifted, preferred_element_type=F32
        )

    if block is not None:
        away_ref, home_ref = refs[0], refs[1]
        me = me_ref[0]

        @pl.loop(0, away_ref.shape[0])
        def _(j):
            away = pl.multiple_of((me ^ (2 * j + 1)) * block, 16)
            home = pl.multiple_of((me ^ (2 * j)) * block, 16)
            away_ref[j] = total_ref[pl.ds(away, block)].astype(BF16)
            home_ref[j] = total_ref[pl.ds(home, block)]


def gradient(turned, cotangent, me, n_member, points, scale):
    channels, rows = turned.shape
    block = 3 * channels // n_member
    flops, moved = 6 * rows * channels * channels, 8 * rows * channels
    specs = smem(1) + vmem(2)
    if block % 16 == 0:
        shape = (n_member // 2, block, channels)
        return call(
            functools.partial(grad_kernel, points, scale, block),
            [(shape, BF16), (shape, F32)],
            [pltpu.VMEM((3 * channels, channels), F32)],
            flops, moved, "gradient", specs,
        )(me[None], turned, cotangent)
    (total,) = call(
        functools.partial(grad_kernel, points, scale, None),
        [((3 * channels, channels), F32)],
        [], flops, moved, "gradient", specs,
    )(me[None], turned, cotangent)
    total = total.reshape(n_member, block, channels)
    order = [lax.dynamic_index_in_dim(total, me ^ j, 0, keepdims=False) for j in range(n_member)]
    return jnp.stack(order[1::2]).astype(BF16), jnp.stack(order[0::2])


def swap(value, axis, size, offset):
    return lax.ppermute(value, axis, [(i, i ^ offset) for i in range(size)])


def order_after(value, *others):
    return lax.optimization_barrier((value,) + others)[0]


TAIL = 64


def pack_kernel(*refs):
    count = len(refs) // 2
    for source, packed in zip(refs[:count], refs[count:]):
        rows, cols = source.shape
        packed[0:rows] = source[:, 0:128]
        rest = source[:, 128:cols]
        short = 4 * TAIL - rows
        rest = jnp.concatenate([rest, jnp.zeros((short, cols - 128), rest.dtype)], axis=0)
        packed[rows:] = jnp.concatenate(
            [rest[q * TAIL : (q + 1) * TAIL] for q in range(4)], axis=1
        )


def unpacked(block_of, rows, n_group):
    parts = []
    for g in range(n_group):
        block = block_of(g)
        rest = block[rows:]
        pieces = [rest[:, 32 * q : 32 * q + 32] for q in range(4)]
        parts += [block[0:rows], jnp.concatenate(pieces, axis=0)[0:rows]]
    return jnp.concatenate(parts, axis=1)


def weight_kernel(rows, n_group, place_ref, mine_ref, other_ref, full_ref):
    group, member = place_ref[0], place_ref[1]

    @pl.loop(0, mine_ref.shape[0])
    def _(k):
        for half, source in ((0, mine_ref), (1, other_ref)):
            start = pl.multiple_of((member ^ (2 * k + half)) * rows, 16)
            full_ref[pl.ds(start, rows)] = unpacked(
                lambda g: source[k, g ^ group], rows, n_group
            )


def rate_kernel(rows, n_group, place_ref, packed_ref, one_ref, two_ref):
    group = place_ref[0]
    for which, out in enumerate((one_ref, two_ref)):
        out[...] = unpacked(lambda g: packed_ref[g ^ group, which], rows, n_group)


def gather_weight(packed, n_group, n_member):
    chips = n_member // 2
    along = [packed] + [swap(packed, "member", n_member, 2 * k) for k in range(1, chips)]
    first, second = jnp.stack(along[: chips // 2]), jnp.stack(along[chips // 2 :])
    first_x = swap(first, "group", n_group, 1)
    second_y = swap(second, "group", n_group, 2)
    first = jnp.stack([first, first_x], axis=1)
    second = jnp.stack([second, second_y], axis=1)
    first_y = swap(first, "group", n_group, 2)
    second_x = swap(second, "group", n_group, 1)
    first = jnp.concatenate([first, first_y], axis=1)
    second = jnp.stack(
        [second[:, 0], second_x[:, 0], second[:, 1], second_x[:, 1]], axis=1
    )
    mine = jnp.concatenate([first, second])
    return mine, swap(mine, "member", n_member, 1)


def weights_and_rates(n_group, n_member, conv1, conv2, rate1, rate2, place):
    rows, cols = conv1.shape
    whole = (n_member * rows, n_group * cols)
    if (cols, n_group, rows % 16) != (160, 4, 0) or rows > 4 * TAIL:

        def full(weight):
            return lax.all_gather(
                lax.all_gather(weight, "group", axis=1, tiled=True), "member", axis=0, tiled=True
            )

        def rates(after):
            return (
                lax.all_gather(rate1, "group", axis=1, tiled=True),
                lax.all_gather(rate2, "group", axis=1, tiled=True),
            )

        return full(conv1), full(conv2), rates
    packed_shape = (rows + TAIL, 128)
    one, two, slow, fast = call(
        pack_kernel, [(packed_shape, BF16)] * 4, [], 0, 8 * rows * cols, "pack", vmem(4)
    )(conv1, conv2, rate1, rate2)

    def unpack(halves):
        return call(
            functools.partial(weight_kernel, rows, n_group),
            [(whole, BF16)], [], 0, 4 * whole[0] * whole[1], "unpack", smem(1) + vmem(2),
        )(place, *halves)[0]

    halves_one = gather_weight(one, n_group, n_member)
    halves_two = gather_weight(two, n_group, n_member)

    def rates(after):
        both = order_after(jnp.stack([slow, fast]), after)
        shape = (rows, whole[1])
        blocks = jnp.stack([both] + [swap(both, "group", n_group, k) for k in range(1, n_group)])
        return call(
            functools.partial(rate_kernel, rows, n_group),
            [(shape, BF16)] * 2, [], 0, 8 * rows * whole[1], "rates", smem(1) + vmem(1),
        )(place, blocks)

    return unpack(halves_one), unpack(halves_two), rates


def pair_sum(home, received):
    return [home[j] + received[j].astype(F32) for j in range(home.shape[0])]


def halve_to_owner(pairs, n_member):
    pairs = list(pairs)
    bit = 1
    while bit < len(pairs):
        away = [k for k in range(len(pairs)) if k & bit and not k & (bit - 1)]
        for k in reversed(away):
            received = swap(pairs[k].astype(BF16), "member", n_member, 2 * bit)
            pairs[k ^ bit] = pairs[k ^ bit] + received.astype(F32)
        bit *= 2
    return pairs[0]


def direct_to_owner(pairs, n_member):
    total = pairs[0]
    for k in reversed(range(1, len(pairs))):
        total = total + swap(pairs[k].astype(BF16), "member", n_member, 2 * k).astype(F32)
    return total


def shards(
    n_group,
    n_member,
    clips,
    targets,
    timestep,
    identity,
    conv1_weight,
    conv2_weight,
    rate1,
    rate2,
    time_proj,
    subject_table,
):
    frames, points, channels = (clips.shape[1], clips.shape[2], clips.shape[3])
    rows, padded = frames * points, (frames + 2) * points
    scale = 1.0 / math.sqrt(3 * channels)
    group, me = lax.axis_index("group"), lax.axis_index("member")
    place = jnp.stack([group, me]).astype(jnp.int32)
    own_rows = conv1_weight.shape[0]
    clip, target = clips.reshape(rows, channels), targets.reshape(rows, channels)
    blocks = np.arange(channels) // (channels // GN_GROUPS)
    same_group = jnp.asarray((blocks[:, None] == blocks[None, :]), BF16)
    product = 6 * rows * channels * channels
    passed = 8 * rows * channels

    full_one, full_two, rates = weights_and_rates(
        n_group, n_member, conv1_weight, conv2_weight, rate1, rate2, place
    )
    bias_row = time_bias(timestep[0], identity[0], subject_table, time_proj)
    act_one, turned_one = call(
        functools.partial(enter_kernel, points),
        [((padded, channels), BF16), ((channels, rows), BF16)],
        [], passed, passed, "enter", vmem(2),
    )(clip, same_group)
    normal, inverse, act_two, turned_two = call(
        functools.partial(first_kernel, points, scale),
        [
            ((rows, channels), F32),
            ((1, channels), F32),
            ((padded, channels), BF16),
            ((channels, rows), BF16),
        ],
        [pltpu.VMEM((rows, channels), F32)],
        product, passed, "conv_norm", vmem(4),
    )(act_one, full_one, bias_row, same_group)
    (error,) = call(
        functools.partial(second_kernel, points, scale),
        [((padded, channels), BF16)],
        [], product, passed, "conv_error", vmem(4),
    )(act_two, full_two, clip, target)
    away_two, home_two = gradient(turned_two, error, me, n_member, points, scale)
    received_two = swap(away_two, "member", n_member, 1)
    (grad_hidden,) = call(
        functools.partial(back_kernel, points, scale),
        [((padded, channels), BF16)],
        [pltpu.VMEM((rows, channels), F32)],
        product, passed, "back_norm", vmem(5),
    )(order_after(error, away_two), full_two, normal, inverse, same_group)
    received_two = order_after(received_two, grad_hidden)
    pairs_two = pair_sum(home_two, received_two)
    grad_hidden = order_after(grad_hidden, *pairs_two)
    grad_two = direct_to_owner(pairs_two, n_member)
    away_one, home_one = gradient(turned_one, grad_hidden, me, n_member, points, scale)
    received_one = swap(away_one, "member", n_member, 1)
    rate_one, rate_two = rates(away_one)
    grad_one = halve_to_owner(pair_sum(home_one, received_one), n_member)
    own_one = lax.dynamic_slice_in_dim(full_one, me * own_rows, own_rows, 0)
    own_two = lax.dynamic_slice_in_dim(full_two, me * own_rows, own_rows, 0)
    adapted_one = own_one.astype(F32) - rate_one.astype(F32) * grad_one
    adapted_two = own_two.astype(F32) - rate_two.astype(F32) * grad_two
    return (adapted_one[None], adapted_two[None])


def solution(mesh):
    n_group, n_member = mesh.shape["group"], mesh.shape["member"]
    return jax.shard_map(
        lambda *arrays: shards(n_group, n_member, *arrays),
        mesh=mesh,
        in_specs=(
            P(("group", "member"), None, None, None),
            P(("group", "member"), None, None, None),
            P(("group", "member")),
            P(("group", "member")),
            P("member", "group"),
            P("member", "group"),
            P("member", "group"),
            P("member", "group"),
            P(),
            P(),
        ),
        out_specs=(P("group", "member", None), P("group", "member", None)),
        check_vma=False,
    )
```

```python
import functools
import math

import jax
import jax.numpy as jnp
import numpy as np
from jax import lax
from jax.experimental import pallas as pl
from jax.experimental.pallas import tpu as pltpu
from jax.sharding import PartitionSpec as P

GN_GROUPS = 32
CHUNK = 128
MEGA = 1024 * 1024
BF16 = jnp.bfloat16
F32 = jnp.float32


def time_bias(step_index, ident, subject_table, time_proj):
    half_width = subject_table.shape[1] // 2
    freqs = jnp.exp(-math.log(10000.0) * jnp.arange(half_width, dtype=F32) / half_width)
    angles = step_index.astype(F32) * freqs
    embedding = jnp.concatenate([jnp.cos(angles), jnp.sin(angles)])
    onehot = (jnp.arange(subject_table.shape[0], dtype=jnp.int32) == ident).astype(F32)
    embedding = embedding + jnp.dot(onehot, subject_table, precision=lax.Precision.HIGHEST)
    activated = jax.nn.silu(embedding).astype(BF16)
    return jnp.dot(activated[None, :], time_proj, preferred_element_type=F32)


def vmem(count):
    return [pl.BlockSpec(memory_space=pltpu.VMEM)] * count


def smem(count):
    return [pl.BlockSpec(memory_space=pltpu.SMEM)] * count


def call(body, out_shape, scratch, name, in_specs):
    outs = len(out_shape)
    return pl.pallas_call(
        body,
        out_shape=tuple(jax.ShapeDtypeStruct(s, d) for s, d in out_shape),
        in_specs=in_specs,
        out_specs=tuple(vmem(outs)),
        scratch_shapes=scratch,
        compiler_params=pltpu.CompilerParams(vmem_limit_bytes=40 * MEGA),
        cost_estimate=pl.CostEstimate(flops=0, bytes_accessed=1024, transcendentals=0),
        name=name,
    )


def spread(row, same_group):
    high = row.astype(BF16)
    rest = row - high.astype(F32)
    middle = rest.astype(BF16)
    low = (rest - middle.astype(F32)).astype(BF16)
    stacked = jnp.concatenate(
        [jnp.broadcast_to(part, (16, row.shape[1])) for part in (high, middle, low)], axis=0
    )
    sums = jnp.dot(stacked, same_group, preferred_element_type=F32)
    return sums[0:1] + sums[16:17] + sums[32:33]


def norm_stats(read, rows, channels, same_group):
    counted = rows * (channels // GN_GROUPS)
    steps = rows // CHUNK
    total = lax.fori_loop(
        0,
        steps,
        lambda i, acc: acc + read(i).reshape(CHUNK // 8, 8, channels).sum(axis=0),
        jnp.zeros((8, channels), F32),
    ).sum(axis=0, keepdims=True)
    centre = spread(total, same_group) * (1.0 / counted)

    def squares(i, acc):
        centred = read(i) - centre
        return acc + (centred * centred).reshape(CHUNK // 8, 8, channels).sum(axis=0)

    square = lax.fori_loop(0, steps, squares, jnp.zeros((8, channels), F32)).sum(
        axis=0, keepdims=True
    )
    variance = spread(square, same_group) * (1.0 / counted)
    return centre, lax.rsqrt(variance + 1e-05)


def at(i, shift=0):
    return pl.ds(pl.multiple_of(i * CHUNK + shift, 64), CHUNK)


def clear_edges(padded_ref, points):
    edge = jnp.zeros((points, padded_ref.shape[1]), padded_ref.dtype)
    padded_ref[0:points] = edge
    padded_ref[padded_ref.shape[0] - points :] = edge


def enter_kernel(points, clip_ref, same_ref, padded_ref, turned_ref):
    rows, channels = clip_ref.shape
    same_group = same_ref[...]
    centre, inverse = norm_stats(
        lambda i: clip_ref[at(i)].astype(F32), rows, channels, same_group
    )
    clear_edges(padded_ref, points)

    @pl.loop(0, rows // CHUNK)
    def _(i):
        normal = (clip_ref[at(i)].astype(F32) - centre) * inverse
        act = (normal / (1.0 + jnp.exp(-normal))).astype(BF16)
        padded_ref[at(i, points)] = act
        turned_ref[:, at(i)] = act.T


def taps_of(padded_ref, start, size, points):
    return jnp.concatenate(
        [padded_ref[pl.ds(start + t * points, size)] for t in range(3)], axis=1
    )


def full_weight(weight_refs, full_ref):
    if len(weight_refs) == 1:
        return weight_refs[0]
    place_ref, mine_ref, other_ref = weight_refs
    member, rows = place_ref[1], mine_ref.shape[1]

    @pl.loop(0, mine_ref.shape[0])
    def _(k):
        for half, source in ((0, mine_ref), (1, other_ref)):
            start = pl.multiple_of((member ^ (2 * k + half)) * rows, 16)
            full_ref[pl.ds(start, rows)] = source[k]

    return full_ref


def first_kernel(points, scale, in_ref, bias_ref, *refs):
    weight_refs = refs[:-2]
    hidden_ref, full_ref = refs[-2:]
    half = hidden_ref.shape[0] // 2
    bias = bias_ref[...]
    weight_ref = full_weight(weight_refs, full_ref)

    @pl.loop(0, 2)
    def _(i):
        start = pl.multiple_of(i * half, 64)
        mixed = jnp.dot(
            taps_of(in_ref, start, half, points), weight_ref[...], preferred_element_type=F32
        )
        hidden_ref[pl.ds(start, half)] = scale * mixed + bias


def norm_kernel(
    points, hidden_ref, same_ref, normal_ref, inverse_ref, padded_ref, turned_ref
):
    rows, channels = normal_ref.shape
    centre, inverse = norm_stats(lambda i: hidden_ref[at(i)], rows, channels, same_ref[...])
    inverse_ref[...] = inverse
    clear_edges(padded_ref, points)

    @pl.loop(0, rows // CHUNK)
    def _(i):
        normal = (hidden_ref[at(i)] - centre) * inverse
        normal_ref[at(i)] = normal
        act = (normal / (1.0 + jnp.exp(-normal))).astype(BF16)
        padded_ref[at(i, points)] = act
        turned_ref[:, at(i)] = act.T


def second_kernel(points, scale, in_ref, clip_ref, target_ref, *refs):
    weight_refs = refs[:-2]
    error_ref, full_ref = refs[-2:]
    rows = clip_ref.shape[0]
    half = rows // 2
    clear_edges(error_ref, points)
    weight_ref = full_weight(weight_refs, full_ref)
    if len(weight_refs) == 1:
        full_ref[...] = weight_ref[...]

    @pl.loop(0, 2)
    def _(i):
        start = pl.multiple_of(i * half, 64)
        mixed = jnp.dot(
            taps_of(in_ref, start, half, points), weight_ref[...], preferred_element_type=F32
        )
        here = pl.ds(start, half)
        output = clip_ref[here].astype(F32) + scale * mixed
        error_ref[pl.ds(pl.multiple_of(start + points, 64), half)] = (
            output - target_ref[here].astype(F32)
        ).astype(BF16)


def back_kernel(points, scale, error_ref, weight_ref, grad_ref):
    rows, channels = grad_ref.shape
    half = rows // 2
    last = (((1,), (1,)), ((), ()))

    @pl.loop(0, 2)
    def _(i):
        start = pl.multiple_of(i * half, 64)
        total = None
        for t in range(3):
            part = lax.dot_general(
                error_ref[pl.ds(pl.multiple_of(start + (2 - t) * points, 64), half)],
                weight_ref[t * channels : (t + 1) * channels],
                last,
                preferred_element_type=F32,
            )
            total = part if total is None else total + part
        grad_ref[pl.ds(start, half)] = scale * total


def norm_back_kernel(
    points, act_grad_ref, normal_ref, inverse_ref, same_ref, out_ref, grad_ref
):
    rows, channels = normal_ref.shape
    counted = rows * (channels // GN_GROUPS)

    def through(i, sums):
        normal = normal_ref[at(i)]
        gate = 1.0 / (1.0 + jnp.exp(-normal))
        grad = act_grad_ref[at(i)] * (gate * (1.0 + normal * (1.0 - gate)))
        grad_ref[at(i)] = grad

        def fold(value):
            return value.reshape(CHUNK // 8, 8, channels).sum(axis=0)

        return sums[0] + fold(grad), sums[1] + fold(grad * normal)

    zero = jnp.zeros((8, channels), F32)
    plain, crossed = lax.fori_loop(0, rows // CHUNK, through, (zero, zero))
    same_group = same_ref[...]
    mean = spread(plain.sum(axis=0, keepdims=True), same_group) * (1.0 / counted)
    slope = spread(crossed.sum(axis=0, keepdims=True), same_group) * (1.0 / counted)
    inverse = inverse_ref[...]
    clear_edges(out_ref, points)

    @pl.loop(0, rows // CHUNK)
    def _(i):
        value = (grad_ref[at(i)] - mean - normal_ref[at(i)] * slope) * inverse
        out_ref[at(i, points)] = value.astype(BF16)


def grad_kernel(points, scale, block, centred, me_ref, turned_ref, cotangent_ref, *refs):
    channels, rows = turned_ref.shape
    refs = list(refs)
    total_ref = refs.pop()
    if centred:
        factor_ref = refs.pop()
        ones = jnp.ones((rows, 128), BF16)
        mean = jnp.dot(turned_ref[...], ones, preferred_element_type=F32) * (1.0 / rows)
        sums = scale * jnp.dot(
            jnp.ones((16, rows), BF16),
            cotangent_ref[pl.ds(points, rows)],
            preferred_element_type=F32,
        )
        factor_ref[0:1] = mean.T[0:1]
        factor_ref[1:2] = sums[0:1]
        factor_ref[2:8] = jnp.zeros((6, channels), F32)
        common = jnp.concatenate([mean] * (channels // 128), axis=1) * sums[0:1]

    @pl.loop(0, 3)
    def _(t):
        shifted = cotangent_ref[pl.ds(pl.multiple_of((2 - t) * points, 64), rows)]
        product = scale * jnp.dot(turned_ref[...], shifted, preferred_element_type=F32)
        if centred:
            product = product - common
        total_ref[pl.ds(pl.multiple_of(t * channels, 128), channels)] = product

    if block is not None:
        away_ref, home_ref = refs
        me = me_ref[0]

        @pl.loop(0, away_ref.shape[0])
        def _(j):
            away = pl.multiple_of((me ^ (2 * j + 1)) * block, 16)
            home = pl.multiple_of((me ^ (2 * j)) * block, 16)
            away_ref[j] = total_ref[pl.ds(away, block)].astype(BF16)
            home_ref[j] = total_ref[pl.ds(home, block)]


def gradient(turned, cotangent, me, n_member, points, scale, centred):
    channels, rows = turned.shape
    block = 3 * channels // n_member
    specs = smem(1) + vmem(2)
    factors = [((8, channels), F32)] if centred else []
    if block % 16 == 0:
        shape = (n_member // 2, block, channels)
        return call(
            functools.partial(grad_kernel, points, scale, block, centred),
            [(shape, BF16), (shape, F32)] + factors,
            [pltpu.VMEM((3 * channels, channels), F32)],
            "gradient", specs,
        )(me[None], turned, cotangent)
    found = call(
        functools.partial(grad_kernel, points, scale, None, centred),
        factors + [((3 * channels, channels), F32)],
        [], "gradient", specs,
    )(me[None], turned, cotangent)
    total = found[-1].reshape(n_member, block, channels)
    order = [lax.dynamic_index_in_dim(total, me ^ j, 0, keepdims=False) for j in range(n_member)]
    return (jnp.stack(order[1::2]).astype(BF16), jnp.stack(order[0::2])) + tuple(found[:-1])


def swap(value, axis, size, offset):
    return lax.ppermute(value, axis, [(i, i ^ offset) for i in range(size)])


def order_after(value, *others):
    return lax.optimization_barrier((value, others))[0]


TAIL = 64


def cut_of(rows):
    return -(-(rows + TAIL) // 32) * 16


def pack_kernel(*refs):
    sources, (early_ref, late_ref, rates_ref) = refs[:4], refs[4:7]
    held, sems = refs[7:11], refs[11]
    copies = [
        pltpu.make_async_copy(source, held[i], sems.at[i]) for i, source in enumerate(sources)
    ]
    for copy in copies:
        copy.start()
    cols, rows = held[0].shape
    size, cut = rows + TAIL, cut_of(rows)

    def packed(i):
        copies[i].wait()
        whole = held[i][...].T
        rest = jnp.concatenate(
            [whole[:, 128:cols], jnp.zeros((4 * TAIL - rows, cols - 128), BF16)], axis=0
        )
        rest = [rest[q * TAIL : (q + 1) * TAIL] for q in range(4)]
        return jnp.concatenate([whole[:, 0:128], jnp.concatenate(rest, axis=1)], axis=0)

    early_ref[0:size] = packed(0)
    second = packed(1)
    early_ref[size:] = second[0:cut]
    late_ref[...] = second[cut:]
    rates_ref[0] = packed(2)
    rates_ref[1] = packed(3)


def unpacked(block_of, rows, n_group):
    parts = []
    for g in range(n_group):
        block = block_of(g)
        rest = block[rows:]
        pieces = [rest[:, 32 * q : 32 * q + 32] for q in range(4)]
        parts += [block[0:rows], jnp.concatenate(pieces, axis=0)[0:rows]]
    return jnp.concatenate(parts, axis=1)


def split_kernel(*refs):
    count = len(refs) - 2
    one_ref, two_ref = refs[count:]
    size = one_ref.shape[1]
    for k, source in enumerate(refs[:count]):
        one_ref[k] = source[0:size]
        two_ref[k] = source[size:]


def weight_kernel(rows, n_group, place_ref, *refs):
    early_refs, late_refs, half_ref = refs[:n_group], refs[n_group:-1], refs[-1]
    for group in range(n_group):

        @pl.when(place_ref[0] == group)
        def _():
            @pl.loop(0, half_ref.shape[0])
            def _(k):
                def block_of(g):
                    parts = [early_refs[g ^ group][k]] + [ref[k, g ^ group] for ref in late_refs]
                    return jnp.concatenate(parts, axis=0)

                half_ref[k] = unpacked(block_of, rows, n_group)


def rate_kernel(rows, n_group, place_ref, packed_ref, one_ref, two_ref):
    group = place_ref[0]
    for which, out in enumerate((one_ref, two_ref)):
        out[...] = unpacked(lambda g: packed_ref[g ^ group, which], rows, n_group)


def along_z(value, n_member):
    chips = n_member // 2
    return [value] + [swap(value, "member", n_member, 2 * k) for k in range(1, chips)]


def across_groups(value, n_group):
    return [value] + [swap(value, "group", n_group, k) for k in range(1, n_group)]


def weights_and_rates(n_group, n_member, conv1, conv2, rate1, rate2, place, early):
    rows, cols = conv1.shape
    width = n_group * cols
    if (cols, n_group, rows % 16) != (160, 4, 0) or rows > 4 * TAIL:
        own = [lax.all_gather(w, "group", axis=1, tiled=True) for w in (conv1, conv2)]
        full = [lax.all_gather(w, "member", axis=0, tiled=True) for w in own]

        def rates(after):
            return [lax.all_gather(w, "group", axis=1, tiled=True) for w in (rate1, rate2)]

        return (full[0],), (full[1],), own[0], own[1], rates
    size, cut = rows + TAIL, cut_of(rows)
    early_rows, late_rows, both_rates = pl.pallas_call(
        pack_kernel,
        out_shape=(
            jax.ShapeDtypeStruct((size + cut, 128), BF16),
            jax.ShapeDtypeStruct((size - cut, 128), BF16),
            jax.ShapeDtypeStruct((2, size, 128), BF16),
        ),
        in_specs=[pl.BlockSpec(memory_space=pltpu.HBM)] * 4,
        out_specs=tuple(vmem(3)),
        scratch_shapes=[pltpu.VMEM((cols, rows), BF16)] * 4 + [pltpu.SemaphoreType.DMA((4,))],
        cost_estimate=pl.CostEstimate(flops=0, bytes_accessed=1024, transcendentals=0),
        name="pack",
    )(conv1.T, conv2.T, rate1.T, rate2.T)

    def unpack(*packed):
        shape = (n_member // 2, rows, width)
        (mine,) = call(
            functools.partial(weight_kernel, rows, n_group),
            [(shape, BF16)], [], "unpack", smem(1) + vmem(len(packed)),
        )(place, *packed)
        return place, mine, swap(mine, "member", n_member, 1)

    along = along_z(early_rows, n_member)
    late = jnp.stack(across_groups(order_after(late_rows, along[1]), n_group))
    along, late = order_after((along, late), early)
    chips = n_member // 2
    along_one, along_two = call(
        split_kernel,
        [((chips, size, 128), BF16), ((chips, cut, 128), BF16)], [], "split", vmem(chips),
    )(*along)
    crossed_one = across_groups(along_one, n_group)
    late = jnp.stack(along_z(order_after(late, crossed_one[1]), n_member))
    halves_one = unpack(*crossed_one)
    along_two = order_after(along_two, crossed_one)
    halves_two = unpack(*across_groups(along_two, n_group), late)

    def rates(after):
        blocks = jnp.stack(across_groups(order_after(both_rates, after), n_group))
        return call(
            functools.partial(rate_kernel, rows, n_group),
            [((rows, width), BF16)] * 2, [], "rates", smem(1) + vmem(1),
        )(place, blocks)

    return halves_one, halves_two, halves_one[1][0], halves_two[1][0], rates


def add_kernel(kept_ref, received_ref, *out_refs):
    away_ref, kept_out = out_refs[0], out_refs[1]

    for k in range(away_ref.shape[0]):
        away_ref[k] = (kept_ref[2 * k + 1] + received_ref[2 * k + 1].astype(F32)).astype(BF16)
        kept_out[k] = kept_ref[2 * k] + received_ref[2 * k].astype(F32)


def add_received(kept, received):
    half = (kept.shape[0] // 2,) + kept.shape[1:]
    return call(add_kernel, [(half, BF16), (half, F32)], [], "add", vmem(2))(kept, received)


def halve_to_owner(away, kept, received, n_member, bit=1):
    while True:
        if received is None:
            received = swap(away, "member", n_member, 2 * bit)
        if kept.shape[0] == 1:
            return kept[0], received[0]
        away, kept = add_received(kept, received)
        received = None
        bit *= 2


def update_kernel(own_ref, rate_ref, kept_ref, received_ref, *refs):
    total = kept_ref[...] + received_ref[...].astype(F32)
    if len(refs) > 1:
        total = total + refs[0][...]
    refs[-1][...] = own_ref[...].astype(F32) - rate_ref[...].astype(F32) * total


def update(*terms):
    shape = terms[0].shape
    return call(update_kernel, [(shape, F32)], [], "update", vmem(len(terms)))(*terms)[0]


def every_member(value, n_member):
    value = value[None]
    bit = 1
    while bit < n_member:
        value = jnp.concatenate([value, swap(value, "member", n_member, bit)])
        bit *= 2
    return value


def common_term(every, me, own_rows):
    mean = jnp.concatenate([every[:, 0]] * 3, axis=1)
    mean = lax.dynamic_slice_in_dim(mean, me * own_rows, own_rows, 1)
    return lax.dot_general(
        mean, every[:, 1], (((0,), (0,)), ((), ())), precision=lax.Precision.HIGHEST
    )


def shards(
    n_group,
    n_member,
    clips,
    targets,
    timestep,
    identity,
    conv1_weight,
    conv2_weight,
    rate1,
    rate2,
    time_proj,
    subject_table,
):
    frames, points, channels = (clips.shape[1], clips.shape[2], clips.shape[3])
    rows, padded = frames * points, (frames + 2) * points
    scale = 1.0 / math.sqrt(3 * channels)
    group, me = lax.axis_index("group"), lax.axis_index("member")
    place = jnp.stack([group, me]).astype(jnp.int32)
    own_rows = conv1_weight.shape[0]
    clip, target = clips.reshape(rows, channels), targets.reshape(rows, channels)
    blocks = np.arange(channels) // (channels // GN_GROUPS)
    same_group = jnp.asarray((blocks[:, None] == blocks[None, :]), BF16)

    bias_row = time_bias(timestep[0], identity[0], subject_table, time_proj)
    act_one, turned_one = call(
        functools.partial(enter_kernel, points),
        [((padded, channels), BF16), ((channels, rows), BF16)],
        [], "enter", vmem(2),
    )(clip, same_group)
    weight_one, weight_two, own_one, own_two, rates = weights_and_rates(
        n_group, n_member, conv1_weight, conv2_weight, rate1, rate2, place, (act_one, bias_row)
    )

    def weight_specs(weight):
        return vmem(1) if len(weight) == 1 else smem(1) + vmem(2)

    (hidden,) = call(
        functools.partial(first_kernel, points, scale),
        [((rows, channels), F32)],
        [pltpu.VMEM((3 * channels, channels), BF16)],
        "conv", vmem(2) + weight_specs(weight_one),
    )(act_one, bias_row, *weight_one)
    normal, inverse, act_two, turned_two = call(
        functools.partial(norm_kernel, points),
        [
            ((rows, channels), F32),
            ((1, channels), F32),
            ((padded, channels), BF16),
            ((channels, rows), BF16),
        ],
        [], "norm", vmem(2),
    )(order_after(hidden, weight_two[:2]), same_group)
    error, full_two = call(
        functools.partial(second_kernel, points, scale),
        [((padded, channels), BF16), ((3 * channels, channels), BF16)],
        [], "conv_error", vmem(3) + weight_specs(weight_two),
    )(act_two, clip, target, *weight_two)
    away_two, home_two, factors = gradient(
        turned_two, error, me, n_member, points, scale, True
    )
    received_two = swap(away_two, "member", n_member, 1)
    (grad_act,) = call(
        functools.partial(back_kernel, points, scale),
        [((rows, channels), F32)], [], "back", vmem(2),
    )(order_after(error, away_two), full_two)
    received_two, grad_act = lax.optimization_barrier((received_two, grad_act))
    away_two, kept_two = add_received(home_two, received_two)
    received_two = swap(away_two, "member", n_member, 2)
    rate_one, rate_two = rates(away_two)
    every = every_member(factors, n_member)
    (grad_hidden,) = call(
        functools.partial(norm_back_kernel, points),
        [((padded, channels), BF16)],
        [pltpu.VMEM((rows, channels), F32)],
        "norm_back", vmem(4),
    )(order_after(grad_act, away_two), normal, inverse, same_group)
    second = 1
    if kept_two.shape[0] > 1:
        second = 2
        away_two, kept_two = add_received(kept_two, received_two)
        received_two = None
    away_two, grad_hidden, every, rate_one, rate_two = lax.optimization_barrier(
        (away_two, grad_hidden, every, rate_one, rate_two)
    )
    away_one, home_one = gradient(
        turned_one, grad_hidden, me, n_member, points, scale, False
    )
    received_one = swap(away_one, "member", n_member, 1)
    common = common_term(every, me, own_rows)
    terms_two = halve_to_owner(away_two, kept_two, received_two, n_member, second)
    adapted_two = update(own_two, rate_two, *terms_two, common)
    away_one, kept_one = add_received(*order_after((home_one, received_one), terms_two[1]))
    adapted_one = update(
        own_one, rate_one, *halve_to_owner(away_one, kept_one, None, n_member)
    )
    return (adapted_one[None], adapted_two[None])


def solution(mesh):
    n_group, n_member = mesh.shape["group"], mesh.shape["member"]
    return jax.shard_map(
        lambda *arrays: shards(n_group, n_member, *arrays),
        mesh=mesh,
        in_specs=(
            P(("group", "member"), None, None, None),
            P(("group", "member"), None, None, None),
            P(("group", "member")),
            P(("group", "member")),
            P("member", "group"),
            P("member", "group"),
            P("member", "group"),
            P("member", "group"),
            P(),
            P(),
        ),
        out_specs=(P("group", "member", None), P("group", "member", None)),
        check_vma=False,
    )
```

```python
import functools
import math

import jax
import jax.numpy as jnp
import numpy as np
from jax import lax
from jax.experimental import pallas as pl
from jax.experimental.pallas import tpu as pltpu
from jax.sharding import PartitionSpec as P

GN_GROUPS = 32
CHUNK = 128
MEGA = 1024 * 1024
BF16 = jnp.bfloat16
F32 = jnp.float32


def time_bias(step_index, ident, subject_table, time_proj):
    half_width = subject_table.shape[1] // 2
    freqs = jnp.exp(-math.log(10000.0) * jnp.arange(half_width, dtype=F32) / half_width)
    angles = step_index.astype(F32) * freqs
    embedding = jnp.concatenate([jnp.cos(angles), jnp.sin(angles)])
    onehot = (jnp.arange(subject_table.shape[0], dtype=jnp.int32) == ident).astype(F32)
    embedding = embedding + jnp.dot(onehot, subject_table, precision=lax.Precision.HIGHEST)
    activated = jax.nn.silu(embedding).astype(BF16)
    return jnp.dot(activated[None, :], time_proj, preferred_element_type=F32)


def vmem(count):
    return [pl.BlockSpec(memory_space=pltpu.VMEM)] * count


def hbm(count):
    return [pl.BlockSpec(memory_space=pltpu.HBM)] * count


def smem(count):
    return [pl.BlockSpec(memory_space=pltpu.SMEM)] * count


def call(body, out_shape, scratch, name, in_specs):
    outs = len(out_shape)
    return pl.pallas_call(
        body,
        out_shape=tuple(jax.ShapeDtypeStruct(s, d) for s, d in out_shape),
        in_specs=in_specs,
        out_specs=tuple(vmem(outs)),
        scratch_shapes=scratch,
        compiler_params=pltpu.CompilerParams(vmem_limit_bytes=24 * MEGA),
        cost_estimate=pl.CostEstimate(flops=0, bytes_accessed=1024, transcendentals=0),
        name=name,
    )


def spread(row, same_group):
    high = row.astype(BF16)
    rest = row - high.astype(F32)
    middle = rest.astype(BF16)
    low = (rest - middle.astype(F32)).astype(BF16)
    stacked = jnp.concatenate(
        [jnp.broadcast_to(part, (16, row.shape[1])) for part in (high, middle, low)], axis=0
    )
    sums = jnp.dot(stacked, same_group, preferred_element_type=F32)
    return sums[0:1] + sums[16:17] + sums[32:33]


def norm_stats(read, rows, channels, same_group):
    counted = rows * (channels // GN_GROUPS)
    steps = rows // CHUNK
    total = lax.fori_loop(
        0,
        steps,
        lambda i, acc: acc + read(i).reshape(CHUNK // 8, 8, channels).sum(axis=0),
        jnp.zeros((8, channels), F32),
    ).sum(axis=0, keepdims=True)
    centre = spread(total, same_group) * (1.0 / counted)

    def squares(i, acc):
        centred = read(i) - centre
        return acc + (centred * centred).reshape(CHUNK // 8, 8, channels).sum(axis=0)

    square = lax.fori_loop(0, steps, squares, jnp.zeros((8, channels), F32)).sum(
        axis=0, keepdims=True
    )
    variance = spread(square, same_group) * (1.0 / counted)
    return centre, lax.rsqrt(variance + 1e-05)


def at(i, shift=0):
    return pl.ds(pl.multiple_of(i * CHUNK + shift, 64), CHUNK)


def clear_edges(padded_ref, points):
    edge = jnp.zeros((points, padded_ref.shape[1]), padded_ref.dtype)
    padded_ref[0:points] = edge
    padded_ref[padded_ref.shape[0] - points :] = edge


def fetch(sources, held, sems):
    copies = [
        pltpu.make_async_copy(source, place, sems.at[i])
        for i, (source, place) in enumerate(zip(sources, held))
    ]
    for copy in copies:
        copy.start()
    return copies


def enter_kernel(points, clip_hbm, same_hbm, padded_ref, turned_ref, same_ref, clip_ref, sems):
    rows, channels = clip_ref.shape
    for copy in fetch((clip_hbm, same_hbm), (clip_ref, same_ref), sems):
        copy.wait()
    centre, inverse = norm_stats(
        lambda i: clip_ref[at(i)].astype(F32), rows, channels, same_ref[...]
    )
    clear_edges(padded_ref, points)

    @pl.loop(0, rows // CHUNK)
    def _(i):
        normal = (clip_ref[at(i)].astype(F32) - centre) * inverse
        act = (normal / (1.0 + jnp.exp(-normal))).astype(BF16)
        padded_ref[at(i, points)] = act
        turned_ref[:, at(i)] = act.T


def taps_of(padded_ref, start, size, points):
    return jnp.concatenate(
        [padded_ref[pl.ds(start + t * points, size)] for t in range(3)], axis=1
    )


def full_weight(weight_refs, full_ref):
    if len(weight_refs) == 1:
        return weight_refs[0]
    place_ref, mine_ref, other_ref = weight_refs
    member, rows = place_ref[1], mine_ref.shape[1]

    @pl.loop(0, mine_ref.shape[0])
    def _(k):
        for half, source in ((0, mine_ref), (1, other_ref)):
            start = pl.multiple_of((member ^ (2 * k + half)) * rows, 16)
            full_ref[pl.ds(start, rows)] = source[k]

    return full_ref


def first_kernel(points, scale, in_ref, bias_ref, *refs):
    weight_refs = refs[:-2]
    hidden_ref, full_ref = refs[-2:]
    half = hidden_ref.shape[0] // 2
    bias = bias_ref[...]
    weight_ref = full_weight(weight_refs, full_ref)

    @pl.loop(0, 2)
    def _(i):
        start = pl.multiple_of(i * half, 64)
        mixed = jnp.dot(
            taps_of(in_ref, start, half, points), weight_ref[...], preferred_element_type=F32
        )
        hidden_ref[pl.ds(start, half)] = scale * mixed + bias


def norm_kernel(
    points, hidden_ref, same_ref, normal_ref, inverse_ref, padded_ref, turned_ref
):
    rows, channels = normal_ref.shape
    centre, inverse = norm_stats(lambda i: hidden_ref[at(i)], rows, channels, same_ref[...])
    inverse_ref[...] = inverse
    clear_edges(padded_ref, points)

    @pl.loop(0, rows // CHUNK)
    def _(i):
        normal = (hidden_ref[at(i)] - centre) * inverse
        normal_ref[at(i)] = normal
        act = (normal / (1.0 + jnp.exp(-normal))).astype(BF16)
        padded_ref[at(i, points)] = act
        turned_ref[:, at(i)] = act.T


def second_kernel(points, scale, in_ref, clip_hbm, target_hbm, *refs):
    weight_refs = refs[:-5]
    error_ref, full_ref, clip_ref, target_ref, sems = refs[-5:]
    copies = fetch((clip_hbm, target_hbm), (clip_ref, target_ref), sems)
    rows = clip_ref.shape[0]
    half = rows // 2
    clear_edges(error_ref, points)
    weight_ref = full_weight(weight_refs, full_ref)
    if len(weight_refs) == 1:
        full_ref[...] = weight_ref[...]
    for copy in copies:
        copy.wait()

    @pl.loop(0, 2)
    def _(i):
        start = pl.multiple_of(i * half, 64)
        mixed = jnp.dot(
            taps_of(in_ref, start, half, points), weight_ref[...], preferred_element_type=F32
        )
        here = pl.ds(start, half)
        output = clip_ref[here].astype(F32) + scale * mixed
        error_ref[pl.ds(pl.multiple_of(start + points, 64), half)] = (
            output - target_ref[here].astype(F32)
        ).astype(BF16)


def back_kernel(points, scale, error_ref, weight_ref, grad_ref):
    rows, channels = grad_ref.shape
    half = rows // 2
    last = (((1,), (1,)), ((), ()))

    @pl.loop(0, 2)
    def _(i):
        start = pl.multiple_of(i * half, 64)
        total = None
        for t in range(3):
            part = lax.dot_general(
                error_ref[pl.ds(pl.multiple_of(start + (2 - t) * points, 64), half)],
                weight_ref[t * channels : (t + 1) * channels],
                last,
                preferred_element_type=F32,
            )
            total = part if total is None else total + part
        grad_ref[pl.ds(start, half)] = scale * total


def norm_back_kernel(
    points, act_grad_ref, normal_ref, inverse_ref, same_ref, out_ref, grad_ref
):
    rows, channels = normal_ref.shape
    counted = rows * (channels // GN_GROUPS)

    def through(i, sums):
        normal = normal_ref[at(i)]
        gate = 1.0 / (1.0 + jnp.exp(-normal))
        grad = act_grad_ref[at(i)] * (gate * (1.0 + normal * (1.0 - gate)))
        grad_ref[at(i)] = grad

        def fold(value):
            return value.reshape(CHUNK // 8, 8, channels).sum(axis=0)

        return sums[0] + fold(grad), sums[1] + fold(grad * normal)

    zero = jnp.zeros((8, channels), F32)
    plain, crossed = lax.fori_loop(0, rows // CHUNK, through, (zero, zero))
    same_group = same_ref[...]
    mean = spread(plain.sum(axis=0, keepdims=True), same_group) * (1.0 / counted)
    slope = spread(crossed.sum(axis=0, keepdims=True), same_group) * (1.0 / counted)
    inverse = inverse_ref[...]
    clear_edges(out_ref, points)

    @pl.loop(0, rows // CHUNK)
    def _(i):
        value = (grad_ref[at(i)] - mean - normal_ref[at(i)] * slope) * inverse
        out_ref[at(i, points)] = value.astype(BF16)


FACTOR_ROWS = 16


def split_rows(row):
    high = row.astype(BF16).astype(F32)
    middle = (row - high).astype(BF16).astype(F32)
    return [high, middle, row - high - middle]


def grad_kernel(points, scale, block, centred, me_ref, turned_ref, cotangent_ref, *refs):
    channels, rows = turned_ref.shape
    refs = list(refs)
    total_ref = refs.pop()
    if centred:
        ones = jnp.ones((rows, 128), BF16)
        mean = jnp.dot(turned_ref[...], ones, preferred_element_type=F32) * (1.0 / rows)
        sums = scale * jnp.dot(
            jnp.ones((16, rows), BF16),
            cotangent_ref[pl.ds(points, rows)],
            preferred_element_type=F32,
        )
        factors = split_rows(mean.T[0:1]) + split_rows(sums[0:1])
        factors += [jnp.zeros((FACTOR_ROWS - len(factors), channels), F32)]
        factors = jnp.concatenate(factors, axis=0)
        common = jnp.concatenate([mean] * (channels // 128), axis=1) * sums[0:1]

    @pl.loop(0, 3)
    def _(t):
        shifted = cotangent_ref[pl.ds(pl.multiple_of((2 - t) * points, 64), rows)]
        product = scale * jnp.dot(turned_ref[...], shifted, preferred_element_type=F32)
        if centred:
            product = product - common
        total_ref[pl.ds(pl.multiple_of(t * channels, 128), channels)] = product

    if block is not None:
        away_ref, home_ref = refs[:2]
        me = me_ref[0]
        count = home_ref.shape[0]

        @pl.loop(0, count)
        def _(j):
            away = pl.multiple_of((me ^ (2 * j + 1)) * block, 16)
            home = pl.multiple_of((me ^ (2 * j)) * block, 16)
            place = pl.ds(pl.multiple_of(j * block, 16), block)
            away_ref[place] = total_ref[pl.ds(away, block)].astype(BF16)
            home_ref[j] = total_ref[pl.ds(home, block)]

        if centred:
            away_ref[count * block :] = factors.astype(BF16)
    elif centred:
        refs[0][...] = factors


def gradient(turned, cotangent, me, n_member, points, scale, centred):
    channels, rows = turned.shape
    block = 3 * channels // n_member
    specs = smem(1) + vmem(2)
    if block % 16 == 0:
        chips = n_member // 2
        extra = FACTOR_ROWS if centred else 0
        return call(
            functools.partial(grad_kernel, points, scale, block, centred),
            [((chips * block + extra, channels), BF16), ((chips, block, channels), F32)],
            [pltpu.VMEM((3 * channels, channels), F32)],
            "gradient", specs,
        )(me[None], turned, cotangent)
    factors = [((FACTOR_ROWS, channels), F32)] if centred else []
    found = call(
        functools.partial(grad_kernel, points, scale, None, centred),
        factors + [((3 * channels, channels), F32)],
        [], "gradient", specs,
    )(me[None], turned, cotangent)
    total = found[-1].reshape(n_member, block, channels)
    order = [lax.dynamic_index_in_dim(total, me ^ j, 0, keepdims=False) for j in range(n_member)]
    away, home = jnp.stack(order[1::2]).astype(BF16), jnp.stack(order[0::2])
    return (away, home) + tuple(found[:-1])


def swap(value, axis, size, offset):
    return lax.ppermute(value, axis, [(i, i ^ offset) for i in range(size)])


def order_after(value, *others):
    return lax.optimization_barrier((value, others))[0]


TAIL = 64


def cut_of(rows):
    return (rows + TAIL) * 3 // 128 * 16


def pack_kernel(*refs):
    sources, (early_ref, late_ref, rates_ref) = refs[:4], refs[4:7]
    held, sems = refs[7:11], refs[11]
    copies = fetch(sources, held, sems)
    cols, rows = held[0].shape
    size, cut = rows + TAIL, cut_of(rows)

    def packed(i):
        copies[i].wait()
        whole = held[i][...].T
        rest = jnp.concatenate(
            [whole[:, 128:cols], jnp.zeros((4 * TAIL - rows, cols - 128), BF16)], axis=0
        )
        rest = [rest[q * TAIL : (q + 1) * TAIL] for q in range(4)]
        return jnp.concatenate([whole[:, 0:128], jnp.concatenate(rest, axis=1)], axis=0)

    early_ref[0:size] = packed(0)
    second = packed(1)
    early_ref[size:] = second[0:cut]
    late_ref[...] = second[cut:]
    rates_ref[0] = packed(2)
    rates_ref[1] = packed(3)


def unpacked(block_of, rows, n_group):
    parts = []
    for g in range(n_group):
        block = block_of(g)
        rest = block[rows:]
        pieces = [rest[:, 32 * q : 32 * q + 32] for q in range(4)]
        parts += [block[0:rows], jnp.concatenate(pieces, axis=0)[0:rows]]
    return jnp.concatenate(parts, axis=1)


def split_kernel(*refs):
    first_ref, second_ref, two_ref = refs[-3:]
    half, size = first_ref.shape[0], first_ref.shape[1]
    for k, source in enumerate(refs[:-3]):
        (first_ref if k < half else second_ref)[k % half] = source[0:size]
        two_ref[k] = source[size:]


def for_group(place_ref, n_group, half_ref, rows, block_of):
    for group in range(n_group):

        @pl.when(place_ref[0] == group)
        def _():
            block_of(
                lambda k, pick: half_ref.__setitem__(
                    k, unpacked(lambda g: pick(g ^ group), rows, n_group)
                )
            )


def two_step_kernel(rows, place_ref, *refs):
    first, first_x, first_y, second, second_y, second_x, half_ref = refs
    half = half_ref.shape[0] // 2

    def fill(store):
        @pl.loop(0, half)
        def _(k):
            pick = (first, first_x, first_y.at[0], first_y.at[1])
            store(k, lambda d: pick[d][k])
            late = (second, second_x.at[0], second_y, second_x.at[1])
            store(half + k, lambda d: late[d][k])

    for_group(place_ref, 4, half_ref, rows, fill)


def direct_kernel(rows, n_group, place_ref, *refs):
    early_refs, late_refs, half_ref = refs[:n_group], refs[n_group:-1], refs[-1]

    def fill(store):
        @pl.loop(0, half_ref.shape[0] // 2)
        def _(i):
            for odd, late_ref in enumerate(late_refs):
                k = 2 * i + odd
                store(k, lambda d: jnp.concatenate([early_refs[d][k], late_ref[i, d]], axis=0))

    for_group(place_ref, n_group, half_ref, rows, fill)


def rate_kernel(rows, n_group, place_ref, packed_ref, one_ref, two_ref):
    group = place_ref[0]
    for which, out in enumerate((one_ref, two_ref)):
        out[...] = unpacked(lambda g: packed_ref[g ^ group, which], rows, n_group)


def along_z(value, n_member):
    chips = n_member // 2
    return [value] + [swap(value, "member", n_member, 2 * k) for k in range(1, chips)]


def across_groups(value, n_group):
    return [value] + [swap(value, "group", n_group, k) for k in range(1, n_group)]


def weights_and_rates(n_group, n_member, conv1, conv2, rate1, rate2, place, clip, enter, bias_row):
    rows, cols = conv1.shape
    width = n_group * cols
    if (cols, n_group, n_member, rows % 16) != (160, 4, 8, 0) or rows > 4 * TAIL:
        own = [lax.all_gather(w, "group", axis=1, tiled=True) for w in (conv1, conv2)]
        full = [lax.all_gather(w, "member", axis=0, tiled=True) for w in own]

        def rates(after):
            return [lax.all_gather(w, "group", axis=1, tiled=True) for w in (rate1, rate2)]

        second = lambda after: (full[1], own[1][None])
        return (full[0],), second, own[0][None], rates, enter(clip), bias_row
    size, cut, chips = rows + TAIL, cut_of(rows), n_member // 2
    early_rows, late, both_rates = pl.pallas_call(
        pack_kernel,
        out_shape=(
            jax.ShapeDtypeStruct((size + cut, 128), BF16),
            jax.ShapeDtypeStruct((size - cut, 128), BF16),
            jax.ShapeDtypeStruct((2, size, 128), BF16),
        ),
        in_specs=hbm(4),
        out_specs=tuple(vmem(3)),
        scratch_shapes=[pltpu.VMEM((cols, rows), BF16)] * 4 + [pltpu.SemaphoreType.DMA((4,))],
        compiler_params=pltpu.CompilerParams(vmem_limit_bytes=40 * MEGA),
        cost_estimate=pl.CostEstimate(flops=0, bytes_accessed=1024, transcendentals=0),
        name="pack",
    )(conv1.T, conv2.T, rate1.T, rate2.T)

    def unpack(kernel, *packed):
        (mine,) = call(
            kernel, [((chips, rows, width), BF16)], [], "unpack", smem(1) + vmem(len(packed))
        )(place, *packed)
        return place, mine, swap(mine, "member", n_member, 1)

    along = along_z(early_rows, n_member)
    late_x = swap(late, "group", n_group, 1)
    late_x, bias_row = order_after((late_x, bias_row), ())
    late = jnp.stack([late, late_x])
    late_y = swap(late, "group", n_group, 2)
    act = enter(order_after(clip, (late, bias_row)))
    along, late_y, act = order_after((along, late_y, act), ())
    first, second, along_two = call(
        split_kernel,
        [((chips // 2, size, 128), BF16)] * 2 + [((chips, cut, 128), BF16)], [],
        "split", vmem(chips),
    )(*along)
    first_x = swap(first, "group", n_group, 1)
    second_y = swap(second, "group", n_group, 2)
    late = order_after(jnp.concatenate([late, late_y]), first)
    late = [late]
    late_z = swap(late[0], "member", n_member, 2 * (chips // 2))
    first_y = swap(jnp.stack([first, first_x]), "group", n_group, 2)
    second_x = swap(jnp.stack([second, second_y]), "group", n_group, 1)
    late = jnp.stack(late + [late_z])
    late_z = swap(late, "member", n_member, 2)
    halves_one = unpack(
        functools.partial(two_step_kernel, rows),
        order_after(first, late), first_x, first_y, second, second_y, second_x,
    )
    along_two = across_groups(order_after(along_two, halves_one[1]), n_group)

    def halves_two(after):
        kernel = functools.partial(direct_kernel, rows, n_group)
        return unpack(kernel, *along_two, *order_after((late, late_z), after))

    def rates(after):
        blocks = jnp.stack(across_groups(order_after(both_rates, after), n_group))
        return call(
            functools.partial(rate_kernel, rows, n_group),
            [((rows, width), BF16)] * 2, [], "rates", smem(1) + vmem(1),
        )(place, blocks)

    return halves_one, halves_two, halves_one[1], rates, act, bias_row


def add_kernel(kept_ref, received_ref, *out_refs):
    away_ref, kept_out = out_refs[0], out_refs[1]

    for k in range(away_ref.shape[0]):
        away_ref[k] = (kept_ref[2 * k + 1] + received_ref[2 * k + 1].astype(F32)).astype(BF16)
        kept_out[k] = kept_ref[2 * k] + received_ref[2 * k].astype(F32)


def add_received(kept, received):
    half = (kept.shape[0] // 2,) + kept.shape[1:]
    return call(add_kernel, [(half, BF16), (half, F32)], [], "add", vmem(2))(kept, received)


def halve_to_owner(away, kept, received, n_member, bit=1):
    while True:
        if received is None:
            received = swap(away, "member", n_member, 2 * bit)
        if kept.shape[0] == 1:
            return kept[0], received[0]
        away, kept = add_received(kept, received)
        received = None
        bit *= 2


def pair_kernel(own_ref, home_ref, received_ref, far_ref, near_ref, middle_ref, kept_ref):
    rows = home_ref.shape[1]
    for k, out in ((3, far_ref), (1, near_ref), (2, middle_ref), (0, kept_ref)):
        total = home_ref[k] + received_ref[k * rows : (k + 1) * rows].astype(F32)
        out[0:rows] = total.astype(out.dtype)
    last = home_ref.shape[0] * rows
    if far_ref.shape[0] > rows:
        far_ref[rows : rows + FACTOR_ROWS] = own_ref[last:]
        far_ref[rows + FACTOR_ROWS :] = received_ref[last:]


def pair_sums(own, home, received):
    chips, rows, channels = home.shape
    shape = (rows, channels)
    extra = 2 * (own.shape[0] - chips * rows)
    return call(
        pair_kernel,
        [((rows + extra, channels), BF16), (shape, BF16), (shape, F32), (shape, F32)], [],
        "pair", vmem(3),
    )(own, home, received)


def merge_kernel(middle_ref, sent_ref, received_ref, out_ref):
    rows = middle_ref.shape[0]
    known = sent_ref.shape[0] - rows
    out_ref[0:rows] = (middle_ref[...] + received_ref[0:rows].astype(F32)).astype(BF16)
    if known:
        out_ref[rows : rows + known] = sent_ref[rows:]
        out_ref[rows + known :] = received_ref[rows:]


def merge(middle, sent, received):
    rows, channels = middle.shape
    shape = (2 * sent.shape[0] - rows, channels)
    return call(merge_kernel, [(shape, BF16)], [], "merge", vmem(3))(middle, sent, received)[0]


def update_kernel(own_ref, rate_ref, *refs):
    rows = rate_ref.shape[0]
    total = refs[0][...]
    for ref in refs[1:-1]:
        total = total + ref[0:rows].astype(F32)
    refs[-1][...] = own_ref[0].astype(F32) - rate_ref[...].astype(F32) * total


def update(own, rate, *terms):
    shape = rate.shape
    return call(
        update_kernel, [(shape, F32)], [], "update", vmem(2 + len(terms)),
    )(own, rate, *terms)[0]


def common_term(every, me, own_rows):
    every = every.astype(F32)
    mean = every[:, 0] + every[:, 1] + every[:, 2]
    sums = every[:, 3] + every[:, 4] + every[:, 5]
    mean = jnp.concatenate([mean] * 3, axis=1)
    mean = lax.dynamic_slice_in_dim(mean, me * own_rows, own_rows, 1)
    return lax.dot_general(
        mean, sums, (((0,), (0,)), ((), ())), precision=lax.Precision.HIGHEST
    )


def shards(
    n_group,
    n_member,
    clips,
    targets,
    timestep,
    identity,
    conv1_weight,
    conv2_weight,
    rate1,
    rate2,
    time_proj,
    subject_table,
):
    frames, points, channels = (clips.shape[1], clips.shape[2], clips.shape[3])
    rows, padded = frames * points, (frames + 2) * points
    scale = 1.0 / math.sqrt(3 * channels)
    group, me = lax.axis_index("group"), lax.axis_index("member")
    place = jnp.stack([group, me]).astype(jnp.int32)
    own_rows = conv1_weight.shape[0]
    clip, target = clips.reshape(rows, channels), targets.reshape(rows, channels)
    blocks = np.arange(channels) // (channels // GN_GROUPS)
    same_group = jnp.asarray((blocks[:, None] == blocks[None, :]), BF16)

    bias_row = time_bias(timestep[0], identity[0], subject_table, time_proj)

    def enter(clip):
        return call(
            functools.partial(enter_kernel, points),
            [((padded, channels), BF16), ((channels, rows), BF16), (same_group.shape, BF16)],
            [pltpu.VMEM((rows, channels), BF16), pltpu.SemaphoreType.DMA((2,))],
            "enter", hbm(2),
        )(clip, same_group)

    weight_one, weight_two, own_one, rates, acts, bias_row = weights_and_rates(
        n_group, n_member, conv1_weight, conv2_weight, rate1, rate2, place, clip, enter, bias_row
    )
    act_one, turned_one, same_group = acts

    def weight_specs(weight):
        return vmem(1) if len(weight) == 1 else smem(1) + vmem(2)

    (hidden,) = call(
        functools.partial(first_kernel, points, scale),
        [((rows, channels), F32)],
        [pltpu.VMEM((3 * channels, channels), BF16)],
        "conv", vmem(2) + weight_specs(weight_one),
    )(act_one, bias_row, *weight_one)
    weight_two = weight_two(hidden)
    own_two = weight_two[1]
    if len(weight_two) == 2:
        weight_two = weight_two[:1]
    normal, inverse, act_two, turned_two = call(
        functools.partial(norm_kernel, points),
        [
            ((rows, channels), F32),
            ((1, channels), F32),
            ((padded, channels), BF16),
            ((channels, rows), BF16),
        ],
        [], "norm", vmem(2),
    )(order_after(hidden, weight_two[:2]), same_group)
    error, full_two = call(
        functools.partial(second_kernel, points, scale),
        [((padded, channels), BF16), ((3 * channels, channels), BF16)],
        [pltpu.VMEM((rows, channels), BF16)] * 2 + [pltpu.SemaphoreType.DMA((2,))],
        "conv_error", vmem(1) + hbm(2) + weight_specs(weight_two),
    )(act_two, clip, target, *weight_two)
    away_two, home_two, *factors = gradient(
        turned_two, error, me, n_member, points, scale, True
    )
    received_two = swap(away_two, "member", n_member, 1)
    (grad_act,) = call(
        functools.partial(back_kernel, points, scale),
        [((rows, channels), F32)], [], "back", vmem(2),
    )(order_after(error, away_two), full_two)
    staged = n_member == 8 and not factors
    received_two, grad_act = lax.optimization_barrier((received_two, grad_act))
    if staged:
        far_two, near_two, middle_two, kept_two = pair_sums(away_two, home_two, received_two)
        from_two = swap(far_two, "member", n_member, 2)
        grad_act = order_after(grad_act, far_two)
    (grad_hidden,) = call(
        functools.partial(norm_back_kernel, points),
        [((padded, channels), BF16)],
        [pltpu.VMEM((rows, channels), F32)],
        "norm_back", vmem(4),
    )(grad_act, normal, inverse, same_group)
    away_one, home_one = gradient(
        turned_one, grad_hidden, me, n_member, points, scale, False
    )
    if staged:
        away_one, from_two = order_after((away_one, from_two), ())
        received_one = swap(away_one, "member", n_member, 1)
        merged_two = merge(middle_two, far_two, from_two)
        across_two = swap(merged_two, "member", n_member, 4)
        beside_two = swap(order_after(near_two, from_two), "member", n_member, 2)
        far_one, near_one, middle_one, kept_one = pair_sums(away_one, home_one, received_one)
        from_one = swap(far_one, "member", n_member, 2)
        rate_one, rate_two = rates(far_one)
        middle_one = order_after(middle_one, (rate_one, rate_two))
        merged_one = merge(middle_one, far_one, from_one)
        terms_one = [
            kept_one,
            swap(merged_one, "member", n_member, 4),
            swap(order_after(near_one, from_one), "member", n_member, 2),
        ]
        across_two, beside_two = order_after((across_two, beside_two), merged_one)
        terms_two = [kept_two, across_two, beside_two]
        every = jnp.concatenate([merged_two[own_rows:], across_two[own_rows:]])
        every = every.reshape(n_member, FACTOR_ROWS, channels)
    else:
        received_one = swap(away_one, "member", n_member, 1)
        rate_one, rate_two = rates(away_one)
        every = lax.all_gather(factors[0], "member")
        terms_two = halve_to_owner(*add_received(home_two, received_two), None, n_member)
        terms_one = halve_to_owner(*add_received(home_one, received_one), None, n_member)
    adapted_two = update(own_two, rate_two, *terms_two, common_term(every, me, own_rows))
    adapted_one = update(own_one, rate_one, *terms_one)
    return (adapted_one[None], adapted_two[None])


def solution(mesh):
    n_group, n_member = mesh.shape["group"], mesh.shape["member"]
    return jax.shard_map(
        lambda *arrays: shards(n_group, n_member, *arrays),
        mesh=mesh,
        in_specs=(
            P(("group", "member"), None, None, None),
            P(("group", "member"), None, None, None),
            P(("group", "member")),
            P(("group", "member")),
            P("member", "group"),
            P("member", "group"),
            P("member", "group"),
            P("member", "group"),
            P(),
            P(),
        ),
        out_specs=(P("group", "member", None), P("group", "member", None)),
        check_vma=False,
    )
```

```python
import functools
import math

import jax
import jax.numpy as jnp
import numpy as np
from jax import lax
from jax.experimental import pallas as pl
from jax.experimental.pallas import tpu as pltpu
from jax.sharding import PartitionSpec as P

GN_GROUPS = 32
CHUNK = 128
MEGA = 1024 * 1024
BF16 = jnp.bfloat16
F32 = jnp.float32


def time_bias(step_index, ident, subject_table, time_proj):
    half_width = subject_table.shape[1] // 2
    freqs = jnp.exp(-math.log(10000.0) * jnp.arange(half_width, dtype=F32) / half_width)
    angles = step_index.astype(F32) * freqs
    embedding = jnp.concatenate([jnp.cos(angles), jnp.sin(angles)])
    onehot = (jnp.arange(subject_table.shape[0], dtype=jnp.int32) == ident).astype(F32)
    embedding = embedding + jnp.dot(onehot, subject_table, precision=lax.Precision.HIGHEST)
    activated = jax.nn.silu(embedding).astype(BF16)
    return jnp.dot(activated[None, :], time_proj, preferred_element_type=F32)


def vmem(count):
    return [pl.BlockSpec(memory_space=pltpu.VMEM)] * count


def hbm(count):
    return [pl.BlockSpec(memory_space=pltpu.HBM)] * count


def smem(count):
    return [pl.BlockSpec(memory_space=pltpu.SMEM)] * count


def call(body, out_shape, scratch, name, in_specs, limit=8):
    outs = len(out_shape)
    return pl.pallas_call(
        body,
        out_shape=tuple(jax.ShapeDtypeStruct(s, d) for s, d in out_shape),
        in_specs=in_specs,
        out_specs=tuple(vmem(outs)),
        scratch_shapes=scratch,
        compiler_params=pltpu.CompilerParams(vmem_limit_bytes=limit * MEGA),
        cost_estimate=pl.CostEstimate(flops=0, bytes_accessed=1024, transcendentals=0),
        name=name,
    )


def spread(row, same_group):
    high = row.astype(BF16)
    rest = row - high.astype(F32)
    middle = rest.astype(BF16)
    low = (rest - middle.astype(F32)).astype(BF16)
    stacked = jnp.concatenate(
        [jnp.broadcast_to(part, (16, row.shape[1])) for part in (high, middle, low)], axis=0
    )
    sums = jnp.dot(stacked, same_group, preferred_element_type=F32)
    return sums[0:1] + sums[16:17] + sums[32:33]


def norm_stats(read, rows, channels, same_ref, copy=None):
    counted = rows * (channels // GN_GROUPS)
    steps = rows // CHUNK
    total = lax.fori_loop(
        0,
        steps,
        lambda i, acc: acc + read(i).reshape(CHUNK // 8, 8, channels).sum(axis=0),
        jnp.zeros((8, channels), F32),
    ).sum(axis=0, keepdims=True)
    if copy is not None:
        copy.wait()
    same_group = same_ref[...]
    centre = spread(total, same_group) * (1.0 / counted)

    def squares(i, acc):
        centred = read(i) - centre
        return acc + (centred * centred).reshape(CHUNK // 8, 8, channels).sum(axis=0)

    square = lax.fori_loop(0, steps, squares, jnp.zeros((8, channels), F32)).sum(
        axis=0, keepdims=True
    )
    variance = spread(square, same_group) * (1.0 / counted)
    return centre, lax.rsqrt(variance + 1e-05)


def at(i, shift=0):
    return pl.ds(pl.multiple_of(i * CHUNK + shift, 64), CHUNK)


def clear_edges(padded_ref, points):
    edge = jnp.zeros((points, padded_ref.shape[1]), padded_ref.dtype)
    padded_ref[0:points] = edge
    padded_ref[padded_ref.shape[0] - points :] = edge


def fetch(sources, held, sems):
    copies = [
        pltpu.make_async_copy(source, place, sems.at[i])
        for i, (source, place) in enumerate(zip(sources, held))
    ]
    for copy in copies:
        copy.start()
    return copies


def enter_kernel(points, clip_hbm, same_hbm, padded_ref, clip_ref, same_ref, sems):
    rows, channels = clip_ref.shape
    for copy in fetch((clip_hbm, same_hbm), (clip_ref, same_ref), sems):
        copy.wait()
    centre, inverse = norm_stats(
        lambda i: clip_ref[at(i)].astype(F32), rows, channels, same_ref
    )
    clear_edges(padded_ref, points)

    @pl.loop(0, rows // CHUNK)
    def _(i):
        normal = (clip_ref[at(i)].astype(F32) - centre) * inverse
        padded_ref[at(i, points)] = (normal / (1.0 + jnp.exp(-normal))).astype(BF16)


def taps_of(padded_ref, start, size, points):
    return jnp.concatenate(
        [padded_ref[pl.ds(start + t * points, size)] for t in range(3)], axis=1
    )


def full_weight(weight_refs, full_ref):
    if len(weight_refs) == 1:
        return weight_refs[0]
    member_ref, mine_ref, other_ref = weight_refs
    member, rows = member_ref[0], mine_ref.shape[1]

    @pl.loop(0, mine_ref.shape[0])
    def _(k):
        for half, source in ((0, mine_ref), (1, other_ref)):
            start = pl.multiple_of((member ^ (2 * k + half)) * rows, 16)
            full_ref[pl.ds(start, rows)] = source[k]

    return full_ref


def first_kernel(points, scale, in_ref, bias_ref, *refs):
    weight_refs = refs[:-2]
    hidden_ref, full_ref = refs[-2:]
    half = hidden_ref.shape[0] // 2
    bias = bias_ref[...]
    weight_ref = full_weight(weight_refs, full_ref)

    @pl.loop(0, 2)
    def _(i):
        start = pl.multiple_of(i * half, 64)
        mixed = jnp.dot(
            taps_of(in_ref, start, half, points), weight_ref[...], preferred_element_type=F32
        )
        hidden_ref[pl.ds(start, half)] = scale * mixed + bias


def norm_kernel(
    points, hidden_ref, same_hbm, normal_ref, inverse_ref, padded_ref, turned_ref, same_ref, sems
):
    rows, channels = normal_ref.shape
    (copy,) = fetch((same_hbm,), (same_ref,), sems)
    centre, inverse = norm_stats(lambda i: hidden_ref[at(i)], rows, channels, same_ref, copy)
    inverse_ref[...] = inverse
    clear_edges(padded_ref, points)

    @pl.loop(0, rows // CHUNK)
    def _(i):
        normal = (hidden_ref[at(i)] - centre) * inverse
        normal_ref[at(i)] = normal
        act = (normal / (1.0 + jnp.exp(-normal))).astype(BF16)
        padded_ref[at(i, points)] = act
        turned_ref[:, at(i)] = act.T


def second_kernel(points, scale, in_ref, clip_hbm, target_hbm, *refs):
    weight_refs = refs[:-5]
    error_ref, full_ref, clip_ref, target_ref, sems = refs[-5:]
    copies = fetch((clip_hbm, target_hbm), (clip_ref, target_ref), sems)
    rows = clip_ref.shape[0]
    half = rows // 2
    clear_edges(error_ref, points)
    weight_ref = full_weight(weight_refs, full_ref)
    if len(weight_refs) == 1:
        full_ref[...] = weight_ref[...]
    for copy in copies:
        copy.wait()

    @pl.loop(0, 2)
    def _(i):
        start = pl.multiple_of(i * half, 64)
        mixed = jnp.dot(
            taps_of(in_ref, start, half, points), weight_ref[...], preferred_element_type=F32
        )
        here = pl.ds(start, half)
        output = clip_ref[here].astype(F32) + scale * mixed
        error_ref[pl.ds(pl.multiple_of(start + points, 64), half)] = (
            output - target_ref[here].astype(F32)
        ).astype(BF16)


def back_kernel(points, scale, error_ref, weight_ref, grad_ref):
    rows, channels = grad_ref.shape
    half = rows // 2
    last = (((1,), (1,)), ((), ()))

    @pl.loop(0, 2)
    def _(i):
        start = pl.multiple_of(i * half, 64)
        total = None
        for t in range(3):
            part = lax.dot_general(
                error_ref[pl.ds(pl.multiple_of(start + (2 - t) * points, 64), half)],
                weight_ref[t * channels : (t + 1) * channels],
                last,
                preferred_element_type=F32,
            )
            total = part if total is None else total + part
        grad_ref[pl.ds(start, half)] = scale * total


def norm_back_kernel(
    points, act_grad_ref, normal_ref, inverse_ref, same_hbm, out_ref, grad_ref, same_ref, sems
):
    (copy,) = fetch((same_hbm,), (same_ref,), sems)
    rows, channels = normal_ref.shape
    counted = rows * (channels // GN_GROUPS)

    def through(i, sums):
        normal = normal_ref[at(i)]
        gate = 1.0 / (1.0 + jnp.exp(-normal))
        grad = act_grad_ref[at(i)] * (gate * (1.0 + normal * (1.0 - gate)))
        grad_ref[at(i)] = grad

        def fold(value):
            return value.reshape(CHUNK // 8, 8, channels).sum(axis=0)

        return sums[0] + fold(grad), sums[1] + fold(grad * normal)

    zero = jnp.zeros((8, channels), F32)
    plain, crossed = lax.fori_loop(0, rows // CHUNK, through, (zero, zero))
    copy.wait()
    same_group = same_ref[...]
    mean = spread(plain.sum(axis=0, keepdims=True), same_group) * (1.0 / counted)
    slope = spread(crossed.sum(axis=0, keepdims=True), same_group) * (1.0 / counted)
    inverse = inverse_ref[...]
    clear_edges(out_ref, points)

    @pl.loop(0, rows // CHUNK)
    def _(i):
        value = (grad_ref[at(i)] - mean - normal_ref[at(i)] * slope) * inverse
        out_ref[at(i, points)] = value.astype(BF16)


FACTOR_ROWS = 16


def split_rows(row):
    high = row.astype(BF16).astype(F32)
    middle = (row - high).astype(BF16).astype(F32)
    return [high, middle, row - high - middle]


def grad_kernel(points, scale, block, centred, me_ref, act_ref, cotangent_ref, *refs):
    refs = list(refs)
    turned_ref = refs.pop()
    total_ref = refs.pop()
    if act_ref.shape == turned_ref.shape:
        turned_ref = act_ref
    channels, rows = turned_ref.shape
    if turned_ref is not act_ref:

        @pl.loop(0, rows // CHUNK)
        def _(i):
            turned_ref[:, at(i)] = act_ref[at(i, points)].T

    if centred:
        ones = jnp.ones((rows, 128), BF16)
        mean = jnp.dot(turned_ref[...], ones, preferred_element_type=F32) * (1.0 / rows)
        sums = scale * jnp.dot(
            jnp.ones((16, rows), BF16),
            cotangent_ref[pl.ds(points, rows)],
            preferred_element_type=F32,
        )
        factors = split_rows(mean.T[0:1]) + split_rows(sums[0:1])
        factors += [jnp.zeros((FACTOR_ROWS - len(factors), channels), F32)]
        factors = jnp.concatenate(factors, axis=0)
        common = jnp.concatenate([mean] * (channels // 128), axis=1) * sums[0:1]

    @pl.loop(0, 3)
    def _(t):
        shifted = cotangent_ref[pl.ds(pl.multiple_of((2 - t) * points, 64), rows)]
        product = scale * jnp.dot(turned_ref[...], shifted, preferred_element_type=F32)
        if centred:
            product = product - common
        total_ref[pl.ds(pl.multiple_of(t * channels, 128), channels)] = product

    if block is not None:
        away_ref, home_ref = refs[:2]
        me = me_ref[0]
        count = home_ref.shape[0]

        @pl.loop(0, count)
        def _(j):
            away = pl.multiple_of((me ^ (2 * j + 1)) * block, 16)
            home = pl.multiple_of((me ^ (2 * j)) * block, 16)
            place = pl.ds(pl.multiple_of(j * block, 16), block)
            away_ref[place] = total_ref[pl.ds(away, block)].astype(BF16)
            home_ref[j] = total_ref[pl.ds(home, block)]

        if centred:
            away_ref[count * block :] = factors.astype(BF16)
    elif centred:
        refs[0][...] = factors


def gradient(act, cotangent, me, n_member, points, scale, centred):
    channels, rows = cotangent.shape[1], cotangent.shape[0] - 2 * points
    turned = pltpu.VMEM((channels, rows), BF16)
    block = 3 * channels // n_member
    specs = smem(1) + vmem(2)
    if block % 16 == 0:
        chips = n_member // 2
        extra = FACTOR_ROWS if centred else 0
        return call(
            functools.partial(grad_kernel, points, scale, block, centred),
            [((chips * block + extra, channels), BF16), ((chips, block, channels), F32)],
            [pltpu.VMEM((3 * channels, channels), F32), turned],
            "gradient", specs, 24,
        )(me, act, cotangent)
    factors = [((FACTOR_ROWS, channels), F32)] if centred else []
    found = call(
        functools.partial(grad_kernel, points, scale, None, centred),
        factors + [((3 * channels, channels), F32)],
        [turned], "gradient", specs, 24,
    )(me, act, cotangent)
    total = found[-1].reshape(n_member, block, channels)
    order = [lax.dynamic_index_in_dim(total, me[0] ^ j, 0, keepdims=False) for j in range(n_member)]
    away, home = jnp.stack(order[1::2]).astype(BF16), jnp.stack(order[0::2])
    return (away, home) + tuple(found[:-1])


def swap(value, axis, size, offset):
    return lax.ppermute(value, axis, [(i, i ^ offset) for i in range(size)])


def order_after(value, *others):
    return lax.optimization_barrier((value, others))[0]


def stack_kernel(*refs):
    for k, source in enumerate(refs[:-1]):
        refs[-1][k] = source[...]


def stacked(*arrays):
    shape = (len(arrays),) + arrays[0].shape
    return call(stack_kernel, [(shape, BF16)], [], "stack", vmem(len(arrays)))(*arrays)[0]


TAIL = 64


def cut_of(rows):
    return (rows + TAIL) // 32 * 16


def pack_kernel(*refs):
    sources, (early_ref, late_ref, rates_ref) = refs[:4], refs[4:7]
    held, sems = refs[7:11], refs[11]
    copies = fetch(sources, held, sems)
    cols, rows = held[0].shape
    size, cut = rows + TAIL, cut_of(rows)

    def packed(i):
        copies[i].wait()
        whole = held[i][...].T
        rest = jnp.concatenate(
            [whole[:, 128:cols], jnp.zeros((4 * TAIL - rows, cols - 128), BF16)], axis=0
        )
        rest = [rest[q * TAIL : (q + 1) * TAIL] for q in range(4)]
        return jnp.concatenate([whole[:, 0:128], jnp.concatenate(rest, axis=1)], axis=0)

    early_ref[0:size] = packed(0)
    second = packed(1)
    early_ref[size:] = second[0:cut]
    late_ref[...] = second[cut:]
    rates_ref[0] = packed(2)
    rates_ref[1] = packed(3)


def unpacked(block_of, rows, n_group):
    parts = []
    for g in range(n_group):
        block = block_of(g)
        rest = block[rows:]
        pieces = [rest[:, 32 * q : 32 * q + 32] for q in range(4)]
        parts += [block[0:rows], jnp.concatenate(pieces, axis=0)[0:rows]]
    return jnp.concatenate(parts, axis=1)


def split_kernel(*refs):
    first_ref, second_ref, two_ref = refs[-3:]
    half, size = first_ref.shape[0], first_ref.shape[1]
    for k, source in enumerate(refs[:-3]):
        (first_ref if k < half else second_ref)[k % half] = source[0:size]
        two_ref[k] = source[size:]


def for_group(group_ref, n_group, half_ref, rows, block_of):
    for group in range(n_group):

        @pl.when(group_ref[0] == group)
        def _():
            block_of(
                lambda k, pick: half_ref.__setitem__(
                    k, unpacked(lambda g: pick(g ^ group), rows, n_group)
                )
            )


def two_step_kernel(rows, group_ref, *refs):
    first, first_x, first_y, second, second_y, second_x, half_ref = refs
    half = half_ref.shape[0] // 2

    def fill(store):
        @pl.loop(0, half)
        def _(k):
            pick = (first, first_x, first_y.at[0], first_y.at[1])
            store(k, lambda d: pick[d][k])
            late = (second, second_x.at[0], second_y, second_x.at[1])
            store(half + k, lambda d: late[d][k])

    for_group(group_ref, 4, half_ref, rows, fill)


def direct_kernel(rows, n_group, group_ref, *refs):
    early_refs, late_refs, half_ref = refs[:n_group], refs[n_group:-1], refs[-1]

    def fill(store):
        @pl.loop(0, half_ref.shape[0] // 2)
        def _(i):
            for odd, late_ref in enumerate(late_refs):
                k = 2 * i + odd
                store(k, lambda d: jnp.concatenate([early_refs[d][k], late_ref[i, d]], axis=0))

    for_group(group_ref, n_group, half_ref, rows, fill)


def rate_kernel(rows, n_group, group_ref, *refs):
    packed_refs, outs = refs[:n_group], refs[n_group:]
    for group in range(n_group):

        @pl.when(group_ref[0] == group)
        def _():
            for which, out in enumerate(outs):
                out[...] = unpacked(lambda g: packed_refs[g ^ group][which], rows, n_group)


def along_z(value, n_member):
    chips = n_member // 2
    return [value] + [swap(value, "member", n_member, 2 * k) for k in range(1, chips)]


def across_groups(value, n_group):
    return [value] + [swap(value, "group", n_group, k) for k in range(1, n_group)]


def weights_and_rates(n_group, n_member, conv1, conv2, rate1, rate2, group, me, clip, enter, bias_row):
    rows, cols = conv1.shape
    width = n_group * cols
    if (cols, n_group, n_member, rows % 16) != (160, 4, 8, 0) or rows > 4 * TAIL:
        own = [lax.all_gather(w, "group", axis=1, tiled=True) for w in (conv1, conv2)]
        full = [lax.all_gather(w, "member", axis=0, tiled=True) for w in own]

        def rates(after):
            return [lax.all_gather(w, "group", axis=1, tiled=True) for w in (rate1, rate2)]

        second = lambda after: (full[1], own[1][None])
        return (full[0],), second, own[0][None], rates, enter(clip), bias_row
    size, cut, chips = rows + TAIL, cut_of(rows), n_member // 2
    early_rows, late, both_rates = pl.pallas_call(
        pack_kernel,
        out_shape=(
            jax.ShapeDtypeStruct((size + cut, 128), BF16),
            jax.ShapeDtypeStruct((size - cut, 128), BF16),
            jax.ShapeDtypeStruct((2, size, 128), BF16),
        ),
        in_specs=hbm(4),
        out_specs=tuple(vmem(3)),
        scratch_shapes=[pltpu.VMEM((cols, rows), BF16)] * 4 + [pltpu.SemaphoreType.DMA((4,))],
        cost_estimate=pl.CostEstimate(flops=0, bytes_accessed=1024, transcendentals=0),
        name="pack",
    )(conv1.T, conv2.T, rate1.T, rate2.T)

    def unpack(kernel, *packed):
        (mine,) = call(
            kernel, [((chips, rows, width), BF16)], [], "unpack", smem(1) + vmem(len(packed))
        )(group, *packed)
        return me, mine, swap(mine, "member", n_member, 1)

    along = along_z(early_rows, n_member)
    late_x = swap(late, "group", n_group, 1)
    late_x, bias_row = order_after((late_x, bias_row), ())
    late = stacked(late, late_x)
    late_y = swap(late, "group", n_group, 2)
    act = enter(order_after(clip, (late, bias_row)))
    along, late_y, act = order_after((along, late_y, act), ())
    first, second, along_two = call(
        split_kernel,
        [((chips // 2, size, 128), BF16)] * 2 + [((chips, cut, 128), BF16)], [],
        "split", vmem(chips),
    )(*along)
    first_x = swap(first, "group", n_group, 1)
    second_y = swap(second, "group", n_group, 2)
    late, late_y = order_after((late, late_y), first)
    late = stacked(late, late_y).reshape(n_group, size - cut, 128)
    late_z = swap(late, "member", n_member, 4)
    first_x, second_y = order_after((first_x, second_y), late)
    first_y = swap(stacked(first, first_x), "group", n_group, 2)
    second_x = swap(stacked(second, second_y), "group", n_group, 1)
    late = stacked(late, late_z)
    late_z = swap(late, "member", n_member, 2)
    halves_one = unpack(
        functools.partial(two_step_kernel, rows),
        order_after(first, late), first_x, first_y, second, second_y, second_x,
    )
    along_two = across_groups(order_after(along_two, halves_one[1]), n_group)

    def halves_two(after):
        kernel = functools.partial(direct_kernel, rows, n_group)
        return unpack(kernel, *along_two, *order_after((late, late_z), after))

    def rates(after):
        blocks = across_groups(order_after(both_rates, after), n_group)
        return call(
            functools.partial(rate_kernel, rows, n_group),
            [((rows, width), BF16)] * 2, [], "rates", smem(1) + vmem(n_group),
        )(group, *blocks)

    return halves_one, halves_two, halves_one[1], rates, act, bias_row


def add_kernel(kept_ref, received_ref, *out_refs):
    away_ref, kept_out = out_refs[0], out_refs[1]

    for k in range(away_ref.shape[0]):
        away_ref[k] = (kept_ref[2 * k + 1] + received_ref[2 * k + 1].astype(F32)).astype(BF16)
        kept_out[k] = kept_ref[2 * k] + received_ref[2 * k].astype(F32)


def add_received(kept, received):
    half = (kept.shape[0] // 2,) + kept.shape[1:]
    return call(add_kernel, [(half, BF16), (half, F32)], [], "add", vmem(2))(kept, received)


def halve_to_owner(away, kept, received, n_member, bit=1):
    while True:
        if received is None:
            received = swap(away, "member", n_member, 2 * bit)
        if kept.shape[0] == 1:
            return kept[0], received[0]
        away, kept = add_received(kept, received)
        received = None
        bit *= 2


def pair_kernel(own_ref, home_ref, received_ref, away_ref, middle_ref, kept_ref):
    rows = home_ref.shape[1]

    def total(k):
        return home_ref[k] + received_ref[k * rows : (k + 1) * rows].astype(F32)

    away_ref[0:rows] = total(3).astype(BF16)
    away_ref[rows : 2 * rows] = total(1).astype(BF16)
    middle_ref[...] = total(2)
    kept_ref[...] = total(0)
    last = home_ref.shape[0] * rows
    if away_ref.shape[0] > 2 * rows:
        away_ref[2 * rows : 2 * rows + FACTOR_ROWS] = own_ref[last:]
        away_ref[2 * rows + FACTOR_ROWS :] = received_ref[last:]


def pair_sums(own, home, received):
    chips, rows, channels = home.shape
    shape = (rows, channels)
    extra = 2 * (own.shape[0] - chips * rows)
    return call(
        pair_kernel,
        [((2 * rows + extra, channels), BF16), (shape, F32), (shape, F32)], [],
        "pair", vmem(3), 12,
    )(own, home, received)


def merge_kernel(middle_ref, sent_ref, received_ref, out_ref):
    rows = middle_ref.shape[0]
    known = sent_ref.shape[0] - 2 * rows
    out_ref[0:rows] = (middle_ref[...] + received_ref[0:rows].astype(F32)).astype(BF16)
    if known:
        out_ref[rows : rows + known] = sent_ref[2 * rows :]
        out_ref[rows + known :] = received_ref[2 * rows :]


def merge(middle, sent, received):
    rows, channels = middle.shape
    shape = (rows + 2 * (sent.shape[0] - 2 * rows), channels)
    return call(merge_kernel, [(shape, BF16)], [], "merge", vmem(3))(middle, sent, received)[0]


def update_kernel(own_ref, rate_ref, *refs):
    rows = rate_ref.shape[0]
    total = refs[0][...]
    for ref in refs[1:-1]:
        start = rows if ref.shape[0] == 2 * rows else 0
        total = total + ref[start : start + rows].astype(F32)
    refs[-1][...] = own_ref[0].astype(F32) - rate_ref[...].astype(F32) * total


def common_update_kernel(
    me_ref, own_ref, rate_ref, kept_ref, half_ref, sent_ref, received_ref, out_ref
):
    rows, channels = rate_ref.shape
    total = kept_ref[...] + half_ref[rows : 2 * rows].astype(F32)
    total = total + received_ref[0:rows].astype(F32)
    means, sums = [], []
    for ref in (sent_ref, received_ref):
        for start in range(rows, ref.shape[0], FACTOR_ROWS):
            parts = ref[start : start + FACTOR_ROWS].astype(F32)
            means.append(parts[0:1] + parts[1:2] + parts[2:3])
            sums.append(parts[3:4] + parts[4:5] + parts[5:6])
    means, sums = jnp.concatenate(means, axis=0), jnp.concatenate(sums, axis=0)
    means = jnp.concatenate([means] * 3, axis=1)
    for member in range(len(range(0, 3 * channels, rows))):

        @pl.when(me_ref[0] == member)
        def _():
            common = lax.dot_general(
                means[:, member * rows : (member + 1) * rows],
                sums,
                (((0,), (0,)), ((), ())),
                precision=lax.Precision.HIGHEST,
                preferred_element_type=F32,
            )
            out_ref[...] = own_ref[0].astype(F32) - rate_ref[...].astype(F32) * (total + common)


def common_update(me, own, rate, *terms):
    return call(
        common_update_kernel, [(rate.shape, F32)], [], "update", smem(1) + vmem(6)
    )(me, own, rate, *terms)[0]


def update(own, rate, *terms):
    shape = rate.shape
    return call(
        update_kernel, [(shape, F32)], [], "update", vmem(2 + len(terms)),
    )(own, rate, *terms)[0]


def common_term(every, me, own_rows):
    every = every.astype(F32)
    mean = every[:, 0] + every[:, 1] + every[:, 2]
    sums = every[:, 3] + every[:, 4] + every[:, 5]
    mean = jnp.concatenate([mean] * 3, axis=1)
    mean = lax.dynamic_slice_in_dim(mean, me[0] * own_rows, own_rows, 1)
    return lax.dot_general(
        mean, sums, (((0,), (0,)), ((), ())), precision=lax.Precision.HIGHEST
    )


def shards(
    n_group,
    n_member,
    clips,
    targets,
    timestep,
    identity,
    conv1_weight,
    conv2_weight,
    rate1,
    rate2,
    time_proj,
    subject_table,
):
    frames, points, channels = (clips.shape[1], clips.shape[2], clips.shape[3])
    rows, padded = frames * points, (frames + 2) * points
    scale = 1.0 / math.sqrt(3 * channels)
    group = lax.axis_index("group").astype(jnp.int32)[None]
    me = lax.axis_index("member").astype(jnp.int32)[None]
    own_rows = conv1_weight.shape[0]
    clip, target = clips.reshape(rows, channels), targets.reshape(rows, channels)
    blocks = np.arange(channels) // (channels // GN_GROUPS)
    same_group = jnp.asarray((blocks[:, None] == blocks[None, :]), BF16)

    bias_row = time_bias(timestep[0], identity[0], subject_table, time_proj)

    def enter(clip):
        return call(
            functools.partial(enter_kernel, points),
            [((padded, channels), BF16)],
            [
                pltpu.VMEM((rows, channels), BF16),
                pltpu.VMEM(same_group.shape, BF16),
                pltpu.SemaphoreType.DMA((2,)),
            ],
            "enter", hbm(2), 12,
        )(clip, same_group)[0]

    weight_one, weight_two, own_one, rates, act_one, bias_row = weights_and_rates(
        n_group, n_member, conv1_weight, conv2_weight, rate1, rate2, group, me, clip, enter, bias_row
    )

    def weight_specs(weight):
        return vmem(1) if len(weight) == 1 else smem(1) + vmem(2)

    (hidden,) = call(
        functools.partial(first_kernel, points, scale),
        [((rows, channels), F32)],
        [pltpu.VMEM((3 * channels, channels), BF16)],
        "conv", vmem(2) + weight_specs(weight_one), 20,
    )(act_one, bias_row, *weight_one)
    weight_two = weight_two(hidden)
    own_two = weight_two[1]
    if len(weight_two) == 2:
        weight_two = weight_two[:1]
    normal, inverse, act_two, turned_two = call(
        functools.partial(norm_kernel, points),
        [
            ((rows, channels), F32),
            ((1, channels), F32),
            ((padded, channels), BF16),
            ((channels, rows), BF16),
        ],
        [pltpu.VMEM(same_group.shape, BF16), pltpu.SemaphoreType.DMA((1,))],
        "norm", vmem(1) + hbm(1), 20,
    )(order_after(hidden, weight_two[:2]), same_group)
    error, full_two = call(
        functools.partial(second_kernel, points, scale),
        [((padded, channels), BF16), ((3 * channels, channels), BF16)],
        [pltpu.VMEM((rows, channels), BF16)] * 2 + [pltpu.SemaphoreType.DMA((2,))],
        "conv_error", vmem(1) + hbm(2) + weight_specs(weight_two), 24,
    )(act_two, clip, target, *weight_two)
    away_two, home_two, *factors = gradient(
        turned_two, error, me, n_member, points, scale, True
    )
    received_two = swap(away_two, "member", n_member, 1)
    (grad_act,) = call(
        functools.partial(back_kernel, points, scale),
        [((rows, channels), F32)], [], "back", vmem(2), 20,
    )(order_after(error, away_two), full_two)
    staged = n_member == 8 and not factors
    received_two, grad_act = lax.optimization_barrier((received_two, grad_act))
    if staged:
        half_two, middle_two, kept_two = pair_sums(away_two, home_two, received_two)
        from_two = swap(half_two, "member", n_member, 2)
        grad_act = order_after(grad_act, half_two)
    (grad_hidden,) = call(
        functools.partial(norm_back_kernel, points),
        [((padded, channels), BF16)],
        [
            pltpu.VMEM((rows, channels), F32),
            pltpu.VMEM(same_group.shape, BF16),
            pltpu.SemaphoreType.DMA((1,)),
        ],
        "norm_back", vmem(3) + hbm(1), 20,
    )(grad_act, normal, inverse, same_group)
    away_one, home_one = gradient(
        act_one, grad_hidden, me, n_member, points, scale, False
    )
    if staged:
        merged_two = merge(middle_two, half_two, order_after(from_two, away_one))
        across_two = swap(merged_two, "member", n_member, 4)
        received_one = swap(order_after(away_one, merged_two), "member", n_member, 1)
        half_one, middle_one, kept_one = pair_sums(away_one, home_one, received_one)
        from_one = swap(half_one, "member", n_member, 2)
        rate_one, rate_two = rates(half_one)
        from_one, across_two, rate_one, rate_two = order_after(
            (from_one, across_two, rate_one, rate_two), ()
        )
        merged_one = merge(middle_one, half_one, from_one)
        across_one = swap(merged_one, "member", n_member, 4)
        adapted_two = common_update(
            me, own_two, rate_two, kept_two, from_two, merged_two,
            order_after(across_two, merged_one),
        )
        terms_one = [kept_one, from_one, across_one]
    else:
        received_one = swap(away_one, "member", n_member, 1)
        rate_one, rate_two = rates(away_one)
        every = lax.all_gather(factors[0], "member")
        terms_two = halve_to_owner(*add_received(home_two, received_two), None, n_member)
        terms_one = halve_to_owner(*add_received(home_one, received_one), None, n_member)
        adapted_two = update(own_two, rate_two, *terms_two, common_term(every, me, own_rows))
    adapted_one = update(own_one, rate_one, *terms_one)
    return (adapted_one[None], adapted_two[None])


def solution(mesh):
    n_group, n_member = mesh.shape["group"], mesh.shape["member"]
    return jax.shard_map(
        lambda *arrays: shards(n_group, n_member, *arrays),
        mesh=mesh,
        in_specs=(
            P(("group", "member"), None, None, None),
            P(("group", "member"), None, None, None),
            P(("group", "member")),
            P(("group", "member")),
            P("member", "group"),
            P("member", "group"),
            P("member", "group"),
            P("member", "group"),
            P(),
            P(),
        ),
        out_specs=(P("group", "member", None), P("group", "member", None)),
        check_vma=False,
    )
```

```python
import functools
import math

import jax
import jax.numpy as jnp
import numpy as np
from jax import lax
from jax.experimental import pallas as pl
from jax.experimental.pallas import tpu as pltpu
from jax.sharding import PartitionSpec as P

GN_GROUPS = 32
CHUNK = 128
MEGA = 1024 * 1024
BF16 = jnp.bfloat16
F32 = jnp.float32


def time_bias(step_index, ident, subject_table, time_proj):
    half_width = subject_table.shape[1] // 2
    freqs = jnp.exp(-math.log(10000.0) * jnp.arange(half_width, dtype=F32) / half_width)
    angles = step_index.astype(F32) * freqs
    embedding = jnp.concatenate([jnp.cos(angles), jnp.sin(angles)])
    onehot = (jnp.arange(subject_table.shape[0], dtype=jnp.int32) == ident).astype(F32)
    embedding = embedding + jnp.dot(onehot, subject_table, precision=lax.Precision.HIGHEST)
    activated = jax.nn.silu(embedding).astype(BF16)
    return jnp.dot(activated[None, :], time_proj, preferred_element_type=F32)


def vmem(count):
    return [pl.BlockSpec(memory_space=pltpu.VMEM)] * count


def hbm(count):
    return [pl.BlockSpec(memory_space=pltpu.HBM)] * count


def smem(count):
    return [pl.BlockSpec(memory_space=pltpu.SMEM)] * count


def call(body, out_shape, scratch, name, in_specs, limit=8):
    outs = len(out_shape)
    return pl.pallas_call(
        body,
        out_shape=tuple(jax.ShapeDtypeStruct(s, d) for s, d in out_shape),
        in_specs=in_specs,
        out_specs=tuple(vmem(outs)),
        scratch_shapes=scratch,
        compiler_params=pltpu.CompilerParams(vmem_limit_bytes=limit * MEGA),
        cost_estimate=pl.CostEstimate(flops=0, bytes_accessed=1024, transcendentals=0),
        name=name,
    )


def spread(row, same_group):
    high = row.astype(BF16)
    rest = row - high.astype(F32)
    middle = rest.astype(BF16)
    low = (rest - middle.astype(F32)).astype(BF16)
    stacked = jnp.concatenate(
        [jnp.broadcast_to(part, (16, row.shape[1])) for part in (high, middle, low)], axis=0
    )
    sums = jnp.dot(stacked, same_group, preferred_element_type=F32)
    return sums[0:1] + sums[16:17] + sums[32:33]


def norm_stats(read, rows, channels, same_ref, copy=None):
    counted = rows * (channels // GN_GROUPS)
    steps = rows // CHUNK
    total = lax.fori_loop(
        0,
        steps,
        lambda i, acc: acc + read(i).reshape(CHUNK // 8, 8, channels).sum(axis=0),
        jnp.zeros((8, channels), F32),
    ).sum(axis=0, keepdims=True)
    if copy is not None:
        copy.wait()
    same_group = same_ref[...]
    centre = spread(total, same_group) * (1.0 / counted)

    def squares(i, acc):
        centred = read(i) - centre
        return acc + (centred * centred).reshape(CHUNK // 8, 8, channels).sum(axis=0)

    square = lax.fori_loop(0, steps, squares, jnp.zeros((8, channels), F32)).sum(
        axis=0, keepdims=True
    )
    variance = spread(square, same_group) * (1.0 / counted)
    return centre, lax.rsqrt(variance + 1e-05)


def at(i, shift=0):
    return pl.ds(pl.multiple_of(i * CHUNK + shift, 64), CHUNK)


def clear_edges(padded_ref, points):
    edge = jnp.zeros((points, padded_ref.shape[1]), padded_ref.dtype)
    padded_ref[0:points] = edge
    padded_ref[padded_ref.shape[0] - points :] = edge


def fetch(sources, held, sems):
    copies = [
        pltpu.make_async_copy(source, place, sems.at[i])
        for i, (source, place) in enumerate(zip(sources, held))
    ]
    for copy in copies:
        copy.start()
    return copies


def enter_kernel(points, clip_hbm, same_hbm, padded_ref, clip_ref, same_ref, sems):
    rows, channels = clip_ref.shape
    for copy in fetch((clip_hbm, same_hbm), (clip_ref, same_ref), sems):
        copy.wait()
    centre, inverse = norm_stats(
        lambda i: clip_ref[at(i)].astype(F32), rows, channels, same_ref
    )
    clear_edges(padded_ref, points)

    @pl.loop(0, rows // CHUNK)
    def _(i):
        normal = (clip_ref[at(i)].astype(F32) - centre) * inverse
        padded_ref[at(i, points)] = (normal / (1.0 + jnp.exp(-normal))).astype(BF16)


def taps_of(padded_ref, start, size, points):
    return jnp.concatenate(
        [padded_ref[pl.ds(start + t * points, size)] for t in range(3)], axis=1
    )


def full_weight(weight_refs, full_ref):
    if len(weight_refs) == 1:
        return weight_refs[0]
    member_ref, mine_ref, other_ref = weight_refs
    member, rows = member_ref[0], mine_ref.shape[1]

    @pl.loop(0, mine_ref.shape[0])
    def _(k):
        for half, source in ((0, mine_ref), (1, other_ref)):
            start = pl.multiple_of((member ^ (2 * k + half)) * rows, 16)
            full_ref[pl.ds(start, rows)] = source[k]

    return full_ref


def first_kernel(points, scale, in_ref, bias_ref, *refs):
    weight_refs = refs[:-2]
    hidden_ref, full_ref = refs[-2:]
    half = hidden_ref.shape[0] // 2
    bias = bias_ref[...]
    weight_ref = full_weight(weight_refs, full_ref)

    @pl.loop(0, 2)
    def _(i):
        start = pl.multiple_of(i * half, 64)
        mixed = jnp.dot(
            taps_of(in_ref, start, half, points), weight_ref[...], preferred_element_type=F32
        )
        hidden_ref[pl.ds(start, half)] = scale * mixed + bias


def norm_kernel(
    points, hidden_ref, same_hbm, normal_ref, inverse_ref, padded_ref, turned_ref, same_ref, sems
):
    rows, channels = normal_ref.shape
    (copy,) = fetch((same_hbm,), (same_ref,), sems)
    centre, inverse = norm_stats(lambda i: hidden_ref[at(i)], rows, channels, same_ref, copy)
    inverse_ref[...] = inverse
    clear_edges(padded_ref, points)

    @pl.loop(0, rows // CHUNK)
    def _(i):
        normal = (hidden_ref[at(i)] - centre) * inverse
        normal_ref[at(i)] = normal
        act = (normal / (1.0 + jnp.exp(-normal))).astype(BF16)
        padded_ref[at(i, points)] = act
        turned_ref[:, at(i)] = act.T


def second_kernel(points, scale, in_ref, clip_hbm, target_hbm, *refs):
    weight_refs = refs[:-5]
    error_ref, full_ref, clip_ref, target_ref, sems = refs[-5:]
    copies = fetch((clip_hbm, target_hbm), (clip_ref, target_ref), sems)
    rows = clip_ref.shape[0]
    half = rows // 2
    clear_edges(error_ref, points)
    weight_ref = full_weight(weight_refs, full_ref)
    if len(weight_refs) == 1:
        full_ref[...] = weight_ref[...]
    for copy in copies:
        copy.wait()

    @pl.loop(0, 2)
    def _(i):
        start = pl.multiple_of(i * half, 64)
        mixed = jnp.dot(
            taps_of(in_ref, start, half, points), weight_ref[...], preferred_element_type=F32
        )
        here = pl.ds(start, half)
        output = clip_ref[here].astype(F32) + scale * mixed
        error_ref[pl.ds(pl.multiple_of(start + points, 64), half)] = (
            output - target_ref[here].astype(F32)
        ).astype(BF16)


def back_kernel(points, scale, error_ref, weight_ref, grad_ref):
    rows, channels = grad_ref.shape
    half = rows // 2
    last = (((1,), (1,)), ((), ()))

    @pl.loop(0, 2)
    def _(i):
        start = pl.multiple_of(i * half, 64)
        total = None
        for t in range(3):
            part = lax.dot_general(
                error_ref[pl.ds(pl.multiple_of(start + (2 - t) * points, 64), half)],
                weight_ref[t * channels : (t + 1) * channels],
                last,
                preferred_element_type=F32,
            )
            total = part if total is None else total + part
        grad_ref[pl.ds(start, half)] = scale * total


def norm_back_kernel(
    points, act_grad_ref, normal_ref, inverse_ref, same_hbm, out_ref, grad_ref, same_ref, sems
):
    (copy,) = fetch((same_hbm,), (same_ref,), sems)
    rows, channels = normal_ref.shape
    counted = rows * (channels // GN_GROUPS)

    def through(i, sums):
        normal = normal_ref[at(i)]
        gate = 1.0 / (1.0 + jnp.exp(-normal))
        grad = act_grad_ref[at(i)] * (gate * (1.0 + normal * (1.0 - gate)))
        grad_ref[at(i)] = grad

        def fold(value):
            return value.reshape(CHUNK // 8, 8, channels).sum(axis=0)

        return sums[0] + fold(grad), sums[1] + fold(grad * normal)

    zero = jnp.zeros((8, channels), F32)
    plain, crossed = lax.fori_loop(0, rows // CHUNK, through, (zero, zero))
    copy.wait()
    same_group = same_ref[...]
    mean = spread(plain.sum(axis=0, keepdims=True), same_group) * (1.0 / counted)
    slope = spread(crossed.sum(axis=0, keepdims=True), same_group) * (1.0 / counted)
    inverse = inverse_ref[...]
    clear_edges(out_ref, points)

    @pl.loop(0, rows // CHUNK)
    def _(i):
        value = (grad_ref[at(i)] - mean - normal_ref[at(i)] * slope) * inverse
        out_ref[at(i, points)] = value.astype(BF16)


FACTOR_ROWS = 16


def split_rows(row):
    high = row.astype(BF16).astype(F32)
    middle = (row - high).astype(BF16).astype(F32)
    return [high, middle, row - high - middle]


def grad_kernel(points, scale, block, centred, me_ref, act_ref, cotangent_ref, *refs):
    refs = list(refs)
    turned_ref = refs.pop()
    total_ref = refs.pop()
    if act_ref.shape == turned_ref.shape:
        turned_ref = act_ref
    channels, rows = turned_ref.shape
    if turned_ref is not act_ref:

        @pl.loop(0, rows // CHUNK)
        def _(i):
            turned_ref[:, at(i)] = act_ref[at(i, points)].T

    if centred:
        ones = jnp.ones((rows, 128), BF16)
        mean = jnp.dot(turned_ref[...], ones, preferred_element_type=F32) * (1.0 / rows)
        sums = scale * jnp.dot(
            jnp.ones((16, rows), BF16),
            cotangent_ref[pl.ds(points, rows)],
            preferred_element_type=F32,
        )
        factors = split_rows(mean.T[0:1]) + split_rows(sums[0:1])
        factors += [jnp.zeros((FACTOR_ROWS - len(factors), channels), F32)]
        factors = jnp.concatenate(factors, axis=0)
        common = jnp.concatenate([mean] * (channels // 128), axis=1) * sums[0:1]

    @pl.loop(0, 3)
    def _(t):
        shifted = cotangent_ref[pl.ds(pl.multiple_of((2 - t) * points, 64), rows)]
        product = scale * jnp.dot(turned_ref[...], shifted, preferred_element_type=F32)
        if centred:
            product = product - common
        total_ref[pl.ds(pl.multiple_of(t * channels, 128), channels)] = product

    if block is not None:
        home_ref, away_refs = refs[0], refs[1:]
        me = me_ref[0]
        count = home_ref.shape[0]

        for j in range(count):
            away = pl.multiple_of((me ^ (2 * j + 1)) * block, 16)
            home = pl.multiple_of((me ^ (2 * j)) * block, 16)
            part = total_ref[pl.ds(away, block)].astype(BF16)
            if centred:
                away_refs[0][j * block : (j + 1) * block] = part
            else:
                away_refs[j][...] = part
            home_ref[j] = total_ref[pl.ds(home, block)]

        if centred:
            away_refs[0][count * block :] = factors.astype(BF16)
    elif centred:
        refs[0][...] = factors


def gradient(act, cotangent, me, n_member, points, scale, centred):
    channels, rows = cotangent.shape[1], cotangent.shape[0] - 2 * points
    turned = pltpu.VMEM((channels, rows), BF16)
    block = 3 * channels // n_member
    specs = smem(1) + vmem(2)
    if block % 16 == 0:
        chips = n_member // 2
        away = [((block, channels), BF16)] * chips
        if centred:
            away = [((chips * block + FACTOR_ROWS, channels), BF16)]
        home, *away = call(
            functools.partial(grad_kernel, points, scale, block, centred),
            [((chips, block, channels), F32)] + away,
            [pltpu.VMEM((3 * channels, channels), F32), turned],
            "gradient", specs, 24,
        )(me, act, cotangent)
        return away, home, None
    factors = [((FACTOR_ROWS, channels), F32)] if centred else []
    found = call(
        functools.partial(grad_kernel, points, scale, None, centred),
        factors + [((3 * channels, channels), F32)],
        [turned], "gradient", specs, 24,
    )(me, act, cotangent)
    total = found[-1].reshape(n_member, block, channels)
    order = [lax.dynamic_index_in_dim(total, me[0] ^ j, 0, keepdims=False) for j in range(n_member)]
    away, home = jnp.stack(order[1::2]).astype(BF16), jnp.stack(order[0::2])
    return [away], home, found[0] if centred else None


def swap(value, axis, size, offset):
    return lax.ppermute(value, axis, [(i, i ^ offset) for i in range(size)])


def order_after(value, *others):
    return lax.optimization_barrier((value, others))[0]


def stack_kernel(*refs):
    for k, source in enumerate(refs[:-1]):
        refs[-1][k] = source[...]


def stacked(*arrays):
    shape = (len(arrays),) + arrays[0].shape
    return call(stack_kernel, [(shape, BF16)], [], "stack", vmem(len(arrays)))(*arrays)[0]


TAIL = 64


def cut_of(rows):
    return (rows + TAIL) // 32 * 16


def pack_kernel(*refs):
    refs = refs[:4] + refs[6:]
    sources, (early_ref, late_ref, rates_ref) = refs[:4], refs[4:7]
    held, sems = refs[7:11], refs[11]
    copies = fetch(sources, held, sems)
    cols, rows = held[0].shape
    size, cut = rows + TAIL, cut_of(rows)

    def packed(i):
        copies[i].wait()
        whole = held[i][...].T
        rest = jnp.concatenate(
            [whole[:, 128:cols], jnp.zeros((4 * TAIL - rows, cols - 128), BF16)], axis=0
        )
        rest = [rest[q * TAIL : (q + 1) * TAIL] for q in range(4)]
        return jnp.concatenate([whole[:, 0:128], jnp.concatenate(rest, axis=1)], axis=0)

    early_ref[0:size] = packed(0)
    second = packed(1)
    early_ref[size:] = second[0:cut]
    late_ref[...] = second[cut:]
    rates_ref[0] = packed(2)
    rates_ref[1] = packed(3)


def unpacked(block_of, rows, n_group):
    parts = []
    for g in range(n_group):
        block = block_of(g)
        rest = block[rows:]
        pieces = [rest[:, 32 * q : 32 * q + 32] for q in range(4)]
        parts += [block[0:rows], jnp.concatenate(pieces, axis=0)[0:rows]]
    return jnp.concatenate(parts, axis=1)


def split_kernel(*refs):
    first_ref, second_ref, two_ref = refs[-3:]
    half, size = first_ref.shape[0], first_ref.shape[1]
    for k, source in enumerate(refs[:-3]):
        (first_ref if k < half else second_ref)[k % half] = source[0:size]
        two_ref[k] = source[size:]


def for_group(group_ref, n_group, half_ref, rows, block_of):
    for group in range(n_group):

        @pl.when(group_ref[0] == group)
        def _():
            block_of(
                lambda k, pick: half_ref.__setitem__(
                    k, unpacked(lambda g: pick(g ^ group), rows, n_group)
                )
            )


def two_step_kernel(rows, group_ref, *refs):
    first, first_x, first_y, second, second_y, second_x, half_ref = refs
    half = half_ref.shape[0] // 2

    def fill(store):
        @pl.loop(0, half)
        def _(k):
            pick = (first, first_x, first_y.at[0], first_y.at[1])
            store(k, lambda d: pick[d][k])
            late = (second, second_x.at[0], second_y, second_x.at[1])
            store(half + k, lambda d: late[d][k])

    for_group(group_ref, 4, half_ref, rows, fill)


def direct_kernel(rows, n_group, group_ref, *refs):
    early_refs, late_refs, half_ref = refs[:n_group], refs[n_group:-1], refs[-1]

    def fill(store):
        @pl.loop(0, half_ref.shape[0] // 2)
        def _(i):
            for odd, late_ref in enumerate(late_refs):
                k = 2 * i + odd
                store(k, lambda d: jnp.concatenate([early_refs[d][k], late_ref[i, d]], axis=0))

    for_group(group_ref, n_group, half_ref, rows, fill)


def rate_kernel(rows, n_group, group_ref, *refs):
    packed_refs, outs = refs[:n_group], refs[n_group:]
    for group in range(n_group):

        @pl.when(group_ref[0] == group)
        def _():
            for which, out in enumerate(outs):
                out[...] = unpacked(lambda g: packed_refs[g ^ group][which], rows, n_group)


def along_z(value, n_member):
    chips = n_member // 2
    return [value] + [swap(value, "member", n_member, 2 * k) for k in range(1, chips)]


def across_groups(value, n_group):
    return [value] + [swap(value, "group", n_group, k) for k in range(1, n_group)]


def weights_and_rates(n_group, n_member, conv1, conv2, rate1, rate2, group, me, clip, enter, bias_row):
    rows, cols = conv1.shape
    width = n_group * cols
    if (cols, n_group, n_member, rows % 16) != (160, 4, 8, 0) or rows > 4 * TAIL:
        own = [lax.all_gather(w, "group", axis=1, tiled=True) for w in (conv1, conv2)]
        full = [lax.all_gather(w, "member", axis=0, tiled=True) for w in own]

        def rates(after):
            return [lax.all_gather(w, "group", axis=1, tiled=True) for w in (rate1, rate2)]

        second = lambda after: (full[1], own[1][None])
        return (full[0],), second, own[0][None], rates, enter(clip), bias_row
    size, cut, chips = rows + TAIL, cut_of(rows), n_member // 2
    early_rows, late, both_rates = pl.pallas_call(
        pack_kernel,
        out_shape=(
            jax.ShapeDtypeStruct((size + cut, 128), BF16),
            jax.ShapeDtypeStruct((size - cut, 128), BF16),
            jax.ShapeDtypeStruct((2, size, 128), BF16),
        ),
        in_specs=hbm(4) + smem(2),
        out_specs=tuple(vmem(3)),
        scratch_shapes=[pltpu.VMEM((cols, rows), BF16)] * 4 + [pltpu.SemaphoreType.DMA((4,))],
        cost_estimate=pl.CostEstimate(flops=0, bytes_accessed=1024, transcendentals=0),
        name="pack",
    )(conv1.T, conv2.T, rate1.T, rate2.T, group, me)

    def unpack(kernel, *packed):
        (mine,) = call(
            kernel, [((chips, rows, width), BF16)], [], "unpack", smem(1) + vmem(len(packed))
        )(group, *packed)
        return me, mine, swap(mine, "member", n_member, 1)

    along = along_z(early_rows, n_member)
    late_x = swap(late, "group", n_group, 1)
    late_x, bias_row = order_after((late_x, bias_row), ())
    late = stacked(late, late_x)
    late_y = swap(late, "group", n_group, 2)
    act = enter(order_after(clip, (late, bias_row)))
    along, late_y, act = order_after((along, late_y, act), ())
    first, second, along_two = call(
        split_kernel,
        [((chips // 2, size, 128), BF16)] * 2 + [((chips, cut, 128), BF16)], [],
        "split", vmem(chips),
    )(*along)
    first_x = swap(first, "group", n_group, 1)
    second_y = swap(second, "group", n_group, 2)
    late, late_y = order_after((late, late_y), first)
    late = stacked(late, late_y).reshape(n_group, size - cut, 128)
    late_z = swap(late, "member", n_member, 4)
    first_y = swap(stacked(first, first_x), "group", n_group, 2)
    second_x = swap(stacked(second, second_y), "group", n_group, 1)
    late = stacked(late, late_z)
    late_z = swap(late, "member", n_member, 2)
    halves_one = unpack(
        functools.partial(two_step_kernel, rows),
        order_after(first, late), first_x, first_y, second, second_y, second_x,
    )
    along_two = across_groups(order_after(along_two, halves_one[1]), n_group)

    def halves_two(after):
        kernel = functools.partial(direct_kernel, rows, n_group)
        return unpack(kernel, *along_two, *order_after((late, late_z), after))

    def rates(after):
        blocks = across_groups(order_after(both_rates, after), n_group)
        return call(
            functools.partial(rate_kernel, rows, n_group),
            [((rows, width), BF16)] * 2, [], "rates", smem(1) + vmem(n_group),
        )(group, *blocks)

    return halves_one, halves_two, halves_one[1], rates, act, bias_row


def add_kernel(kept_ref, received_ref, *out_refs):
    away_ref, kept_out = out_refs[0], out_refs[1]

    for k in range(away_ref.shape[0]):
        away_ref[k] = (kept_ref[2 * k + 1] + received_ref[2 * k + 1].astype(F32)).astype(BF16)
        kept_out[k] = kept_ref[2 * k] + received_ref[2 * k].astype(F32)


def add_received(kept, received):
    half = (kept.shape[0] // 2,) + kept.shape[1:]
    return call(add_kernel, [(half, BF16), (half, F32)], [], "add", vmem(2))(kept, received)


def halve_to_owner(away, kept, received, n_member, bit=1):
    while True:
        if received is None:
            received = swap(away, "member", n_member, 2 * bit)
        if kept.shape[0] == 1:
            return kept[0], received[0]
        away, kept = add_received(kept, received)
        received = None
        bit *= 2


def pair_kernel(own_ref, home_ref, received_ref, away_ref, middle_ref, kept_ref):
    rows = home_ref.shape[1]

    def total(k):
        return home_ref[k] + received_ref[k * rows : (k + 1) * rows].astype(F32)

    away_ref[0:rows] = total(3).astype(BF16)
    away_ref[rows : 2 * rows] = total(1).astype(BF16)
    middle_ref[...] = total(2)
    kept_ref[...] = total(0)
    last = home_ref.shape[0] * rows
    if away_ref.shape[0] > 2 * rows:
        away_ref[2 * rows : 2 * rows + FACTOR_ROWS] = own_ref[last:]
        away_ref[2 * rows + FACTOR_ROWS :] = received_ref[last:]


def pair_sums(own, home, received):
    chips, rows, channels = home.shape
    shape = (rows, channels)
    extra = 2 * (own.shape[0] - chips * rows)
    return call(
        pair_kernel,
        [((2 * rows + extra, channels), BF16), (shape, F32), (shape, F32)], [],
        "pair", vmem(3), 12,
    )(own, home, received)


def parts_kernel(home_ref, *refs):
    received_refs, outs = refs[:4], refs[4:]
    for k, out in zip((3, 1, 2, 0), outs):
        out[...] = (home_ref[k] + received_refs[k][...].astype(F32)).astype(out.dtype)


def pair_parts(home, received):
    shape = home.shape[1:]
    return call(
        parts_kernel, [(shape, BF16), (shape, BF16), (shape, F32), (shape, F32)], [],
        "pair", vmem(5), 12,
    )(home, *received)


def merge_kernel(middle_ref, *refs):
    *sent_refs, received_ref, out_ref = refs
    rows = middle_ref.shape[0]
    out_ref[0:rows] = (middle_ref[...] + received_ref[0:rows].astype(F32)).astype(BF16)
    for sent_ref in sent_refs:
        known = sent_ref.shape[0] - 2 * rows
        out_ref[rows : rows + known] = sent_ref[2 * rows :]
        out_ref[rows + known :] = received_ref[2 * rows :]


def merge(middle, received, *sent):
    rows, channels = middle.shape
    known = [part.shape[0] - 2 * rows for part in sent]
    shape = (rows + 2 * sum(known), channels)
    operands = (middle,) + sent + (received,)
    return call(merge_kernel, [(shape, BF16)], [], "merge", vmem(len(operands)))(*operands)[0]


def update_kernel(own_ref, rate_ref, *refs):
    total = refs[0][...]
    for ref in refs[1:-1]:
        total = total + ref[...].astype(F32)
    refs[-1][...] = own_ref[0].astype(F32) - rate_ref[...].astype(F32) * total


def both_kernel(
    me_ref, own_ref, rate_ref, kept_ref, half_ref, sent_ref, received_ref, *refs
):
    *first_refs, first_out, out_ref = refs
    update_kernel(*first_refs, first_out)
    rows, channels = rate_ref.shape
    total = kept_ref[...] + half_ref[rows : 2 * rows].astype(F32)
    total = total + received_ref[0:rows].astype(F32)
    means, sums = [], []
    for ref in (sent_ref, received_ref):
        for start in range(rows, ref.shape[0], FACTOR_ROWS):
            parts = ref[start : start + FACTOR_ROWS].astype(F32)
            means.append(parts[0:1] + parts[1:2] + parts[2:3])
            sums.append(parts[3:4] + parts[4:5] + parts[5:6])
    means, sums = jnp.concatenate(means, axis=0), jnp.concatenate(sums, axis=0)
    means = jnp.concatenate([means] * 3, axis=1)
    for member in range(3 * channels // rows):

        @pl.when(me_ref[0] == member)
        def _():
            common = lax.dot_general(
                means[:, member * rows : (member + 1) * rows],
                sums,
                (((0,), (0,)), ((), ())),
                precision=lax.Precision.HIGHEST,
                preferred_element_type=F32,
            )
            out_ref[...] = own_ref[0].astype(F32) - rate_ref[...].astype(F32) * (total + common)


def update_both(me, second_terms, first_terms):
    terms = second_terms + first_terms
    shape = (second_terms[1].shape, F32)
    return call(
        both_kernel, [shape, shape], [], "update", smem(1) + vmem(len(terms)), 16
    )(me, *terms)


def update(own, rate, *terms):
    shape = rate.shape
    return call(
        update_kernel, [(shape, F32)], [], "update", vmem(2 + len(terms)),
    )(own, rate, *terms)[0]


def common_term(every, me, own_rows):
    every = every.astype(F32)
    mean = every[:, 0] + every[:, 1] + every[:, 2]
    sums = every[:, 3] + every[:, 4] + every[:, 5]
    mean = jnp.concatenate([mean] * 3, axis=1)
    mean = lax.dynamic_slice_in_dim(mean, me[0] * own_rows, own_rows, 1)
    return lax.dot_general(
        mean, sums, (((0,), (0,)), ((), ())), precision=lax.Precision.HIGHEST
    )


def shards(
    n_group,
    n_member,
    clips,
    targets,
    timestep,
    identity,
    conv1_weight,
    conv2_weight,
    rate1,
    rate2,
    time_proj,
    subject_table,
):
    frames, points, channels = (clips.shape[1], clips.shape[2], clips.shape[3])
    rows, padded = frames * points, (frames + 2) * points
    scale = 1.0 / math.sqrt(3 * channels)
    group = lax.axis_index("group").astype(jnp.int32)[None]
    me = lax.axis_index("member").astype(jnp.int32)[None]
    own_rows = conv1_weight.shape[0]
    clip, target = clips.reshape(rows, channels), targets.reshape(rows, channels)
    blocks = np.arange(channels) // (channels // GN_GROUPS)
    same_group = jnp.asarray((blocks[:, None] == blocks[None, :]), BF16)

    bias_row = time_bias(timestep[0], identity[0], subject_table, time_proj)

    def enter(clip):
        return call(
            functools.partial(enter_kernel, points),
            [((padded, channels), BF16)],
            [
                pltpu.VMEM((rows, channels), BF16),
                pltpu.VMEM(same_group.shape, BF16),
                pltpu.SemaphoreType.DMA((2,)),
            ],
            "enter", hbm(2), 12,
        )(clip, same_group)[0]

    weight_one, weight_two, own_one, rates, act_one, bias_row = weights_and_rates(
        n_group, n_member, conv1_weight, conv2_weight, rate1, rate2, group, me, clip, enter, bias_row
    )

    def weight_specs(weight):
        return vmem(1) if len(weight) == 1 else smem(1) + vmem(2)

    (hidden,) = call(
        functools.partial(first_kernel, points, scale),
        [((rows, channels), F32)],
        [pltpu.VMEM((3 * channels, channels), BF16)],
        "conv", vmem(2) + weight_specs(weight_one), 20,
    )(act_one, bias_row, *weight_one)
    weight_two = weight_two(hidden)
    own_two = weight_two[1]
    if len(weight_two) == 2:
        weight_two = weight_two[:1]
    normal, inverse, act_two, turned_two = call(
        functools.partial(norm_kernel, points),
        [
            ((rows, channels), F32),
            ((1, channels), F32),
            ((padded, channels), BF16),
            ((channels, rows), BF16),
        ],
        [pltpu.VMEM(same_group.shape, BF16), pltpu.SemaphoreType.DMA((1,))],
        "norm", vmem(1) + hbm(1), 20,
    )(order_after(hidden, weight_two[:2]), same_group)
    error, full_two = call(
        functools.partial(second_kernel, points, scale),
        [((padded, channels), BF16), ((3 * channels, channels), BF16)],
        [pltpu.VMEM((rows, channels), BF16)] * 2 + [pltpu.SemaphoreType.DMA((2,))],
        "conv_error", vmem(1) + hbm(2) + weight_specs(weight_two), 24,
    )(act_two, clip, target, *weight_two)
    (away_two,), home_two, factors = gradient(
        turned_two, error, me, n_member, points, scale, True
    )
    received_two = swap(away_two, "member", n_member, 1)
    (grad_act,) = call(
        functools.partial(back_kernel, points, scale),
        [((rows, channels), F32)], [], "back", vmem(2), 20,
    )(order_after(error, away_two), full_two)
    staged = n_member == 8 and factors is None
    received_two, grad_act = lax.optimization_barrier((received_two, grad_act))
    if staged:
        half_two, middle_two, kept_two = pair_sums(away_two, home_two, received_two)
        from_two = swap(half_two, "member", n_member, 2)
        grad_act = order_after(grad_act, half_two)
    (grad_hidden,) = call(
        functools.partial(norm_back_kernel, points),
        [((padded, channels), BF16)],
        [
            pltpu.VMEM((rows, channels), F32),
            pltpu.VMEM(same_group.shape, BF16),
            pltpu.SemaphoreType.DMA((1,)),
        ],
        "norm_back", vmem(3) + hbm(1), 20,
    )(grad_act, normal, inverse, same_group)
    away_one, home_one, _ = gradient(
        act_one, grad_hidden, me, n_member, points, scale, False
    )
    received_one = [swap(part, "member", n_member, 1) for part in away_one]
    if staged:
        far_one, near_one, middle_one, kept_one = pair_parts(home_one, received_one)
        from_one = swap(far_one, "member", n_member, 2)
        beside_one = swap(near_one, "member", n_member, 2)
        merged_two = merge(middle_two, from_two, half_two)
        across_two = swap(merged_two, "member", n_member, 4)
        rate_one, rate_two = rates(far_one)
        middle_one = order_after(middle_one, (rate_one, rate_two))
        across_one = swap(merge(middle_one, from_one), "member", n_member, 4)
        adapted_one, adapted_two = update_both(
            me,
            (own_two, rate_two, kept_two, from_two, merged_two, across_two),
            (own_one, rate_one, kept_one, beside_one, across_one),
        )
    else:
        rate_one, rate_two = rates(away_one)
        every = lax.all_gather(factors, "member")
        terms_two = halve_to_owner(*add_received(home_two, received_two), None, n_member)
        terms_one = halve_to_owner(*add_received(home_one, received_one[0]), None, n_member)
        adapted_two = update(own_two, rate_two, *terms_two, common_term(every, me, own_rows))
        adapted_one = update(own_one, rate_one, *terms_one)
    return (adapted_one[None], adapted_two[None])


def solution(mesh):
    n_group, n_member = mesh.shape["group"], mesh.shape["member"]
    return jax.shard_map(
        lambda *arrays: shards(n_group, n_member, *arrays),
        mesh=mesh,
        in_specs=(
            P(("group", "member"), None, None, None),
            P(("group", "member"), None, None, None),
            P(("group", "member")),
            P(("group", "member")),
            P("member", "group"),
            P("member", "group"),
            P("member", "group"),
            P("member", "group"),
            P(),
            P(),
        ),
        out_specs=(P("group", "member", None), P("group", "member", None)),
        check_vma=False,
    )
```

```python
import functools
import math

import jax
import jax.numpy as jnp
import numpy as np
from jax import lax
from jax.experimental import pallas as pl
from jax.experimental.pallas import tpu as pltpu
from jax.sharding import PartitionSpec as P

GN_GROUPS = 32
CHUNK = 128
MEGA = 1024 * 1024
BF16 = jnp.bfloat16
F32 = jnp.float32


def time_bias(step_index, ident, subject_table, time_proj):
    half_width = subject_table.shape[1] // 2
    freqs = jnp.exp(-math.log(10000.0) * jnp.arange(half_width, dtype=F32) / half_width)
    angles = step_index.astype(F32) * freqs
    embedding = jnp.concatenate([jnp.cos(angles), jnp.sin(angles)])
    onehot = (jnp.arange(subject_table.shape[0], dtype=jnp.int32) == ident).astype(F32)
    embedding = embedding + jnp.dot(onehot, subject_table, precision=lax.Precision.HIGHEST)
    activated = jax.nn.silu(embedding).astype(BF16)
    return jnp.dot(activated[None, :], time_proj, preferred_element_type=F32)


def vmem(count):
    return [pl.BlockSpec(memory_space=pltpu.VMEM)] * count


def hbm(count):
    return [pl.BlockSpec(memory_space=pltpu.HBM)] * count


def smem(count):
    return [pl.BlockSpec(memory_space=pltpu.SMEM)] * count


def call(body, out_shape, scratch, name, in_specs, limit=8):
    outs = len(out_shape)
    return pl.pallas_call(
        body,
        out_shape=tuple(jax.ShapeDtypeStruct(s, d) for s, d in out_shape),
        in_specs=in_specs,
        out_specs=tuple(vmem(outs)),
        scratch_shapes=scratch,
        compiler_params=pltpu.CompilerParams(vmem_limit_bytes=limit * MEGA),
        cost_estimate=pl.CostEstimate(flops=0, bytes_accessed=1024, transcendentals=0),
        name=name,
    )


def spread(row, same_group):
    high = row.astype(BF16)
    rest = row - high.astype(F32)
    middle = rest.astype(BF16)
    low = (rest - middle.astype(F32)).astype(BF16)
    stacked = jnp.concatenate(
        [jnp.broadcast_to(part, (16, row.shape[1])) for part in (high, middle, low)], axis=0
    )
    sums = jnp.dot(stacked, same_group, preferred_element_type=F32)
    return sums[0:1] + sums[16:17] + sums[32:33]


def norm_stats(read, rows, channels, same_ref, copy=None):
    counted = rows * (channels // GN_GROUPS)
    steps = rows // CHUNK
    total = lax.fori_loop(
        0,
        steps,
        lambda i, acc: acc + read(i).reshape(CHUNK // 8, 8, channels).sum(axis=0),
        jnp.zeros((8, channels), F32),
    ).sum(axis=0, keepdims=True)
    if copy is not None:
        copy.wait()
    same_group = same_ref[...]
    centre = spread(total, same_group) * (1.0 / counted)

    def squares(i, acc):
        centred = read(i) - centre
        return acc + (centred * centred).reshape(CHUNK // 8, 8, channels).sum(axis=0)

    square = lax.fori_loop(0, steps, squares, jnp.zeros((8, channels), F32)).sum(
        axis=0, keepdims=True
    )
    variance = spread(square, same_group) * (1.0 / counted)
    return centre, lax.rsqrt(variance + 1e-05)


def at(i, shift=0):
    return pl.ds(pl.multiple_of(i * CHUNK + shift, 64), CHUNK)


def clear_edges(padded_ref, points):
    edge = jnp.zeros((points, padded_ref.shape[1]), padded_ref.dtype)
    padded_ref[0:points] = edge
    padded_ref[padded_ref.shape[0] - points :] = edge


def fetch(sources, held, sems):
    copies = [
        pltpu.make_async_copy(source, place, sems.at[i])
        for i, (source, place) in enumerate(zip(sources, held))
    ]
    for copy in copies:
        copy.start()
    return copies


def enter_kernel(points, clip_hbm, same_hbm, padded_ref, clip_ref, same_ref, sems):
    rows, channels = clip_ref.shape
    for copy in fetch((clip_hbm, same_hbm), (clip_ref, same_ref), sems):
        copy.wait()
    centre, inverse = norm_stats(
        lambda i: clip_ref[at(i)].astype(F32), rows, channels, same_ref
    )
    clear_edges(padded_ref, points)

    @pl.loop(0, rows // CHUNK)
    def _(i):
        normal = (clip_ref[at(i)].astype(F32) - centre) * inverse
        padded_ref[at(i, points)] = (normal / (1.0 + jnp.exp(-normal))).astype(BF16)


def taps_of(padded_ref, start, size, points):
    return jnp.concatenate(
        [padded_ref[pl.ds(start + t * points, size)] for t in range(3)], axis=1
    )


def full_weight(weight_refs, full_ref):
    if len(weight_refs) == 1:
        return weight_refs[0]
    member_ref, mine_ref, other_ref = weight_refs
    member, rows = member_ref[0], mine_ref.shape[1]

    @pl.loop(0, mine_ref.shape[0])
    def _(k):
        for half, source in ((0, mine_ref), (1, other_ref)):
            start = pl.multiple_of((member ^ (2 * k + half)) * rows, 16)
            full_ref[pl.ds(start, rows)] = source[k]

    return full_ref


def first_kernel(points, scale, in_ref, bias_ref, *refs):
    weight_refs = refs[:-2]
    hidden_ref, full_ref = refs[-2:]
    half = hidden_ref.shape[0] // 2
    bias = bias_ref[...]
    weight_ref = full_weight(weight_refs, full_ref)

    @pl.loop(0, 2)
    def _(i):
        start = pl.multiple_of(i * half, 64)
        mixed = jnp.dot(
            taps_of(in_ref, start, half, points), weight_ref[...], preferred_element_type=F32
        )
        hidden_ref[pl.ds(start, half)] = scale * mixed + bias


def norm_kernel(
    points, hidden_ref, same_hbm, normal_ref, inverse_ref, padded_ref, turned_ref, same_ref, sems
):
    rows, channels = normal_ref.shape
    (copy,) = fetch((same_hbm,), (same_ref,), sems)
    centre, inverse = norm_stats(lambda i: hidden_ref[at(i)], rows, channels, same_ref, copy)
    inverse_ref[...] = inverse
    clear_edges(padded_ref, points)

    @pl.loop(0, rows // CHUNK)
    def _(i):
        normal = (hidden_ref[at(i)] - centre) * inverse
        normal_ref[at(i)] = normal
        act = (normal / (1.0 + jnp.exp(-normal))).astype(BF16)
        padded_ref[at(i, points)] = act
        turned_ref[:, at(i)] = act.T


def second_kernel(points, scale, in_ref, clip_hbm, target_hbm, *refs):
    weight_refs = refs[:-5]
    error_ref, full_ref, clip_ref, target_ref, sems = refs[-5:]
    copies = fetch((clip_hbm, target_hbm), (clip_ref, target_ref), sems)
    rows = clip_ref.shape[0]
    half = rows // 2
    clear_edges(error_ref, points)
    weight_ref = full_weight(weight_refs, full_ref)
    if len(weight_refs) == 1:
        full_ref[...] = weight_ref[...]
    for copy in copies:
        copy.wait()

    @pl.loop(0, 2)
    def _(i):
        start = pl.multiple_of(i * half, 64)
        mixed = jnp.dot(
            taps_of(in_ref, start, half, points), weight_ref[...], preferred_element_type=F32
        )
        here = pl.ds(start, half)
        output = clip_ref[here].astype(F32) + scale * mixed
        error_ref[pl.ds(pl.multiple_of(start + points, 64), half)] = (
            output - target_ref[here].astype(F32)
        ).astype(BF16)


def back_kernel(points, scale, error_ref, weight_ref, grad_ref):
    rows, channels = grad_ref.shape
    half = rows // 2
    last = (((1,), (1,)), ((), ()))

    @pl.loop(0, 2)
    def _(i):
        start = pl.multiple_of(i * half, 64)
        total = None
        for t in range(3):
            part = lax.dot_general(
                error_ref[pl.ds(pl.multiple_of(start + (2 - t) * points, 64), half)],
                weight_ref[t * channels : (t + 1) * channels],
                last,
                preferred_element_type=F32,
            )
            total = part if total is None else total + part
        grad_ref[pl.ds(start, half)] = scale * total


def norm_back_kernel(
    points, act_grad_ref, normal_ref, inverse_ref, same_hbm, out_ref, grad_ref, same_ref, sems
):
    (copy,) = fetch((same_hbm,), (same_ref,), sems)
    rows, channels = normal_ref.shape
    counted = rows * (channels // GN_GROUPS)

    def through(i, sums):
        normal = normal_ref[at(i)]
        gate = 1.0 / (1.0 + jnp.exp(-normal))
        grad = act_grad_ref[at(i)] * (gate * (1.0 + normal * (1.0 - gate)))
        grad_ref[at(i)] = grad

        def fold(value):
            return value.reshape(CHUNK // 8, 8, channels).sum(axis=0)

        return sums[0] + fold(grad), sums[1] + fold(grad * normal)

    zero = jnp.zeros((8, channels), F32)
    plain, crossed = lax.fori_loop(0, rows // CHUNK, through, (zero, zero))
    copy.wait()
    same_group = same_ref[...]
    mean = spread(plain.sum(axis=0, keepdims=True), same_group) * (1.0 / counted)
    slope = spread(crossed.sum(axis=0, keepdims=True), same_group) * (1.0 / counted)
    inverse = inverse_ref[...]
    clear_edges(out_ref, points)

    @pl.loop(0, rows // CHUNK)
    def _(i):
        value = (grad_ref[at(i)] - mean - normal_ref[at(i)] * slope) * inverse
        out_ref[at(i, points)] = value.astype(BF16)


FACTOR_ROWS = 16
MEMBER_ROWS = 4


def split_rows(row):
    high = row.astype(BF16).astype(F32)
    return [high, row - high]


def join_factors(first, second, count):
    rest = jnp.zeros((FACTOR_ROWS - 2 * count, first.shape[1]), F32)
    rows = [first.astype(F32)[0:count], second.astype(F32)[0:count]]
    rows += [rest] if rest.shape[0] else []
    return jnp.concatenate(rows, axis=0).astype(BF16)


def grad_kernel(points, scale, block, centred, me_ref, act_ref, cotangent_ref, *refs):
    refs = list(refs)
    turned_ref = refs.pop()
    total_ref = refs.pop()
    if act_ref.shape == turned_ref.shape:
        turned_ref = act_ref
    channels, rows = turned_ref.shape
    if turned_ref is not act_ref:

        @pl.loop(0, rows // CHUNK)
        def _(i):
            turned_ref[:, at(i)] = act_ref[at(i, points)].T

    if centred:
        ones = jnp.ones((rows, 128), BF16)
        mean = jnp.dot(turned_ref[...], ones, preferred_element_type=F32) * (1.0 / rows)
        sums = scale * jnp.dot(
            jnp.ones((16, rows), BF16),
            cotangent_ref[pl.ds(points, rows)],
            preferred_element_type=F32,
        )
        factors = [mean.T[0:1], sums[0:1], jnp.zeros((FACTOR_ROWS - 2, channels), F32)]
        factors = jnp.concatenate(factors, axis=0)
        common = jnp.concatenate([mean] * (channels // 128), axis=1) * sums[0:1]

    @pl.loop(0, 3)
    def _(t):
        shifted = cotangent_ref[pl.ds(pl.multiple_of((2 - t) * points, 64), rows)]
        product = scale * jnp.dot(turned_ref[...], shifted, preferred_element_type=F32)
        if centred:
            product = product - common
        total_ref[pl.ds(pl.multiple_of(t * channels, 128), channels)] = product

    if block is not None:
        home_ref, away_refs = refs[0], refs[1:]
        me = me_ref[0]
        count = home_ref.shape[0]

        for j in range(count):
            away = pl.multiple_of((me ^ (2 * j + 1)) * block, 16)
            home = pl.multiple_of((me ^ (2 * j)) * block, 16)
            away_refs[j][...] = total_ref[pl.ds(away, block)].astype(BF16)
            home_ref[j] = total_ref[pl.ds(home, block)]

    elif centred:
        refs[0][...] = factors


def mean_and_sums(scale, turned, cotangent):
    rows = turned.shape[1]
    mean = jnp.dot(turned, jnp.ones((rows, 128), BF16), preferred_element_type=F32) * (1.0 / rows)
    sums = jnp.dot(jnp.ones((16, rows), BF16), cotangent, preferred_element_type=F32)
    return mean, scale * sums[0:8]


def half_kernel(points, scale, odd, me_ref, turned_ref, cotangent_ref, *refs):
    refs, total_ref = refs[:-1], refs[-1]
    channels, rows = turned_ref.shape
    if odd:
        away_ref, home_ref, mean_ref, sums_ref = refs
        mean, sums = mean_and_sums(scale, turned_ref[...], cotangent_ref[pl.ds(points, rows)])
        mean_ref[...] = mean
        sums_ref[...] = sums
        factors = split_rows(mean.T[0:1]) + split_rows(sums[0:1])
        factors += [jnp.zeros((FACTOR_ROWS - MEMBER_ROWS, channels), F32)]
    else:
        mean_ref, sums_ref, away_ref, home_ref = refs
    size, block = total_ref.shape[0] // 2, home_ref.shape[1]
    chip = lax.shift_right_logical(me_ref[0], 1)
    for first in range(2):

        @pl.when(((chip & 1) ^ odd) == first)
        def _():
            for i, start in enumerate((first * size, (first + 2) * size)):
                row = start
                while row < start + size:
                    t, low = divmod(row, channels)
                    high = min(channels, low + start + size - row)
                    shift = (2 - t) * points
                    product = scale * jnp.dot(
                        turned_ref[low:high],
                        cotangent_ref[shift : shift + rows],
                        preferred_element_type=F32,
                    )
                    common = jnp.concatenate([mean_ref[low:high]] * (channels // 128), axis=1)
                    place = i * size + row - start
                    total_ref[place : place + high - low] = product - common * sums_ref[0:1]
                    row += high - low

    for k, top in enumerate((1, 0)):
        start = (lax.shift_right_logical(chip, 1) ^ top) * size
        for ref, core in ((away_ref, 1 - (me_ref[0] & 1)), (home_ref, me_ref[0] & 1)):
            part = total_ref[pl.ds(pl.multiple_of(start + core * block, 16), block)]
            if ref is home_ref:
                home_ref[k] = part
            else:
                away_ref[k * block : (k + 1) * block] = part.astype(BF16)
    if odd:
        away_ref[2 * block :] = jnp.concatenate(factors, axis=0).astype(BF16)


def odd_half(turned, cotangent, me, block, points, scale):
    channels = turned.shape[0]
    return call(
        functools.partial(half_kernel, points, scale, 1),
        [
            ((2 * block + FACTOR_ROWS, channels), BF16),
            ((2, block, channels), F32),
            ((channels, 128), F32),
            ((8, channels), F32),
        ],
        [pltpu.VMEM((4 * block, channels), F32)],
        "gradient_odd", smem(1) + vmem(2), 20,
    )(me, turned, cotangent)


def even_half(turned, cotangent, me, block, points, scale, mean, sums):
    channels = turned.shape[0]
    return call(
        functools.partial(half_kernel, points, scale, 0),
        [((2 * block, channels), BF16), ((2, block, channels), F32)],
        [pltpu.VMEM((4 * block, channels), F32)],
        "gradient_even", smem(1) + vmem(4), 20,
    )(me, turned, cotangent, mean, sums)


def gradient(act, cotangent, me, n_member, points, scale, centred):
    channels, rows = cotangent.shape[1], cotangent.shape[0] - 2 * points
    turned = pltpu.VMEM((channels, rows), BF16)
    block = 3 * channels // n_member
    specs = smem(1) + vmem(2)
    if block % 16 == 0 and not centred:
        chips = n_member // 2
        away = [((block, channels), BF16)] * chips
        home, *away = call(
            functools.partial(grad_kernel, points, scale, block, centred),
            [((chips, block, channels), F32)] + away,
            [pltpu.VMEM((3 * channels, channels), F32), turned],
            "gradient", specs, 24,
        )(me, act, cotangent)
        return away, home, None
    factors = [((FACTOR_ROWS, channels), F32)] if centred else []
    found = call(
        functools.partial(grad_kernel, points, scale, None, centred),
        factors + [((3 * channels, channels), F32)],
        [turned], "gradient", specs, 24,
    )(me, act, cotangent)
    total = found[-1].reshape(n_member, block, channels)
    order = [lax.dynamic_index_in_dim(total, me[0] ^ j, 0, keepdims=False) for j in range(n_member)]
    away, home = jnp.stack(order[1::2]).astype(BF16), jnp.stack(order[0::2])
    return [away], home, found[0] if centred else None


def swap(value, axis, size, offset):
    return lax.ppermute(value, axis, [(i, i ^ offset) for i in range(size)])


def order_after(value, *others):
    return lax.optimization_barrier((value, others))[0]


def stack_kernel(*refs):
    for k, source in enumerate(refs[:-1]):
        refs[-1][k] = source[...]


def stacked(*arrays):
    shape = (len(arrays),) + arrays[0].shape
    return call(stack_kernel, [(shape, BF16)], [], "stack", vmem(len(arrays)))(*arrays)[0]


TAIL = 64


def cut_of(rows):
    return (rows + TAIL) // 32 * 16


def pack_kernel(*refs):
    refs = refs[:4] + refs[6:]
    sources, (early_ref, late_ref, rates_ref) = refs[:4], refs[4:7]
    held, sems = refs[7:11], refs[11]
    copies = fetch(sources, held, sems)
    cols, rows = held[0].shape
    size, cut = rows + TAIL, cut_of(rows)

    def packed(i):
        copies[i].wait()
        whole = held[i][...].T
        rest = jnp.concatenate(
            [whole[:, 128:cols], jnp.zeros((4 * TAIL - rows, cols - 128), BF16)], axis=0
        )
        rest = [rest[q * TAIL : (q + 1) * TAIL] for q in range(4)]
        return jnp.concatenate([whole[:, 0:128], jnp.concatenate(rest, axis=1)], axis=0)

    early_ref[0:size] = packed(0)
    second = packed(1)
    early_ref[size:] = second[0:cut]
    late_ref[...] = second[cut:]
    rates_ref[0] = packed(2)
    rates_ref[1] = packed(3)


def unpacked(block_of, rows, n_group):
    parts = []
    for g in range(n_group):
        block = block_of(g)
        rest = block[rows:]
        pieces = [rest[:, 32 * q : 32 * q + 32] for q in range(4)]
        parts += [block[0:rows], jnp.concatenate(pieces, axis=0)[0:rows]]
    return jnp.concatenate(parts, axis=1)


def split_kernel(*refs):
    first_ref, second_ref, two_ref = refs[-3:]
    half, size = first_ref.shape[0], first_ref.shape[1]
    for k, source in enumerate(refs[:-3]):
        (first_ref if k < half else second_ref)[k % half] = source[0:size]
        two_ref[k] = source[size:]


def for_group(group_ref, n_group, half_ref, rows, block_of):
    for group in range(n_group):

        @pl.when(group_ref[0] == group)
        def _():
            block_of(
                lambda k, pick: half_ref.__setitem__(
                    k, unpacked(lambda g: pick(g ^ group), rows, n_group)
                )
            )


def two_step_kernel(rows, group_ref, *refs):
    first, first_x, first_y, second, second_y, second_x, half_ref = refs
    half = half_ref.shape[0] // 2

    def fill(store):
        @pl.loop(0, half)
        def _(k):
            pick = (first, first_x, first_y.at[0], first_y.at[1])
            store(k, lambda d: pick[d][k])
            late = (second, second_x.at[0], second_y, second_x.at[1])
            store(half + k, lambda d: late[d][k])

    for_group(group_ref, 4, half_ref, rows, fill)


def direct_kernel(rows, n_group, group_ref, *refs):
    early_refs, late_refs, half_ref = refs[:n_group], refs[n_group:-1], refs[-1]

    def fill(store):
        @pl.loop(0, half_ref.shape[0] // 2)
        def _(i):
            for odd, late_ref in enumerate(late_refs):
                k = 2 * i + odd
                store(k, lambda d: jnp.concatenate([early_refs[d][k], late_ref[i, d]], axis=0))

    for_group(group_ref, n_group, half_ref, rows, fill)


def rate_kernel(rows, n_group, group_ref, *refs):
    packed_refs, outs = refs[:n_group], refs[n_group:]
    for group in range(n_group):

        @pl.when(group_ref[0] == group)
        def _():
            for which, out in enumerate(outs):
                out[...] = unpacked(lambda g: packed_refs[g ^ group][which], rows, n_group)


def along_z(value, n_member):
    chips = n_member // 2
    return [value] + [swap(value, "member", n_member, 2 * k) for k in range(1, chips)]


def across_groups(value, n_group):
    return [value] + [swap(value, "group", n_group, k) for k in range(1, n_group)]


def weights_and_rates(n_group, n_member, conv1, conv2, rate1, rate2, group, me, clip, enter, bias_row):
    rows, cols = conv1.shape
    width = n_group * cols
    if (cols, n_group, n_member, rows % 16) != (160, 4, 8, 0) or rows > 4 * TAIL:
        own = [lax.all_gather(w, "group", axis=1, tiled=True) for w in (conv1, conv2)]
        full = [lax.all_gather(w, "member", axis=0, tiled=True) for w in own]

        def rates(after):
            return [lax.all_gather(w, "group", axis=1, tiled=True) for w in (rate1, rate2)]

        second = lambda after: (full[1], own[1][None])
        return (full[0],), second, own[0][None], rates, enter(clip), bias_row
    size, cut, chips = rows + TAIL, cut_of(rows), n_member // 2
    early_rows, late, both_rates = pl.pallas_call(
        pack_kernel,
        out_shape=(
            jax.ShapeDtypeStruct((size + cut, 128), BF16),
            jax.ShapeDtypeStruct((size - cut, 128), BF16),
            jax.ShapeDtypeStruct((2, size, 128), BF16),
        ),
        in_specs=hbm(4) + smem(2),
        out_specs=tuple(vmem(3)),
        scratch_shapes=[pltpu.VMEM((cols, rows), BF16)] * 4 + [pltpu.SemaphoreType.DMA((4,))],
        cost_estimate=pl.CostEstimate(flops=0, bytes_accessed=1024, transcendentals=0),
        name="pack",
    )(conv1.T, conv2.T, rate1.T, rate2.T, group, me)

    def unpack(kernel, *packed):
        (mine,) = call(
            kernel, [((chips, rows, width), BF16)], [], "unpack", smem(1) + vmem(len(packed))
        )(group, *packed)
        return me, mine, swap(mine, "member", n_member, 1)

    along = along_z(early_rows, n_member)
    late_x = swap(late, "group", n_group, 1)
    late_x, bias_row = order_after((late_x, bias_row), ())
    late = stacked(late, late_x)
    late_y = swap(late, "group", n_group, 2)
    act = enter(order_after(clip, (late, bias_row)))
    along, late_y, act = order_after((along, late_y, act), ())
    first, second, along_two = call(
        split_kernel,
        [((chips // 2, size, 128), BF16)] * 2 + [((chips, cut, 128), BF16)], [],
        "split", vmem(chips),
    )(*along)
    first_x = swap(first, "group", n_group, 1)
    second_y = swap(second, "group", n_group, 2)
    late, late_y = order_after((late, late_y), first)
    late = stacked(late, late_y).reshape(n_group, size - cut, 128)
    late_z = swap(late, "member", n_member, 4)
    first_y = swap(stacked(first, first_x), "group", n_group, 2)
    second_x = swap(stacked(second, second_y), "group", n_group, 1)
    late = stacked(late, late_z)
    late_z = swap(late, "member", n_member, 2)
    halves_one = unpack(
        functools.partial(two_step_kernel, rows),
        order_after(first, late), first_x, first_y, second, second_y, second_x,
    )
    along_two = across_groups(order_after(along_two, halves_one[1]), n_group)

    def halves_two(after):
        kernel = functools.partial(direct_kernel, rows, n_group)
        return unpack(kernel, *along_two, *order_after((late, late_z), after))

    def rates(after):
        blocks = across_groups(order_after(both_rates, after), n_group)
        return call(
            functools.partial(rate_kernel, rows, n_group),
            [((rows, width), BF16)] * 2, [], "rates", smem(1) + vmem(n_group),
        )(group, *blocks)

    return halves_one, halves_two, halves_one[1], rates, act, bias_row


def add_kernel(kept_ref, received_ref, *out_refs):
    away_ref, kept_out = out_refs[0], out_refs[1]

    for k in range(away_ref.shape[0]):
        away_ref[k] = (kept_ref[2 * k + 1] + received_ref[2 * k + 1].astype(F32)).astype(BF16)
        kept_out[k] = kept_ref[2 * k] + received_ref[2 * k].astype(F32)


def add_received(kept, received):
    half = (kept.shape[0] // 2,) + kept.shape[1:]
    return call(add_kernel, [(half, BF16), (half, F32)], [], "add", vmem(2))(kept, received)


def halve_to_owner(away, kept, received, n_member, bit=1):
    while True:
        if received is None:
            received = swap(away, "member", n_member, 2 * bit)
        if kept.shape[0] == 1:
            return kept[0], received[0]
        away, kept = add_received(kept, received)
        received = None
        bit *= 2


def pair_kernel(own_ref, home_ref, received_ref, away_ref):
    rows = home_ref.shape[1]
    for k in range(2):
        here = slice(k * rows, (k + 1) * rows)
        away_ref[here] = (home_ref[k] + received_ref[here].astype(F32)).astype(BF16)
    away_ref[2 * rows :] = join_factors(
        own_ref[2 * rows :], received_ref[2 * rows :], MEMBER_ROWS
    )


def pair_sums(own, home, received):
    return call(pair_kernel, [(own.shape, BF16)], [], "pair", vmem(3), 12)(own, home, received)[0]


def parts_kernel(home_ref, *refs):
    received_refs, outs = refs[:4], refs[4:]
    for k, out in zip((3, 1, 2, 0), outs):
        out[...] = (home_ref[k] + received_refs[k][...].astype(F32)).astype(out.dtype)


def pair_parts(home, received):
    shape = home.shape[1:]
    return call(
        parts_kernel, [(shape, BF16), (shape, BF16), (shape, F32), (shape, F32)], [],
        "pair", vmem(5), 12,
    )(home, *received)


def merge_kernel(middle_ref, received_ref, out_ref):
    out_ref[...] = (middle_ref[...] + received_ref[...].astype(F32)).astype(BF16)


def merge(middle, received):
    return call(merge_kernel, [(middle.shape, BF16)], [], "merge", vmem(2))(middle, received)[0]


def merge_factors_kernel(home_ref, pair_ref, sent_ref, received_ref, out_ref):
    rows = home_ref.shape[1]
    total = home_ref[0] + pair_ref[0:rows].astype(F32) + received_ref[0:rows].astype(F32)
    out_ref[0:rows] = total.astype(BF16)
    out_ref[rows:] = join_factors(
        sent_ref[2 * rows :], received_ref[2 * rows :], 2 * MEMBER_ROWS
    )


def merge_factors(home, pair, sent, received):
    shape = (home.shape[1] + FACTOR_ROWS, home.shape[2])
    return call(merge_factors_kernel, [(shape, BF16)], [], "merge", vmem(4))(
        home, pair, sent, received
    )[0]


def update_kernel(own_ref, rate_ref, *refs):
    total = refs[0][...]
    for ref in refs[1:-1]:
        total = total + ref[...].astype(F32)
    refs[-1][...] = own_ref[0].astype(F32) - rate_ref[...].astype(F32) * total


def common_update_kernel(
    me_ref, own_ref, rate_ref, home_ref, pair_ref, half_ref, sent_ref, received_ref, out_ref
):
    rows, channels = rate_ref.shape
    total = home_ref[1] + pair_ref[rows : 2 * rows].astype(F32)
    total = total + half_ref[rows : 2 * rows].astype(F32) + received_ref[0:rows].astype(F32)
    means, sums = [], []
    for ref in (sent_ref, received_ref):
        parts = ref[rows:].astype(F32)
        for start in range(0, FACTOR_ROWS, MEMBER_ROWS):
            means.append(parts[start : start + 1] + parts[start + 1 : start + 2])
            sums.append(parts[start + 2 : start + 3] + parts[start + 3 : start + 4])
    means, sums = jnp.concatenate(means, axis=0), jnp.concatenate(sums, axis=0)
    means = jnp.concatenate([means] * 3, axis=1)
    for member in range(3 * channels // rows):

        @pl.when(me_ref[0] == member)
        def _():
            common = lax.dot_general(
                means[:, member * rows : (member + 1) * rows],
                sums,
                (((0,), (0,)), ((), ())),
                precision=lax.Precision.HIGHEST,
                preferred_element_type=F32,
            )
            out_ref[...] = own_ref[0].astype(F32) - rate_ref[...].astype(F32) * (total + common)


def common_update(me, own, rate, *terms):
    return call(
        common_update_kernel, [(rate.shape, F32)], [], "update", smem(1) + vmem(7), 12
    )(me, own, rate, *terms)[0]


def update(own, rate, *terms):
    shape = rate.shape
    return call(
        update_kernel, [(shape, F32)], [], "update", vmem(2 + len(terms)),
    )(own, rate, *terms)[0]


def common_term(every, me, own_rows):
    sums = every[:, 1]
    mean = jnp.concatenate([every[:, 0]] * 3, axis=1)
    mean = lax.dynamic_slice_in_dim(mean, me[0] * own_rows, own_rows, 1)
    return lax.dot_general(
        mean, sums, (((0,), (0,)), ((), ())), precision=lax.Precision.HIGHEST
    )


def shards(
    n_group,
    n_member,
    clips,
    targets,
    timestep,
    identity,
    conv1_weight,
    conv2_weight,
    rate1,
    rate2,
    time_proj,
    subject_table,
):
    frames, points, channels = (clips.shape[1], clips.shape[2], clips.shape[3])
    rows, padded = frames * points, (frames + 2) * points
    scale = 1.0 / math.sqrt(3 * channels)
    group = lax.axis_index("group").astype(jnp.int32)[None]
    me = lax.axis_index("member").astype(jnp.int32)[None]
    own_rows = conv1_weight.shape[0]
    clip, target = clips.reshape(rows, channels), targets.reshape(rows, channels)
    blocks = np.arange(channels) // (channels // GN_GROUPS)
    same_group = jnp.asarray((blocks[:, None] == blocks[None, :]), BF16)

    bias_row = time_bias(timestep[0], identity[0], subject_table, time_proj)

    def enter(clip):
        return call(
            functools.partial(enter_kernel, points),
            [((padded, channels), BF16)],
            [
                pltpu.VMEM((rows, channels), BF16),
                pltpu.VMEM(same_group.shape, BF16),
                pltpu.SemaphoreType.DMA((2,)),
            ],
            "enter", hbm(2), 12,
        )(clip, same_group)[0]

    weight_one, weight_two, own_one, rates, act_one, bias_row = weights_and_rates(
        n_group, n_member, conv1_weight, conv2_weight, rate1, rate2, group, me, clip, enter, bias_row
    )

    def weight_specs(weight):
        return vmem(1) if len(weight) == 1 else smem(1) + vmem(2)

    (hidden,) = call(
        functools.partial(first_kernel, points, scale),
        [((rows, channels), F32)],
        [pltpu.VMEM((3 * channels, channels), BF16)],
        "conv", vmem(2) + weight_specs(weight_one), 20,
    )(act_one, bias_row, *weight_one)
    weight_two = weight_two(hidden)
    own_two = weight_two[1]
    if len(weight_two) == 2:
        weight_two = weight_two[:1]
    normal, inverse, act_two, turned_two = call(
        functools.partial(norm_kernel, points),
        [
            ((rows, channels), F32),
            ((1, channels), F32),
            ((padded, channels), BF16),
            ((channels, rows), BF16),
        ],
        [pltpu.VMEM(same_group.shape, BF16), pltpu.SemaphoreType.DMA((1,))],
        "norm", vmem(1) + hbm(1), 20,
    )(order_after(hidden, weight_two[:2]), same_group)
    error, full_two = call(
        functools.partial(second_kernel, points, scale),
        [((padded, channels), BF16), ((3 * channels, channels), BF16)],
        [pltpu.VMEM((rows, channels), BF16)] * 2 + [pltpu.SemaphoreType.DMA((2,))],
        "conv_error", vmem(1) + hbm(2) + weight_specs(weight_two), 24,
    )(act_two, clip, target, *weight_two)
    staged = n_member == 8 and own_rows % 16 == 0
    if staged:
        away_two, home_two, *means = odd_half(turned_two, error, me, own_rows, points, scale)
        received_two = swap(away_two, "member", n_member, 1)
        away_even, home_even = even_half(
            turned_two, error, me, own_rows, points, scale, *means
        )
        received_even = swap(away_even, "member", n_member, 1)
        half_two = pair_sums(away_two, home_two, order_after(received_two, away_even))
        from_two = swap(half_two, "member", n_member, 2)
        error = order_after(error, half_two)
    else:
        (away_two,), home_two, factors = gradient(
            turned_two, error, me, n_member, points, scale, True
        )
        received_two = swap(away_two, "member", n_member, 1)
    (grad_act,) = call(
        functools.partial(back_kernel, points, scale),
        [((rows, channels), F32)], [], "back", vmem(2), 20,
    )(error, full_two)
    (grad_hidden,) = call(
        functools.partial(norm_back_kernel, points),
        [((padded, channels), BF16)],
        [
            pltpu.VMEM((rows, channels), F32),
            pltpu.VMEM(same_group.shape, BF16),
            pltpu.SemaphoreType.DMA((1,)),
        ],
        "norm_back", vmem(3) + hbm(1), 20,
    )(grad_act, normal, inverse, same_group)
    away_one, home_one, _ = gradient(
        act_one, grad_hidden, me, n_member, points, scale, False
    )
    received_one = [swap(part, "member", n_member, 1) for part in away_one]
    if staged:
        received_one, from_two = order_after((received_one, from_two), ())
        far_one, near_one, middle_one, kept_one = pair_parts(home_one, received_one)
        from_one = swap(far_one, "member", n_member, 2)
        beside_one = swap(near_one, "member", n_member, 2)
        merged_two = merge_factors(home_even, received_even, half_two, from_two)
        across_two = swap(merged_two, "member", n_member, 4)
        rate_one, rate_two = rates(far_one)
        middle_one = order_after(middle_one, (rate_one, rate_two))
        merged_one = merge(middle_one, from_one)
        across_one = swap(merged_one, "member", n_member, 4)
        adapted_two = common_update(
            me, own_two, rate_two, home_even, received_even, from_two, merged_two,
            order_after(across_two, merged_one),
        )
        kept_one, adapted_two = order_after((kept_one, adapted_two), ())
        adapted_one = update(own_one, rate_one, kept_one, beside_one, across_one)
    else:
        rate_one, rate_two = rates(away_one)
        every = lax.all_gather(factors, "member")
        terms_two = halve_to_owner(*add_received(home_two, received_two), None, n_member)
        terms_one = halve_to_owner(*add_received(home_one, received_one[0]), None, n_member)
        adapted_two = update(own_two, rate_two, *terms_two, common_term(every, me, own_rows))
        adapted_one = update(own_one, rate_one, *terms_one)
    return (adapted_one[None], adapted_two[None])


def solution(mesh):
    n_group, n_member = mesh.shape["group"], mesh.shape["member"]
    return jax.shard_map(
        lambda *arrays: shards(n_group, n_member, *arrays),
        mesh=mesh,
        in_specs=(
            P(("group", "member"), None, None, None),
            P(("group", "member"), None, None, None),
            P(("group", "member")),
            P(("group", "member")),
            P("member", "group"),
            P("member", "group"),
            P("member", "group"),
            P("member", "group"),
            P(),
            P(),
        ),
        out_specs=(P("group", "member", None), P("group", "member", None)),
        check_vma=False,
    )
```

```python
import functools
import math

import jax
import jax.numpy as jnp
import numpy as np
from jax import lax
from jax.experimental import pallas as pl
from jax.experimental.pallas import tpu as pltpu
from jax.sharding import PartitionSpec as P

GN_GROUPS = 32
CHUNK = 128
MEGA = 1024 * 1024
BF16 = jnp.bfloat16
F32 = jnp.float32


def time_bias(step_index, ident, subject_table, time_proj):
    half_width = subject_table.shape[1] // 2
    freqs = jnp.exp(-math.log(10000.0) * jnp.arange(half_width, dtype=F32) / half_width)
    angles = step_index.astype(F32) * freqs
    embedding = jnp.concatenate([jnp.cos(angles), jnp.sin(angles)])
    onehot = (jnp.arange(subject_table.shape[0], dtype=jnp.int32) == ident).astype(F32)
    embedding = embedding + jnp.dot(onehot, subject_table, precision=lax.Precision.HIGHEST)
    activated = jax.nn.silu(embedding).astype(BF16)
    return jnp.dot(activated[None, :], time_proj, preferred_element_type=F32)


def vmem(count):
    return [pl.BlockSpec(memory_space=pltpu.VMEM)] * count


def hbm(count):
    return [pl.BlockSpec(memory_space=pltpu.HBM)] * count


def smem(count):
    return [pl.BlockSpec(memory_space=pltpu.SMEM)] * count


def call(body, out_shape, scratch, name, in_specs, limit=8):
    outs = len(out_shape)
    return pl.pallas_call(
        body,
        out_shape=tuple(jax.ShapeDtypeStruct(s, d) for s, d in out_shape),
        in_specs=in_specs,
        out_specs=tuple(vmem(outs)),
        scratch_shapes=scratch,
        compiler_params=pltpu.CompilerParams(vmem_limit_bytes=limit * MEGA),
        cost_estimate=pl.CostEstimate(flops=0, bytes_accessed=1024, transcendentals=0),
        name=name,
    )


def spread(row, same_group):
    high = row.astype(BF16)
    rest = row - high.astype(F32)
    middle = rest.astype(BF16)
    low = (rest - middle.astype(F32)).astype(BF16)
    stacked = jnp.concatenate(
        [jnp.broadcast_to(part, (16, row.shape[1])) for part in (high, middle, low)], axis=0
    )
    sums = jnp.dot(stacked, same_group, preferred_element_type=F32)
    return sums[0:1] + sums[16:17] + sums[32:33]


def norm_stats(read, rows, channels, same_ref, copy=None):
    counted = rows * (channels // GN_GROUPS)
    steps = rows // CHUNK
    total = lax.fori_loop(
        0,
        steps,
        lambda i, acc: acc + read(i).reshape(CHUNK // 8, 8, channels).sum(axis=0),
        jnp.zeros((8, channels), F32),
    ).sum(axis=0, keepdims=True)
    if copy is not None:
        copy.wait()
    same_group = same_ref[...]
    centre = spread(total, same_group) * (1.0 / counted)

    def squares(i, acc):
        centred = read(i) - centre
        return acc + (centred * centred).reshape(CHUNK // 8, 8, channels).sum(axis=0)

    square = lax.fori_loop(0, steps, squares, jnp.zeros((8, channels), F32)).sum(
        axis=0, keepdims=True
    )
    variance = spread(square, same_group) * (1.0 / counted)
    return centre, lax.rsqrt(variance + 1e-05)


def at(i, shift=0):
    return pl.ds(pl.multiple_of(i * CHUNK + shift, 64), CHUNK)


def clear_edges(padded_ref, points):
    edge = jnp.zeros((points, padded_ref.shape[1]), padded_ref.dtype)
    padded_ref[0:points] = edge
    padded_ref[padded_ref.shape[0] - points :] = edge


def fetch(sources, held, sems):
    copies = [
        pltpu.make_async_copy(source, place, sems.at[i])
        for i, (source, place) in enumerate(zip(sources, held))
    ]
    for copy in copies:
        copy.start()
    return copies


def enter_kernel(points, clip_hbm, same_hbm, padded_ref, clip_ref, same_ref, sems):
    rows, channels = clip_ref.shape
    for copy in fetch((clip_hbm, same_hbm), (clip_ref, same_ref), sems):
        copy.wait()
    centre, inverse = norm_stats(
        lambda i: clip_ref[at(i)].astype(F32), rows, channels, same_ref
    )
    clear_edges(padded_ref, points)

    @pl.loop(0, rows // CHUNK)
    def _(i):
        normal = (clip_ref[at(i)].astype(F32) - centre) * inverse
        padded_ref[at(i, points)] = (normal / (1.0 + jnp.exp(-normal))).astype(BF16)


def taps_of(padded_ref, start, size, points):
    return jnp.concatenate(
        [padded_ref[pl.ds(start + t * points, size)] for t in range(3)], axis=1
    )


def full_weight(weight_refs, full_ref):
    if len(weight_refs) == 1:
        return weight_refs[0]
    member_ref, mine_ref, other_ref = weight_refs
    member, rows = member_ref[0], mine_ref.shape[1]

    @pl.loop(0, mine_ref.shape[0])
    def _(k):
        for half, source in ((0, mine_ref), (1, other_ref)):
            start = pl.multiple_of((member ^ (2 * k + half)) * rows, 16)
            full_ref[pl.ds(start, rows)] = source[k]

    return full_ref


def first_kernel(points, scale, in_ref, bias_ref, *refs):
    weight_refs = refs[:-2]
    hidden_ref, full_ref = refs[-2:]
    half = hidden_ref.shape[0] // 2
    bias = bias_ref[...]
    weight_ref = full_weight(weight_refs, full_ref)

    @pl.loop(0, 2)
    def _(i):
        start = pl.multiple_of(i * half, 64)
        mixed = jnp.dot(
            taps_of(in_ref, start, half, points), weight_ref[...], preferred_element_type=F32
        )
        hidden_ref[pl.ds(start, half)] = scale * mixed + bias


def norm_kernel(
    points, hidden_ref, same_hbm, normal_ref, inverse_ref, padded_ref, turned_ref, same_ref, sems
):
    rows, channels = normal_ref.shape
    (copy,) = fetch((same_hbm,), (same_ref,), sems)
    centre, inverse = norm_stats(lambda i: hidden_ref[at(i)], rows, channels, same_ref, copy)
    inverse_ref[...] = inverse
    clear_edges(padded_ref, points)

    @pl.loop(0, rows // CHUNK)
    def _(i):
        normal = (hidden_ref[at(i)] - centre) * inverse
        normal_ref[at(i)] = normal
        act = (normal / (1.0 + jnp.exp(-normal))).astype(BF16)
        padded_ref[at(i, points)] = act
        turned_ref[:, at(i)] = act.T


def second_kernel(points, scale, in_ref, clip_hbm, target_hbm, *refs):
    weight_refs = refs[:-5]
    error_ref, full_ref, clip_ref, target_ref, sems = refs[-5:]
    copies = fetch((clip_hbm, target_hbm), (clip_ref, target_ref), sems)
    rows = clip_ref.shape[0]
    half = rows // 2
    clear_edges(error_ref, points)
    weight_ref = full_weight(weight_refs, full_ref)
    if len(weight_refs) == 1:
        full_ref[...] = weight_ref[...]
    for copy in copies:
        copy.wait()

    @pl.loop(0, 2)
    def _(i):
        start = pl.multiple_of(i * half, 64)
        mixed = jnp.dot(
            taps_of(in_ref, start, half, points), weight_ref[...], preferred_element_type=F32
        )
        here = pl.ds(start, half)
        output = clip_ref[here].astype(F32) + scale * mixed
        error_ref[pl.ds(pl.multiple_of(start + points, 64), half)] = (
            output - target_ref[here].astype(F32)
        ).astype(BF16)


def back_kernel(points, scale, error_ref, weight_ref, grad_ref):
    rows, channels = grad_ref.shape
    half = rows // 2
    last = (((1,), (1,)), ((), ()))

    @pl.loop(0, 2)
    def _(i):
        start = pl.multiple_of(i * half, 64)
        total = None
        for t in range(3):
            part = lax.dot_general(
                error_ref[pl.ds(pl.multiple_of(start + (2 - t) * points, 64), half)],
                weight_ref[t * channels : (t + 1) * channels],
                last,
                preferred_element_type=F32,
            )
            total = part if total is None else total + part
        grad_ref[pl.ds(start, half)] = scale * total


def norm_back_kernel(
    points, act_grad_ref, normal_ref, inverse_ref, same_hbm, out_ref, grad_ref, same_ref, sems
):
    (copy,) = fetch((same_hbm,), (same_ref,), sems)
    rows, channels = normal_ref.shape
    counted = rows * (channels // GN_GROUPS)

    def through(i, sums):
        normal = normal_ref[at(i)]
        gate = 1.0 / (1.0 + jnp.exp(-normal))
        grad = act_grad_ref[at(i)] * (gate * (1.0 + normal * (1.0 - gate)))
        grad_ref[at(i)] = grad

        def fold(value):
            return value.reshape(CHUNK // 8, 8, channels).sum(axis=0)

        return sums[0] + fold(grad), sums[1] + fold(grad * normal)

    zero = jnp.zeros((8, channels), F32)
    plain, crossed = lax.fori_loop(0, rows // CHUNK, through, (zero, zero))
    copy.wait()
    same_group = same_ref[...]
    mean = spread(plain.sum(axis=0, keepdims=True), same_group) * (1.0 / counted)
    slope = spread(crossed.sum(axis=0, keepdims=True), same_group) * (1.0 / counted)
    inverse = inverse_ref[...]
    clear_edges(out_ref, points)

    @pl.loop(0, rows // CHUNK)
    def _(i):
        value = (grad_ref[at(i)] - mean - normal_ref[at(i)] * slope) * inverse
        out_ref[at(i, points)] = value.astype(BF16)


FACTOR_ROWS = 16
MEMBER_ROWS = 4


def split_rows(row):
    high = row.astype(BF16).astype(F32)
    return [high, row - high]


def join_factors(first, second, count):
    rest = jnp.zeros((FACTOR_ROWS - 2 * count, first.shape[1]), F32)
    rows = [first.astype(F32)[0:count], second.astype(F32)[0:count]]
    rows += [rest] if rest.shape[0] else []
    return jnp.concatenate(rows, axis=0).astype(BF16)


def grad_kernel(points, scale, block, centred, me_ref, act_ref, cotangent_ref, *refs):
    refs = list(refs)
    turned_ref = refs.pop()
    total_ref = refs.pop()
    if act_ref.shape == turned_ref.shape:
        turned_ref = act_ref
    channels, rows = turned_ref.shape
    if turned_ref is not act_ref:

        @pl.loop(0, rows // CHUNK)
        def _(i):
            turned_ref[:, at(i)] = act_ref[at(i, points)].T

    if centred:
        ones = jnp.ones((rows, 128), BF16)
        mean = jnp.dot(turned_ref[...], ones, preferred_element_type=F32) * (1.0 / rows)
        sums = scale * jnp.dot(
            jnp.ones((16, rows), BF16),
            cotangent_ref[pl.ds(points, rows)],
            preferred_element_type=F32,
        )
        factors = [mean.T[0:1], sums[0:1], jnp.zeros((FACTOR_ROWS - 2, channels), F32)]
        factors = jnp.concatenate(factors, axis=0)
        common = jnp.concatenate([mean] * (channels // 128), axis=1) * sums[0:1]

    @pl.loop(0, 3)
    def _(t):
        shifted = cotangent_ref[pl.ds(pl.multiple_of((2 - t) * points, 64), rows)]
        product = scale * jnp.dot(turned_ref[...], shifted, preferred_element_type=F32)
        if centred:
            product = product - common
        total_ref[pl.ds(pl.multiple_of(t * channels, 128), channels)] = product

    if block is not None:
        home_ref, away_refs = refs[0], refs[1:]
        me = me_ref[0]
        count = home_ref.shape[0]

        for j in range(count):
            away = pl.multiple_of((me ^ (2 * j + 1)) * block, 16)
            home = pl.multiple_of((me ^ (2 * j)) * block, 16)
            away_refs[j][...] = total_ref[pl.ds(away, block)].astype(BF16)
            home_ref[j] = total_ref[pl.ds(home, block)]

    elif centred:
        refs[0][...] = factors


def mean_and_sums(scale, turned, cotangent):
    rows = turned.shape[1]
    mean = jnp.dot(turned, jnp.ones((rows, 128), BF16), preferred_element_type=F32) * (1.0 / rows)
    sums = jnp.dot(jnp.ones((16, rows), BF16), cotangent, preferred_element_type=F32)
    return mean, scale * sums[0:8]


def half_kernel(points, scale, odd, me_ref, turned_ref, cotangent_ref, *refs):
    refs, total_ref = refs[:-1], refs[-1]
    channels, rows = turned_ref.shape
    if odd:
        away_ref, home_ref, mean_ref, sums_ref = refs
        mean, sums = mean_and_sums(scale, turned_ref[...], cotangent_ref[pl.ds(points, rows)])
        mean_ref[...] = mean
        sums_ref[...] = sums
        factors = split_rows(mean.T[0:1]) + split_rows(sums[0:1])
        factors += [jnp.zeros((FACTOR_ROWS - MEMBER_ROWS, channels), F32)]
    else:
        mean_ref, sums_ref, away_ref, home_ref = refs
    size, block = total_ref.shape[0] // 2, home_ref.shape[1]
    chip = lax.shift_right_logical(me_ref[0], 1)
    for first in range(2):

        @pl.when(((chip & 1) ^ odd) == first)
        def _():
            for i, start in enumerate((first * size, (first + 2) * size)):
                row = start
                while row < start + size:
                    t, low = divmod(row, channels)
                    high = min(channels, low + start + size - row)
                    shift = (2 - t) * points
                    product = scale * jnp.dot(
                        turned_ref[low:high],
                        cotangent_ref[shift : shift + rows],
                        preferred_element_type=F32,
                    )
                    common = jnp.concatenate([mean_ref[low:high]] * (channels // 128), axis=1)
                    place = i * size + row - start
                    total_ref[place : place + high - low] = product - common * sums_ref[0:1]
                    row += high - low

    for k, top in enumerate((1, 0)):
        start = (lax.shift_right_logical(chip, 1) ^ top) * size
        for ref, core in ((away_ref, 1 - (me_ref[0] & 1)), (home_ref, me_ref[0] & 1)):
            part = total_ref[pl.ds(pl.multiple_of(start + core * block, 16), block)]
            if ref is home_ref:
                home_ref[k] = part
            else:
                away_ref[k * block : (k + 1) * block] = part.astype(BF16)
    if odd:
        away_ref[2 * block :] = jnp.concatenate(factors, axis=0).astype(BF16)


def odd_half(turned, cotangent, me, block, points, scale):
    channels = turned.shape[0]
    return call(
        functools.partial(half_kernel, points, scale, 1),
        [
            ((2 * block + FACTOR_ROWS, channels), BF16),
            ((2, block, channels), F32),
            ((channels, 128), F32),
            ((8, channels), F32),
        ],
        [pltpu.VMEM((4 * block, channels), F32)],
        "gradient_odd", smem(1) + vmem(2), 20,
    )(me, turned, cotangent)


def even_half(turned, cotangent, me, block, points, scale, mean, sums):
    channels = turned.shape[0]
    return call(
        functools.partial(half_kernel, points, scale, 0),
        [((2 * block, channels), BF16), ((2, block, channels), F32)],
        [pltpu.VMEM((4 * block, channels), F32)],
        "gradient_even", smem(1) + vmem(4), 20,
    )(me, turned, cotangent, mean, sums)


def gradient(act, cotangent, me, n_member, points, scale, centred):
    channels, rows = cotangent.shape[1], cotangent.shape[0] - 2 * points
    turned = pltpu.VMEM((channels, rows), BF16)
    block = 3 * channels // n_member
    specs = smem(1) + vmem(2)
    if block % 16 == 0 and not centred:
        chips = n_member // 2
        away = [((block, channels), BF16)] * chips
        home, *away = call(
            functools.partial(grad_kernel, points, scale, block, centred),
            [((chips, block, channels), F32)] + away,
            [pltpu.VMEM((3 * channels, channels), F32), turned],
            "gradient", specs, 24,
        )(me, act, cotangent)
        return away, home, None
    factors = [((FACTOR_ROWS, channels), F32)] if centred else []
    found = call(
        functools.partial(grad_kernel, points, scale, None, centred),
        factors + [((3 * channels, channels), F32)],
        [turned], "gradient", specs, 24,
    )(me, act, cotangent)
    total = found[-1].reshape(n_member, block, channels)
    order = [lax.dynamic_index_in_dim(total, me[0] ^ j, 0, keepdims=False) for j in range(n_member)]
    away, home = jnp.stack(order[1::2]).astype(BF16), jnp.stack(order[0::2])
    return [away], home, found[0] if centred else None


def swap(value, axis, size, offset):
    return lax.ppermute(value, axis, [(i, i ^ offset) for i in range(size)])


def order_after(value, *others):
    return lax.optimization_barrier((value, others))[0]


def stack_kernel(*refs):
    for k, source in enumerate(refs[:-1]):
        refs[-1][k] = source[...]


def stacked(*arrays):
    shape = (len(arrays),) + arrays[0].shape
    return call(stack_kernel, [(shape, BF16)], [], "stack", vmem(len(arrays)))(*arrays)[0]


TAIL = 64


def cut_of(rows):
    return (rows + TAIL) // 32 * 16


def packed_block(whole):
    rows, cols = whole.shape
    rest = jnp.concatenate(
        [whole[:, 128:cols], jnp.zeros((4 * TAIL - rows, cols - 128), BF16)], axis=0
    )
    rest = [rest[q * TAIL : (q + 1) * TAIL] for q in range(4)]
    return jnp.concatenate([whole[:, 0:128], jnp.concatenate(rest, axis=1)], axis=0)


def pack_kernel(*refs):
    sources, (early_ref, late_ref), held, sems = refs[:2], refs[4:6], refs[6:8], refs[8]
    copies = fetch(sources, held, sems)
    cols, rows = held[0].shape
    size, cut = rows + TAIL, cut_of(rows)
    copies[0].wait()
    early_ref[0:size] = packed_block(held[0][...].T)
    copies[1].wait()
    second = packed_block(held[1][...].T)
    early_ref[size:] = second[0:cut]
    late_ref[...] = second[cut:]


def pack_rates_kernel(one_ref, two_ref, out_ref):
    out_ref[0] = packed_block(one_ref[...].T)
    out_ref[1] = packed_block(two_ref[...].T)


def unpacked(block_of, rows, n_group):
    parts = []
    for g in range(n_group):
        block = block_of(g)
        rest = block[rows:]
        pieces = [rest[:, 32 * q : 32 * q + 32] for q in range(4)]
        parts += [block[0:rows], jnp.concatenate(pieces, axis=0)[0:rows]]
    return jnp.concatenate(parts, axis=1)


def split_kernel(*refs):
    first_ref, second_ref, two_ref = refs[-3:]
    half, size = first_ref.shape[0], first_ref.shape[1]
    for k, source in enumerate(refs[:-3]):
        (first_ref if k < half else second_ref)[k % half] = source[0:size]
        two_ref[k] = source[size:]


def for_group(group_ref, n_group, half_ref, rows, block_of):
    for group in range(n_group):

        @pl.when(group_ref[0] == group)
        def _():
            block_of(
                lambda k, pick: half_ref.__setitem__(
                    k, unpacked(lambda g: pick(g ^ group), rows, n_group)
                )
            )


def two_step_kernel(rows, group_ref, *refs):
    first, first_x, first_y, second, second_y, second_x, half_ref = refs
    half = half_ref.shape[0] // 2

    def fill(store):
        @pl.loop(0, half)
        def _(k):
            pick = (first, first_x, first_y.at[0], first_y.at[1])
            store(k, lambda d: pick[d][k])
            late = (second, second_x.at[0], second_y, second_x.at[1])
            store(half + k, lambda d: late[d][k])

    for_group(group_ref, 4, half_ref, rows, fill)


def direct_kernel(rows, n_group, group_ref, *refs):
    early_refs, late_refs, half_ref = refs[:n_group], refs[n_group:-1], refs[-1]

    def fill(store):
        @pl.loop(0, half_ref.shape[0] // 2)
        def _(i):
            for odd, late_ref in enumerate(late_refs):
                k = 2 * i + odd
                store(k, lambda d: jnp.concatenate([early_refs[d][k], late_ref[i, d]], axis=0))

    for_group(group_ref, n_group, half_ref, rows, fill)


def rate_kernel(rows, n_group, group_ref, *refs):
    packed_refs, outs = refs[:n_group], refs[n_group:]
    for group in range(n_group):

        @pl.when(group_ref[0] == group)
        def _():
            for which, out in enumerate(outs):
                out[...] = unpacked(lambda g: packed_refs[g ^ group][which], rows, n_group)


def along_z(value, n_member):
    chips = n_member // 2
    return [value] + [swap(value, "member", n_member, 2 * k) for k in range(1, chips)]


def across_groups(value, n_group):
    return [value] + [swap(value, "group", n_group, k) for k in range(1, n_group)]


def weights_and_rates(n_group, n_member, conv1, conv2, rate1, rate2, group, me, clip, enter, bias_row):
    rows, cols = conv1.shape
    width = n_group * cols
    if (cols, n_group, n_member, rows % 16) != (160, 4, 8, 0) or rows > 4 * TAIL:
        own = [lax.all_gather(w, "group", axis=1, tiled=True) for w in (conv1, conv2)]
        full = [lax.all_gather(w, "member", axis=0, tiled=True) for w in own]

        def rates(after):
            return [lax.all_gather(w, "group", axis=1, tiled=True) for w in (rate1, rate2)]

        second = lambda after: (full[1], own[1][None])
        return (full[0],), second, own[0][None], rates, enter(clip), bias_row
    size, cut, chips = rows + TAIL, cut_of(rows), n_member // 2
    early_rows, late = pl.pallas_call(
        pack_kernel,
        out_shape=(
            jax.ShapeDtypeStruct((size + cut, 128), BF16),
            jax.ShapeDtypeStruct((size - cut, 128), BF16),
        ),
        in_specs=hbm(2) + smem(2),
        out_specs=tuple(vmem(2)),
        scratch_shapes=[pltpu.VMEM((cols, rows), BF16)] * 2 + [pltpu.SemaphoreType.DMA((2,))],
        cost_estimate=pl.CostEstimate(flops=0, bytes_accessed=1024, transcendentals=0),
        name="pack",
    )(conv1.T, conv2.T, group, me)

    def unpack(kernel, *packed):
        (mine,) = call(
            kernel, [((chips, rows, width), BF16)], [], "unpack", smem(1) + vmem(len(packed))
        )(group, *packed)
        return me, mine, swap(mine, "member", n_member, 1)

    along = along_z(early_rows, n_member)
    late_x = swap(late, "group", n_group, 1)
    late_x, bias_row = order_after((late_x, bias_row), ())
    late = stacked(late, late_x)
    late_y = swap(late, "group", n_group, 2)
    act = enter(order_after(clip, (late, bias_row)))
    along, late_y, act = order_after((along, late_y, act), ())
    first, second, along_two = call(
        split_kernel,
        [((chips // 2, size, 128), BF16)] * 2 + [((chips, cut, 128), BF16)], [],
        "split", vmem(chips),
    )(*along)
    first_x = swap(first, "group", n_group, 1)
    second_y = swap(second, "group", n_group, 2)
    late, late_y = order_after((late, late_y), first)
    late = stacked(late, late_y).reshape(n_group, size - cut, 128)
    late_z = swap(late, "member", n_member, 4)
    first_y = swap(stacked(first, first_x), "group", n_group, 2)
    second_x = swap(stacked(second, second_y), "group", n_group, 1)
    late = stacked(late, late_z)
    late_z = swap(late, "member", n_member, 2)
    halves_one = unpack(
        functools.partial(two_step_kernel, rows),
        order_after(first, late), first_x, first_y, second, second_y, second_x,
    )
    along_two = across_groups(order_after(along_two, halves_one[1]), n_group)

    def halves_two(after):
        kernel = functools.partial(direct_kernel, rows, n_group)
        return unpack(kernel, *along_two, *order_after((late, late_z), after))

    def rates(after):
        (both,) = call(pack_rates_kernel, [((2, size, 128), BF16)], [], "pack_rates", vmem(2))(
            rate1.T, rate2.T
        )
        blocks = across_groups(order_after(both, after), n_group)
        return call(
            functools.partial(rate_kernel, rows, n_group),
            [((rows, width), BF16)] * 2, [], "rates", smem(1) + vmem(n_group),
        )(group, *blocks)

    return halves_one, halves_two, halves_one[1], rates, act, bias_row


def add_kernel(kept_ref, received_ref, *out_refs):
    away_ref, kept_out = out_refs[0], out_refs[1]

    for k in range(away_ref.shape[0]):
        away_ref[k] = (kept_ref[2 * k + 1] + received_ref[2 * k + 1].astype(F32)).astype(BF16)
        kept_out[k] = kept_ref[2 * k] + received_ref[2 * k].astype(F32)


def add_received(kept, received):
    half = (kept.shape[0] // 2,) + kept.shape[1:]
    return call(add_kernel, [(half, BF16), (half, F32)], [], "add", vmem(2))(kept, received)


def halve_to_owner(away, kept, received, n_member, bit=1):
    while True:
        if received is None:
            received = swap(away, "member", n_member, 2 * bit)
        if kept.shape[0] == 1:
            return kept[0], received[0]
        away, kept = add_received(kept, received)
        received = None
        bit *= 2


def pair_kernel(own_ref, home_ref, received_ref, away_ref):
    rows = home_ref.shape[1]
    for k in range(2):
        here = slice(k * rows, (k + 1) * rows)
        away_ref[here] = (home_ref[k] + received_ref[here].astype(F32)).astype(BF16)
    away_ref[2 * rows :] = join_factors(
        own_ref[2 * rows :], received_ref[2 * rows :], MEMBER_ROWS
    )


def pair_sums(own, home, received):
    return call(pair_kernel, [(own.shape, BF16)], [], "pair", vmem(3), 12)(own, home, received)[0]


def parts_kernel(home_ref, *refs):
    received_refs, outs = refs[:4], refs[4:]
    for k, out in zip((3, 1, 2, 0), outs):
        out[...] = (home_ref[k] + received_refs[k][...].astype(F32)).astype(out.dtype)


def pair_parts(home, received):
    shape = home.shape[1:]
    return call(
        parts_kernel, [(shape, BF16), (shape, BF16), (shape, F32), (shape, F32)], [],
        "pair", vmem(5), 12,
    )(home, *received)


def merge_kernel(middle_ref, received_ref, out_ref):
    out_ref[...] = (middle_ref[...] + received_ref[...].astype(F32)).astype(BF16)


def merge(middle, received):
    return call(merge_kernel, [(middle.shape, BF16)], [], "merge", vmem(2))(middle, received)[0]


def merge_factors_kernel(home_ref, pair_ref, sent_ref, received_ref, out_ref):
    rows = home_ref.shape[1]
    total = home_ref[0] + pair_ref[0:rows].astype(F32) + received_ref[0:rows].astype(F32)
    out_ref[0:rows] = total.astype(BF16)
    out_ref[rows:] = join_factors(
        sent_ref[2 * rows :], received_ref[2 * rows :], 2 * MEMBER_ROWS
    )


def merge_factors(home, pair, sent, received):
    shape = (home.shape[1] + FACTOR_ROWS, home.shape[2])
    return call(merge_factors_kernel, [(shape, BF16)], [], "merge", vmem(4))(
        home, pair, sent, received
    )[0]


def update_kernel(own_ref, rate_ref, *refs):
    total = refs[0][...]
    for ref in refs[1:-1]:
        total = total + ref[...].astype(F32)
    refs[-1][...] = own_ref[0].astype(F32) - rate_ref[...].astype(F32) * total


def common_update_kernel(
    me_ref, own_ref, rate_ref, home_ref, pair_ref, half_ref, sent_ref, received_ref, out_ref
):
    rows, channels = rate_ref.shape
    total = home_ref[1] + pair_ref[rows : 2 * rows].astype(F32)
    total = total + half_ref[rows : 2 * rows].astype(F32) + received_ref[0:rows].astype(F32)
    means, sums = [], []
    for ref in (sent_ref, received_ref):
        parts = ref[rows:].astype(F32)
        for start in range(0, FACTOR_ROWS, MEMBER_ROWS):
            means.append(parts[start : start + 1] + parts[start + 1 : start + 2])
            sums.append(parts[start + 2 : start + 3] + parts[start + 3 : start + 4])
    means, sums = jnp.concatenate(means, axis=0), jnp.concatenate(sums, axis=0)
    means = jnp.concatenate([means] * 3, axis=1)
    for member in range(3 * channels // rows):

        @pl.when(me_ref[0] == member)
        def _():
            common = lax.dot_general(
                means[:, member * rows : (member + 1) * rows],
                sums,
                (((0,), (0,)), ((), ())),
                precision=lax.Precision.HIGHEST,
                preferred_element_type=F32,
            )
            out_ref[...] = own_ref[0].astype(F32) - rate_ref[...].astype(F32) * (total + common)


def common_update(me, own, rate, *terms):
    return call(
        common_update_kernel, [(rate.shape, F32)], [], "update", smem(1) + vmem(7), 12
    )(me, own, rate, *terms)[0]


def update(own, rate, *terms):
    shape = rate.shape
    return call(
        update_kernel, [(shape, F32)], [], "update", vmem(2 + len(terms)),
    )(own, rate, *terms)[0]


def common_term(every, me, own_rows):
    sums = every[:, 1]
    mean = jnp.concatenate([every[:, 0]] * 3, axis=1)
    mean = lax.dynamic_slice_in_dim(mean, me[0] * own_rows, own_rows, 1)
    return lax.dot_general(
        mean, sums, (((0,), (0,)), ((), ())), precision=lax.Precision.HIGHEST
    )


def shards(
    n_group,
    n_member,
    clips,
    targets,
    timestep,
    identity,
    conv1_weight,
    conv2_weight,
    rate1,
    rate2,
    time_proj,
    subject_table,
):
    frames, points, channels = (clips.shape[1], clips.shape[2], clips.shape[3])
    rows, padded = frames * points, (frames + 2) * points
    scale = 1.0 / math.sqrt(3 * channels)
    group = lax.axis_index("group").astype(jnp.int32)[None]
    me = lax.axis_index("member").astype(jnp.int32)[None]
    own_rows = conv1_weight.shape[0]
    clip, target = clips.reshape(rows, channels), targets.reshape(rows, channels)
    blocks = np.arange(channels) // (channels // GN_GROUPS)
    same_group = jnp.asarray((blocks[:, None] == blocks[None, :]), BF16)

    bias_row = time_bias(timestep[0], identity[0], subject_table, time_proj)

    def enter(clip):
        return call(
            functools.partial(enter_kernel, points),
            [((padded, channels), BF16)],
            [
                pltpu.VMEM((rows, channels), BF16),
                pltpu.VMEM(same_group.shape, BF16),
                pltpu.SemaphoreType.DMA((2,)),
            ],
            "enter", hbm(2), 12,
        )(clip, same_group)[0]

    weight_one, weight_two, own_one, rates, act_one, bias_row = weights_and_rates(
        n_group, n_member, conv1_weight, conv2_weight, rate1, rate2, group, me, clip, enter, bias_row
    )

    def weight_specs(weight):
        return vmem(1) if len(weight) == 1 else smem(1) + vmem(2)

    (hidden,) = call(
        functools.partial(first_kernel, points, scale),
        [((rows, channels), F32)],
        [pltpu.VMEM((3 * channels, channels), BF16)],
        "conv", vmem(2) + weight_specs(weight_one), 20,
    )(act_one, bias_row, *weight_one)
    weight_two = weight_two(hidden)
    own_two = weight_two[1]
    if len(weight_two) == 2:
        weight_two = weight_two[:1]
    normal, inverse, act_two, turned_two = call(
        functools.partial(norm_kernel, points),
        [
            ((rows, channels), F32),
            ((1, channels), F32),
            ((padded, channels), BF16),
            ((channels, rows), BF16),
        ],
        [pltpu.VMEM(same_group.shape, BF16), pltpu.SemaphoreType.DMA((1,))],
        "norm", vmem(1) + hbm(1), 20,
    )(order_after(hidden, weight_two[:2]), same_group)
    error, full_two = call(
        functools.partial(second_kernel, points, scale),
        [((padded, channels), BF16), ((3 * channels, channels), BF16)],
        [pltpu.VMEM((rows, channels), BF16)] * 2 + [pltpu.SemaphoreType.DMA((2,))],
        "conv_error", vmem(1) + hbm(2) + weight_specs(weight_two), 24,
    )(act_two, clip, target, *weight_two)
    staged = n_member == 8 and own_rows % 16 == 0
    if staged:
        away_two, home_two, *means = odd_half(turned_two, error, me, own_rows, points, scale)
        received_two = swap(away_two, "member", n_member, 1)
        away_even, home_even = even_half(
            turned_two, error, me, own_rows, points, scale, *means
        )
        received_even = swap(away_even, "member", n_member, 1)
        half_two = pair_sums(away_two, home_two, order_after(received_two, away_even))
        from_two = swap(half_two, "member", n_member, 2)
        error = order_after(error, half_two)
    else:
        (away_two,), home_two, factors = gradient(
            turned_two, error, me, n_member, points, scale, True
        )
        received_two = swap(away_two, "member", n_member, 1)
    (grad_act,) = call(
        functools.partial(back_kernel, points, scale),
        [((rows, channels), F32)], [], "back", vmem(2), 20,
    )(error, full_two)
    (grad_hidden,) = call(
        functools.partial(norm_back_kernel, points),
        [((padded, channels), BF16)],
        [
            pltpu.VMEM((rows, channels), F32),
            pltpu.VMEM(same_group.shape, BF16),
            pltpu.SemaphoreType.DMA((1,)),
        ],
        "norm_back", vmem(3) + hbm(1), 20,
    )(grad_act, normal, inverse, same_group)
    away_one, home_one, _ = gradient(
        act_one, grad_hidden, me, n_member, points, scale, False
    )
    received_one = [swap(part, "member", n_member, 1) for part in away_one]
    if staged:
        received_one, from_two = order_after((received_one, from_two), ())
        far_one, near_one, middle_one, kept_one = pair_parts(home_one, received_one)
        from_one = swap(far_one, "member", n_member, 2)
        beside_one = swap(order_after(near_one, from_one), "member", n_member, 2)
        merged_two = merge_factors(home_even, received_even, half_two, from_two)
        across_two = swap(merged_two, "member", n_member, 4)
        rate_one, rate_two = rates(from_one)
        merged_one = merge(middle_one, from_one)
        across_one = swap(merged_one, "member", n_member, 4)
        adapted_two = common_update(
            me, own_two, rate_two, home_even, received_even, from_two, merged_two,
            order_after(across_two, merged_one),
        )
        kept_one, adapted_two = order_after((kept_one, adapted_two), ())
        adapted_one = update(own_one, rate_one, kept_one, beside_one, across_one)
    else:
        rate_one, rate_two = rates(away_one)
        every = lax.all_gather(factors, "member")
        terms_two = halve_to_owner(*add_received(home_two, received_two), None, n_member)
        terms_one = halve_to_owner(*add_received(home_one, received_one[0]), None, n_member)
        adapted_two = update(own_two, rate_two, *terms_two, common_term(every, me, own_rows))
        adapted_one = update(own_one, rate_one, *terms_one)
    return (adapted_one[None], adapted_two[None])


def solution(mesh):
    n_group, n_member = mesh.shape["group"], mesh.shape["member"]
    return jax.shard_map(
        lambda *arrays: shards(n_group, n_member, *arrays),
        mesh=mesh,
        in_specs=(
            P(("group", "member"), None, None, None),
            P(("group", "member"), None, None, None),
            P(("group", "member")),
            P(("group", "member")),
            P("member", "group"),
            P("member", "group"),
            P("member", "group"),
            P("member", "group"),
            P(),
            P(),
        ),
        out_specs=(P("group", "member", None), P("group", "member", None)),
        check_vma=False,
    )
```

```python
import functools
import math

import jax
import jax.numpy as jnp
import numpy as np
from jax import lax
from jax.experimental import pallas as pl
from jax.experimental.pallas import tpu as pltpu
from jax.sharding import PartitionSpec as P

GN_GROUPS = 32
CHUNK = 128
MEGA = 1024 * 1024
BF16 = jnp.bfloat16
F32 = jnp.float32


def time_bias(step_index, ident, subject_table, time_proj):
    half_width = subject_table.shape[1] // 2
    freqs = jnp.exp(-math.log(10000.0) * jnp.arange(half_width, dtype=F32) / half_width)
    angles = step_index.astype(F32) * freqs
    embedding = jnp.concatenate([jnp.cos(angles), jnp.sin(angles)])
    onehot = (jnp.arange(subject_table.shape[0], dtype=jnp.int32) == ident).astype(F32)
    embedding = embedding + jnp.dot(onehot, subject_table, precision=lax.Precision.HIGHEST)
    activated = jax.nn.silu(embedding).astype(BF16)
    return jnp.dot(activated[None, :], time_proj, preferred_element_type=F32)


def vmem(count):
    return [pl.BlockSpec(memory_space=pltpu.VMEM)] * count


def hbm(count):
    return [pl.BlockSpec(memory_space=pltpu.HBM)] * count


def smem(count):
    return [pl.BlockSpec(memory_space=pltpu.SMEM)] * count


def call(body, out_shape, scratch, name, in_specs, limit=8):
    outs = len(out_shape)
    return pl.pallas_call(
        body,
        out_shape=tuple(jax.ShapeDtypeStruct(s, d) for s, d in out_shape),
        in_specs=in_specs,
        out_specs=tuple(vmem(outs)),
        scratch_shapes=scratch,
        compiler_params=pltpu.CompilerParams(vmem_limit_bytes=limit * MEGA),
        cost_estimate=pl.CostEstimate(flops=0, bytes_accessed=1024, transcendentals=0),
        name=name,
    )


def spread(row, same_group):
    high = row.astype(BF16)
    rest = row - high.astype(F32)
    middle = rest.astype(BF16)
    low = (rest - middle.astype(F32)).astype(BF16)
    stacked = jnp.concatenate(
        [jnp.broadcast_to(part, (16, row.shape[1])) for part in (high, middle, low)], axis=0
    )
    sums = jnp.dot(stacked, same_group, preferred_element_type=F32)
    return sums[0:1] + sums[16:17] + sums[32:33]


def norm_stats(read, rows, channels, same_ref, total=None):
    counted = rows * (channels // GN_GROUPS)
    steps = rows // CHUNK
    if total is None:
        total = lax.fori_loop(
            0,
            steps,
            lambda i, acc: acc + read(i).reshape(CHUNK // 8, 8, channels).sum(axis=0),
            jnp.zeros((8, channels), F32),
        )
    total = total.sum(axis=0, keepdims=True)
    same_group = same_ref[...]
    centre = spread(total, same_group) * (1.0 / counted)

    def squares(i, acc):
        centred = read(i) - centre
        return acc + (centred * centred).reshape(CHUNK // 8, 8, channels).sum(axis=0)

    square = lax.fori_loop(0, steps, squares, jnp.zeros((8, channels), F32)).sum(
        axis=0, keepdims=True
    )
    variance = spread(square, same_group) * (1.0 / counted)
    return centre, lax.rsqrt(variance + 1e-05)


def at(i, shift=0):
    return pl.ds(pl.multiple_of(i * CHUNK + shift, 64), CHUNK)


def clear_edges(padded_ref, points):
    edge = jnp.zeros((points, padded_ref.shape[1]), padded_ref.dtype)
    padded_ref[0:points] = edge
    padded_ref[padded_ref.shape[0] - points :] = edge


def fetch(sources, held, sems):
    copies = [
        pltpu.make_async_copy(source, place, sems.at[i])
        for i, (source, place) in enumerate(zip(sources, held))
    ]
    for copy in copies:
        copy.start()
    return copies


def enter_kernel(
    points, clip_hbm, same_hbm, padded_ref, turned_ref, clip_ref, same_ref, sems
):
    rows, channels = clip_ref.shape
    for copy in fetch((clip_hbm, same_hbm), (clip_ref, same_ref), sems):
        copy.wait()
    centre, inverse = norm_stats(
        lambda i: clip_ref[at(i)].astype(F32), rows, channels, same_ref
    )
    clear_edges(padded_ref, points)

    @pl.loop(0, rows // CHUNK)
    def _(i):
        normal = (clip_ref[at(i)].astype(F32) - centre) * inverse
        act = (normal / (1.0 + jnp.exp(-normal))).astype(BF16)
        padded_ref[at(i, points)] = act
        turned_ref[:, at(i)] = act.T


def taps_of(padded_ref, start, size, points):
    return jnp.concatenate(
        [padded_ref[pl.ds(start + t * points, size)] for t in range(3)], axis=1
    )


def full_weight(weight_refs, full_ref):
    if len(weight_refs) == 1:
        return weight_refs[0]
    member_ref, mine_ref, other_ref = weight_refs
    member, rows = member_ref[0], mine_ref.shape[1]

    @pl.loop(0, mine_ref.shape[0])
    def _(k):
        for half, source in ((0, mine_ref), (1, other_ref)):
            start = pl.multiple_of((member ^ (2 * k + half)) * rows, 16)
            full_ref[pl.ds(start, rows)] = source[k]

    return full_ref


def first_kernel(points, scale, in_ref, bias_ref, *refs):
    weight_refs = refs[:-3]
    hidden_ref, sums_ref, full_ref = refs[-3:]
    rows, channels = hidden_ref.shape
    weight_ref = full_weight(weight_refs, full_ref)
    mixed = jnp.dot(
        taps_of(in_ref, 0, rows, points), weight_ref[...], preferred_element_type=F32
    )
    hidden = scale * mixed + bias_ref[...]
    hidden_ref[...] = hidden
    sums_ref[...] = hidden.reshape(rows // 8, 8, channels).sum(axis=0)


def norm_kernel(
    points, hidden_ref, sums_ref, same_ref,
    normal_ref, inverse_ref, padded_ref, turned_ref, mean_ref,
):
    rows, channels = normal_ref.shape
    centre, inverse = norm_stats(
        lambda i: hidden_ref[at(i)], rows, channels, same_ref, sums_ref[...]
    )
    inverse_ref[...] = inverse
    clear_edges(padded_ref, points)

    @pl.loop(0, rows // CHUNK)
    def _(i):
        normal = (hidden_ref[at(i)] - centre) * inverse
        normal_ref[at(i)] = normal
        act = (normal / (1.0 + jnp.exp(-normal))).astype(BF16)
        padded_ref[at(i, points)] = act
        turned_ref[:, at(i)] = act.T

    ones = jnp.ones((rows, 128), BF16)
    mean_ref[...] = jnp.dot(turned_ref[...], ones, preferred_element_type=F32) * (1.0 / rows)


def second_kernel(points, scale, in_ref, clip_ref, target_ref, *refs):
    weight_refs = refs[:-2]
    error_ref, full_ref = refs[-2:]
    rows = clip_ref.shape[0]
    clear_edges(error_ref, points)
    weight_ref = full_weight(weight_refs, full_ref)
    if len(weight_refs) == 1:
        full_ref[...] = weight_ref[...]
    mixed = jnp.dot(
        taps_of(in_ref, 0, rows, points), weight_ref[...], preferred_element_type=F32
    )
    output = clip_ref[...].astype(F32) + scale * mixed
    error_ref[points : points + rows] = (output - target_ref[...].astype(F32)).astype(BF16)


def back_kernel(points, scale, error_ref, weight_ref, grad_ref):
    rows, channels = grad_ref.shape
    half = rows // 2
    last = (((1,), (1,)), ((), ()))

    @pl.loop(0, 2)
    def _(i):
        start = pl.multiple_of(i * half, 64)
        total = None
        for t in range(3):
            part = lax.dot_general(
                error_ref[pl.ds(pl.multiple_of(start + (2 - t) * points, 64), half)],
                weight_ref[t * channels : (t + 1) * channels],
                last,
                preferred_element_type=F32,
            )
            total = part if total is None else total + part
        grad_ref[pl.ds(start, half)] = scale * total


def norm_back_kernel(
    points, act_grad_ref, normal_ref, inverse_ref, same_hbm, out_ref, grad_ref, same_ref, sems
):
    (copy,) = fetch((same_hbm,), (same_ref,), sems)
    rows, channels = normal_ref.shape
    counted = rows * (channels // GN_GROUPS)

    def through(i, sums):
        normal = normal_ref[at(i)]
        gate = 1.0 / (1.0 + jnp.exp(-normal))
        grad = act_grad_ref[at(i)] * (gate * (1.0 + normal * (1.0 - gate)))
        grad_ref[at(i)] = grad

        def fold(value):
            return value.reshape(CHUNK // 8, 8, channels).sum(axis=0)

        return sums[0] + fold(grad), sums[1] + fold(grad * normal)

    zero = jnp.zeros((8, channels), F32)
    plain, crossed = lax.fori_loop(0, rows // CHUNK, through, (zero, zero))
    copy.wait()
    same_group = same_ref[...]
    mean = spread(plain.sum(axis=0, keepdims=True), same_group) * (1.0 / counted)
    slope = spread(crossed.sum(axis=0, keepdims=True), same_group) * (1.0 / counted)
    inverse = inverse_ref[...]
    clear_edges(out_ref, points)

    @pl.loop(0, rows // CHUNK)
    def _(i):
        value = (grad_ref[at(i)] - mean - normal_ref[at(i)] * slope) * inverse
        out_ref[at(i, points)] = value.astype(BF16)


FACTOR_ROWS = 16
MEMBER_ROWS = 4


def split_rows(row):
    high = row.astype(BF16).astype(F32)
    return [high, row - high]


def join_factors(first, second, count):
    rest = jnp.zeros((FACTOR_ROWS - 2 * count, first.shape[1]), F32)
    rows = [first.astype(F32)[0:count], second.astype(F32)[0:count]]
    rows += [rest] if rest.shape[0] else []
    return jnp.concatenate(rows, axis=0).astype(BF16)


def grad_kernel(points, scale, block, centred, me_ref, act_ref, cotangent_ref, *refs):
    refs = list(refs)
    turned_ref = refs.pop()
    total_ref = refs.pop()
    if act_ref.shape == turned_ref.shape:
        turned_ref = act_ref
    channels, rows = turned_ref.shape
    if turned_ref is not act_ref:

        @pl.loop(0, rows // CHUNK)
        def _(i):
            turned_ref[:, at(i)] = act_ref[at(i, points)].T

    if centred:
        ones = jnp.ones((rows, 128), BF16)
        mean = jnp.dot(turned_ref[...], ones, preferred_element_type=F32) * (1.0 / rows)
        sums = scale * jnp.dot(
            jnp.ones((16, rows), BF16),
            cotangent_ref[pl.ds(points, rows)],
            preferred_element_type=F32,
        )
        factors = [mean.T[0:1], sums[0:1], jnp.zeros((FACTOR_ROWS - 2, channels), F32)]
        factors = jnp.concatenate(factors, axis=0)
        common = jnp.concatenate([mean] * (channels // 128), axis=1) * sums[0:1]

    @pl.loop(0, 3)
    def _(t):
        shifted = cotangent_ref[pl.ds(pl.multiple_of((2 - t) * points, 64), rows)]
        product = scale * jnp.dot(turned_ref[...], shifted, preferred_element_type=F32)
        if centred:
            product = product - common
        total_ref[pl.ds(pl.multiple_of(t * channels, 128), channels)] = product

    if block is not None:
        home_ref, away_refs = refs[0], refs[1:]
        me = me_ref[0]
        count = home_ref.shape[0]

        for j in range(count):
            away = pl.multiple_of((me ^ (2 * j + 1)) * block, 16)
            home = pl.multiple_of((me ^ (2 * j)) * block, 16)
            away_refs[j][...] = total_ref[pl.ds(away, block)].astype(BF16)
            home_ref[j] = total_ref[pl.ds(home, block)]

    elif centred:
        refs[0][...] = factors


def half_kernel(points, scale, odd, me_ref, turned_ref, cotangent_ref, mean_ref, *refs):
    refs, total_ref = refs[:-1], refs[-1]
    channels, rows = turned_ref.shape
    if odd:
        away_ref, home_ref, sums_ref = refs
        sums = jnp.dot(
            jnp.ones((16, rows), BF16),
            cotangent_ref[pl.ds(points, rows)],
            preferred_element_type=F32,
        )
        sums = scale * sums[0:8]
        sums_ref[...] = sums
        factors = split_rows(mean_ref[...].T[0:1]) + split_rows(sums[0:1])
        factors += [jnp.zeros((FACTOR_ROWS - MEMBER_ROWS, channels), F32)]
    else:
        sums_ref, away_ref, home_ref = refs
    size, block = total_ref.shape[0] // 2, home_ref.shape[1]
    chip = lax.shift_right_logical(me_ref[0], 1)
    for first in range(2):

        @pl.when(((chip & 1) ^ odd) == first)
        def _():
            for i, start in enumerate((first * size, (first + 2) * size)):
                row = start
                while row < start + size:
                    t, low = divmod(row, channels)
                    high = min(channels, low + start + size - row)
                    shift = (2 - t) * points
                    product = scale * jnp.dot(
                        turned_ref[low:high],
                        cotangent_ref[shift : shift + rows],
                        preferred_element_type=F32,
                    )
                    common = jnp.concatenate([mean_ref[low:high]] * (channels // 128), axis=1)
                    place = i * size + row - start
                    total_ref[place : place + high - low] = product - common * sums_ref[0:1]
                    row += high - low

    for k, top in enumerate((1, 0)):
        start = (lax.shift_right_logical(chip, 1) ^ top) * size
        for ref, core in ((away_ref, 1 - (me_ref[0] & 1)), (home_ref, me_ref[0] & 1)):
            part = total_ref[pl.ds(pl.multiple_of(start + core * block, 16), block)]
            if ref is home_ref:
                home_ref[k] = part
            else:
                away_ref[k * block : (k + 1) * block] = part.astype(BF16)
    if odd:
        away_ref[2 * block :] = jnp.concatenate(factors, axis=0).astype(BF16)


def odd_half(turned, cotangent, me, block, points, scale, mean):
    channels = turned.shape[0]
    return call(
        functools.partial(half_kernel, points, scale, 1),
        [
            ((2 * block + FACTOR_ROWS, channels), BF16),
            ((2, block, channels), F32),
            ((8, channels), F32),
        ],
        [pltpu.VMEM((4 * block, channels), F32)],
        "gradient_odd", smem(1) + vmem(3), 20,
    )(me, turned, cotangent, mean)


def even_half(turned, cotangent, me, block, points, scale, mean, sums):
    channels = turned.shape[0]
    return call(
        functools.partial(half_kernel, points, scale, 0),
        [((2 * block, channels), BF16), ((2, block, channels), F32)],
        [pltpu.VMEM((4 * block, channels), F32)],
        "gradient_even", smem(1) + vmem(4), 20,
    )(me, turned, cotangent, mean, sums)


def gradient(act, cotangent, me, n_member, points, scale, centred):
    channels, rows = cotangent.shape[1], cotangent.shape[0] - 2 * points
    turned = pltpu.VMEM((channels, rows), BF16)
    block = 3 * channels // n_member
    specs = smem(1) + vmem(2)
    if block % 16 == 0 and not centred:
        chips = n_member // 2
        away = [((block, channels), BF16)] * chips
        home, *away = call(
            functools.partial(grad_kernel, points, scale, block, centred),
            [((chips, block, channels), F32)] + away,
            [pltpu.VMEM((3 * channels, channels), F32), turned],
            "gradient", specs, 24,
        )(me, act, cotangent)
        return away, home, None
    factors = [((FACTOR_ROWS, channels), F32)] if centred else []
    found = call(
        functools.partial(grad_kernel, points, scale, None, centred),
        factors + [((3 * channels, channels), F32)],
        [turned], "gradient", specs, 24,
    )(me, act, cotangent)
    total = found[-1].reshape(n_member, block, channels)
    order = [lax.dynamic_index_in_dim(total, me[0] ^ j, 0, keepdims=False) for j in range(n_member)]
    away, home = jnp.stack(order[1::2]).astype(BF16), jnp.stack(order[0::2])
    return [away], home, found[0] if centred else None


def swap(value, axis, size, offset):
    return lax.ppermute(value, axis, [(i, i ^ offset) for i in range(size)])


def order_after(value, *others):
    return lax.optimization_barrier((value, others))[0]


def stack_kernel(*refs):
    for k, source in enumerate(refs[:-1]):
        refs[-1][k] = source[...]


def stacked(*arrays):
    shape = (len(arrays),) + arrays[0].shape
    return call(stack_kernel, [(shape, BF16)], [], "stack", vmem(len(arrays)))(*arrays)[0]


TAIL = 64


def cut_of(rows):
    return (rows + TAIL) // 32 * 16


def packed_block(whole):
    rows, cols = whole.shape
    rest = jnp.concatenate(
        [whole[:, 128:cols], jnp.zeros((4 * TAIL - rows, cols - 128), BF16)], axis=0
    )
    rest = [rest[q * TAIL : (q + 1) * TAIL] for q in range(4)]
    return jnp.concatenate([whole[:, 0:128], jnp.concatenate(rest, axis=1)], axis=0)


def pack_kernel(*refs):
    sources, (early_ref, late_ref), held, sems = refs[:2], refs[4:6], refs[6:8], refs[8]
    copies = fetch(sources, held, sems)
    cols, rows = held[0].shape
    size, cut = rows + TAIL, cut_of(rows)
    copies[0].wait()
    early_ref[0:size] = packed_block(held[0][...].T)
    copies[1].wait()
    second = packed_block(held[1][...].T)
    early_ref[size:] = second[0:cut]
    late_ref[...] = second[cut:]


def pack_rates_kernel(one_ref, two_ref, out_ref):
    out_ref[0] = packed_block(one_ref[...].T)
    out_ref[1] = packed_block(two_ref[...].T)


def unpacked(block_of, rows, n_group):
    parts = []
    for g in range(n_group):
        block = block_of(g)
        rest = block[rows:]
        pieces = [rest[:, 32 * q : 32 * q + 32] for q in range(4)]
        parts += [block[0:rows], jnp.concatenate(pieces, axis=0)[0:rows]]
    return jnp.concatenate(parts, axis=1)


def split_kernel(*refs):
    first_ref, second_ref, two_ref = refs[-3:]
    half, size = first_ref.shape[0], first_ref.shape[1]
    for k, source in enumerate(refs[:-3]):
        (first_ref if k < half else second_ref)[k % half] = source[0:size]
        two_ref[k] = source[size:]


def for_group(group_ref, n_group, half_ref, rows, block_of):
    for group in range(n_group):

        @pl.when(group_ref[0] == group)
        def _():
            block_of(
                lambda k, pick: half_ref.__setitem__(
                    k, unpacked(lambda g: pick(g ^ group), rows, n_group)
                )
            )


def two_step_kernel(rows, group_ref, *refs):
    first, first_x, first_y, second, second_y, second_x, half_ref = refs
    half = half_ref.shape[0] // 2

    def fill(store):
        @pl.loop(0, half)
        def _(k):
            pick = (first, first_x, first_y.at[0], first_y.at[1])
            store(k, lambda d: pick[d][k])
            late = (second, second_x.at[0], second_y, second_x.at[1])
            store(half + k, lambda d: late[d][k])

    for_group(group_ref, 4, half_ref, rows, fill)


def direct_kernel(rows, n_group, group_ref, *refs):
    early_refs, late_refs, half_ref = refs[:n_group], refs[n_group:-1], refs[-1]

    def fill(store):
        @pl.loop(0, half_ref.shape[0] // 2)
        def _(i):
            for odd, late_ref in enumerate(late_refs):
                k = 2 * i + odd
                store(k, lambda d: jnp.concatenate([early_refs[d][k], late_ref[i, d]], axis=0))

    for_group(group_ref, n_group, half_ref, rows, fill)


def rate_kernel(rows, n_group, group_ref, *refs):
    packed_refs, outs = refs[:n_group], refs[n_group:]
    for group in range(n_group):

        @pl.when(group_ref[0] == group)
        def _():
            for which, out in enumerate(outs):
                out[...] = unpacked(lambda g: packed_refs[g ^ group][which], rows, n_group)


def along_z(value, n_member):
    chips = n_member // 2
    return [value] + [swap(value, "member", n_member, 2 * k) for k in range(1, chips)]


def across_groups(value, n_group):
    return [value] + [swap(value, "group", n_group, k) for k in range(1, n_group)]


def weights_and_rates(n_group, n_member, conv1, conv2, rate1, rate2, group, me, clip, enter, bias_row):
    rows, cols = conv1.shape
    width = n_group * cols
    if (cols, n_group, n_member, rows % 16) != (160, 4, 8, 0) or rows > 4 * TAIL:
        own = [lax.all_gather(w, "group", axis=1, tiled=True) for w in (conv1, conv2)]
        full = [lax.all_gather(w, "member", axis=0, tiled=True) for w in own]

        def rates(after):
            return [lax.all_gather(w, "group", axis=1, tiled=True) for w in (rate1, rate2)]

        second = lambda after: (full[1], own[1][None])
        return (full[0],), second, own[0][None], rates, enter(clip), bias_row
    size, cut, chips = rows + TAIL, cut_of(rows), n_member // 2
    early_rows, late = pl.pallas_call(
        pack_kernel,
        out_shape=(
            jax.ShapeDtypeStruct((size + cut, 128), BF16),
            jax.ShapeDtypeStruct((size - cut, 128), BF16),
        ),
        in_specs=hbm(2) + smem(2),
        out_specs=tuple(vmem(2)),
        scratch_shapes=[pltpu.VMEM((cols, rows), BF16)] * 2 + [pltpu.SemaphoreType.DMA((2,))],
        cost_estimate=pl.CostEstimate(flops=0, bytes_accessed=1024, transcendentals=0),
        name="pack",
    )(conv1.T, conv2.T, group, me)

    def unpack(kernel, *packed):
        (mine,) = call(
            kernel, [((chips, rows, width), BF16)], [], "unpack", smem(1) + vmem(len(packed))
        )(group, *packed)
        return me, mine, swap(mine, "member", n_member, 1)

    along = along_z(early_rows, n_member)
    late_x = swap(late, "group", n_group, 1)
    late_x, bias_row = order_after((late_x, bias_row), ())
    late = stacked(late, late_x)
    late_y = swap(late, "group", n_group, 2)
    act = enter(order_after(clip, (late, bias_row)))
    along, late_y, act = order_after((along, late_y, act), ())
    first, second, along_two = call(
        split_kernel,
        [((chips // 2, size, 128), BF16)] * 2 + [((chips, cut, 128), BF16)], [],
        "split", vmem(chips),
    )(*along)
    first_x = swap(first, "group", n_group, 1)
    second_y = swap(second, "group", n_group, 2)
    late, late_y = order_after((late, late_y), first)
    late = stacked(late, late_y).reshape(n_group, size - cut, 128)
    late_z = swap(late, "member", n_member, 4)
    first_y = swap(stacked(first, first_x), "group", n_group, 2)
    second_x = swap(stacked(second, second_y), "group", n_group, 1)
    late = stacked(late, late_z)
    late_z = swap(late, "member", n_member, 2)
    halves_one = unpack(
        functools.partial(two_step_kernel, rows),
        order_after(first, late), first_x, first_y, second, second_y, second_x,
    )
    along_two = across_groups(order_after(along_two, halves_one[1]), n_group)

    def halves_two(after):
        kernel = functools.partial(direct_kernel, rows, n_group)
        return unpack(kernel, *along_two, *order_after((late, late_z), after))

    def rates(after):
        (both,) = call(pack_rates_kernel, [((2, size, 128), BF16)], [], "pack_rates", vmem(2))(
            rate1.T, rate2.T
        )
        blocks = across_groups(order_after(both, after), n_group)
        return call(
            functools.partial(rate_kernel, rows, n_group),
            [((rows, width), BF16)] * 2, [], "rates", smem(1) + vmem(n_group),
        )(group, *blocks)

    return halves_one, halves_two, halves_one[1], rates, act, bias_row


def add_kernel(kept_ref, received_ref, *out_refs):
    away_ref, kept_out = out_refs[0], out_refs[1]

    for k in range(away_ref.shape[0]):
        away_ref[k] = (kept_ref[2 * k + 1] + received_ref[2 * k + 1].astype(F32)).astype(BF16)
        kept_out[k] = kept_ref[2 * k] + received_ref[2 * k].astype(F32)


def add_received(kept, received):
    half = (kept.shape[0] // 2,) + kept.shape[1:]
    return call(add_kernel, [(half, BF16), (half, F32)], [], "add", vmem(2))(kept, received)


def halve_to_owner(away, kept, received, n_member, bit=1):
    while True:
        if received is None:
            received = swap(away, "member", n_member, 2 * bit)
        if kept.shape[0] == 1:
            return kept[0], received[0]
        away, kept = add_received(kept, received)
        received = None
        bit *= 2


def pair_kernel(own_ref, home_ref, received_ref, away_ref):
    rows = home_ref.shape[1]
    for k in range(2):
        here = slice(k * rows, (k + 1) * rows)
        away_ref[here] = (home_ref[k] + received_ref[here].astype(F32)).astype(BF16)
    away_ref[2 * rows :] = join_factors(
        own_ref[2 * rows :], received_ref[2 * rows :], MEMBER_ROWS
    )


def pair_sums(own, home, received):
    return call(pair_kernel, [(own.shape, BF16)], [], "pair", vmem(3), 12)(own, home, received)[0]


def parts_kernel(home_ref, *refs):
    received_refs, outs = refs[:4], refs[4:]
    for k, out in zip((3, 1, 2, 0), outs):
        out[...] = (home_ref[k] + received_refs[k][...].astype(F32)).astype(out.dtype)


def pair_parts(home, received):
    shape = home.shape[1:]
    return call(
        parts_kernel, [(shape, BF16), (shape, BF16), (shape, F32), (shape, F32)], [],
        "pair", vmem(5), 12,
    )(home, *received)


def merge_kernel(middle_ref, received_ref, out_ref):
    out_ref[...] = (middle_ref[...] + received_ref[...].astype(F32)).astype(BF16)


def merge(middle, received):
    return call(merge_kernel, [(middle.shape, BF16)], [], "merge", vmem(2))(middle, received)[0]


def merge_factors_kernel(home_ref, pair_ref, sent_ref, received_ref, out_ref):
    rows = home_ref.shape[1]
    total = home_ref[0] + pair_ref[0:rows].astype(F32) + received_ref[0:rows].astype(F32)
    out_ref[0:rows] = total.astype(BF16)
    out_ref[rows:] = join_factors(
        sent_ref[2 * rows :], received_ref[2 * rows :], 2 * MEMBER_ROWS
    )


def merge_factors(home, pair, sent, received):
    shape = (home.shape[1] + FACTOR_ROWS, home.shape[2])
    return call(merge_factors_kernel, [(shape, BF16)], [], "merge", vmem(4))(
        home, pair, sent, received
    )[0]


def update_kernel(own_ref, rate_ref, *refs):
    total = refs[0][...]
    for ref in refs[1:-1]:
        total = total + ref[...].astype(F32)
    refs[-1][...] = own_ref[0].astype(F32) - rate_ref[...].astype(F32) * total


def common_update_kernel(
    me_ref, own_ref, rate_ref, home_ref, pair_ref, half_ref, sent_ref, received_ref, out_ref
):
    rows, channels = rate_ref.shape
    total = home_ref[1] + pair_ref[rows : 2 * rows].astype(F32)
    total = total + half_ref[rows : 2 * rows].astype(F32) + received_ref[0:rows].astype(F32)
    means, sums = [], []
    for ref in (sent_ref, received_ref):
        parts = ref[rows:].astype(F32)
        for start in range(0, FACTOR_ROWS, MEMBER_ROWS):
            means.append(parts[start : start + 1] + parts[start + 1 : start + 2])
            sums.append(parts[start + 2 : start + 3] + parts[start + 3 : start + 4])
    means, sums = jnp.concatenate(means, axis=0), jnp.concatenate(sums, axis=0)
    means = jnp.concatenate([means] * 3, axis=1)
    for member in range(3 * channels // rows):

        @pl.when(me_ref[0] == member)
        def _():
            common = lax.dot_general(
                means[:, member * rows : (member + 1) * rows],
                sums,
                (((0,), (0,)), ((), ())),
                precision=lax.Precision.HIGHEST,
                preferred_element_type=F32,
            )
            out_ref[...] = own_ref[0].astype(F32) - rate_ref[...].astype(F32) * (total + common)


def common_update(me, own, rate, *terms):
    return call(
        common_update_kernel, [(rate.shape, F32)], [], "update", smem(1) + vmem(7), 12
    )(me, own, rate, *terms)[0]


def update(own, rate, *terms):
    shape = rate.shape
    return call(
        update_kernel, [(shape, F32)], [], "update", vmem(2 + len(terms)),
    )(own, rate, *terms)[0]


def common_term(every, me, own_rows):
    sums = every[:, 1]
    mean = jnp.concatenate([every[:, 0]] * 3, axis=1)
    mean = lax.dynamic_slice_in_dim(mean, me[0] * own_rows, own_rows, 1)
    return lax.dot_general(
        mean, sums, (((0,), (0,)), ((), ())), precision=lax.Precision.HIGHEST
    )


def shards(
    n_group,
    n_member,
    clips,
    targets,
    timestep,
    identity,
    conv1_weight,
    conv2_weight,
    rate1,
    rate2,
    time_proj,
    subject_table,
):
    frames, points, channels = (clips.shape[1], clips.shape[2], clips.shape[3])
    rows, padded = frames * points, (frames + 2) * points
    scale = 1.0 / math.sqrt(3 * channels)
    group = lax.axis_index("group").astype(jnp.int32)[None]
    me = lax.axis_index("member").astype(jnp.int32)[None]
    own_rows = conv1_weight.shape[0]
    clip, target = clips.reshape(rows, channels), targets.reshape(rows, channels)
    blocks = np.arange(channels) // (channels // GN_GROUPS)
    same_group = jnp.asarray((blocks[:, None] == blocks[None, :]), BF16)

    bias_row = time_bias(timestep[0], identity[0], subject_table, time_proj)

    def enter(clip):
        return call(
            functools.partial(enter_kernel, points),
            [((padded, channels), BF16), ((channels, rows), BF16)],
            [
                pltpu.VMEM((rows, channels), BF16),
                pltpu.VMEM(same_group.shape, BF16),
                pltpu.SemaphoreType.DMA((2,)),
            ],
            "enter", hbm(2), 12,
        )(clip, same_group)

    weight_one, weight_two, own_one, rates, acts, bias_row = weights_and_rates(
        n_group, n_member, conv1_weight, conv2_weight, rate1, rate2, group, me, clip, enter, bias_row
    )

    act_one, turned_one = acts

    def weight_specs(weight):
        return vmem(1) if len(weight) == 1 else smem(1) + vmem(2)

    hidden, sums = call(
        functools.partial(first_kernel, points, scale),
        [((rows, channels), F32), ((8, channels), F32)],
        [pltpu.VMEM((3 * channels, channels), BF16)],
        "conv", vmem(2) + weight_specs(weight_one), 20,
    )(act_one, bias_row, *weight_one)
    weight_two = weight_two(hidden)
    own_two = weight_two[1]
    if len(weight_two) == 2:
        weight_two = weight_two[:1]
    normal, inverse, act_two, turned_two, mean_two = call(
        functools.partial(norm_kernel, points),
        [
            ((rows, channels), F32),
            ((1, channels), F32),
            ((padded, channels), BF16),
            ((channels, rows), BF16),
            ((channels, 128), F32),
        ],
        [], "norm", vmem(3), 20,
    )(order_after(hidden, weight_two[:2]), sums, same_group)
    error, full_two = call(
        functools.partial(second_kernel, points, scale),
        [((padded, channels), BF16), ((3 * channels, channels), BF16)],
        [], "conv_error", vmem(3) + weight_specs(weight_two), 24,
    )(act_two, clip, target, *weight_two)
    staged = n_member == 8 and own_rows % 16 == 0
    if staged:
        away_two, home_two, sums_two = odd_half(
            turned_two, error, me, own_rows, points, scale, mean_two
        )
        received_two = swap(away_two, "member", n_member, 1)
        away_even, home_even = even_half(
            turned_two, error, me, own_rows, points, scale, mean_two, sums_two
        )
        received_even = swap(away_even, "member", n_member, 1)
        half_two = pair_sums(away_two, home_two, order_after(received_two, away_even))
        from_two = swap(half_two, "member", n_member, 2)
        error = order_after(error, half_two)
    else:
        (away_two,), home_two, factors = gradient(
            turned_two, error, me, n_member, points, scale, True
        )
        received_two = swap(away_two, "member", n_member, 1)
    (grad_act,) = call(
        functools.partial(back_kernel, points, scale),
        [((rows, channels), F32)], [], "back", vmem(2), 20,
    )(error, full_two)
    (grad_hidden,) = call(
        functools.partial(norm_back_kernel, points),
        [((padded, channels), BF16)],
        [
            pltpu.VMEM((rows, channels), F32),
            pltpu.VMEM(same_group.shape, BF16),
            pltpu.SemaphoreType.DMA((1,)),
        ],
        "norm_back", vmem(3) + hbm(1), 20,
    )(grad_act, normal, inverse, same_group)
    away_one, home_one, _ = gradient(
        turned_one, grad_hidden, me, n_member, points, scale, False
    )
    received_one = [swap(part, "member", n_member, 1) for part in away_one]
    if staged:
        received_one, from_two = order_after((received_one, from_two), ())
        far_one, near_one, middle_one, kept_one = pair_parts(home_one, received_one)
        from_one = swap(far_one, "member", n_member, 2)
        beside_one = swap(order_after(near_one, from_one), "member", n_member, 2)
        merged_two = merge_factors(home_even, received_even, half_two, from_two)
        across_two = swap(merged_two, "member", n_member, 4)
        rate_one, rate_two = rates(from_one)
        merged_one = merge(middle_one, from_one)
        across_one = swap(merged_one, "member", n_member, 4)
        adapted_two = common_update(
            me, own_two, rate_two, home_even, received_even, from_two, merged_two,
            order_after(across_two, merged_one),
        )
        kept_one, adapted_two = order_after((kept_one, adapted_two), ())
        adapted_one = update(own_one, rate_one, kept_one, beside_one, across_one)
    else:
        rate_one, rate_two = rates(away_one)
        every = lax.all_gather(factors, "member")
        terms_two = halve_to_owner(*add_received(home_two, received_two), None, n_member)
        terms_one = halve_to_owner(*add_received(home_one, received_one[0]), None, n_member)
        adapted_two = update(own_two, rate_two, *terms_two, common_term(every, me, own_rows))
        adapted_one = update(own_one, rate_one, *terms_one)
    return (adapted_one[None], adapted_two[None])


def solution(mesh):
    n_group, n_member = mesh.shape["group"], mesh.shape["member"]
    return jax.shard_map(
        lambda *arrays: shards(n_group, n_member, *arrays),
        mesh=mesh,
        in_specs=(
            P(("group", "member"), None, None, None),
            P(("group", "member"), None, None, None),
            P(("group", "member")),
            P(("group", "member")),
            P("member", "group"),
            P("member", "group"),
            P("member", "group"),
            P("member", "group"),
            P(),
            P(),
        ),
        out_specs=(P("group", "member", None), P("group", "member", None)),
        check_vma=False,
    )
```
